32 devices in a mesh: fsdp: 8 (over y, x, core), rep: 4 (over z).
Axes of the slice: x: 2, y: 2, z: 4, core: 2. Of those that a mesh axis runs over, the one named last changes fastest.
Arguments:
- incoming_symbols: bfloat16 [32, 128, 2048], P(('fsdp', 'rep')), may hold values from -6 to 6
- string_extents: int32 [32], P(('fsdp', 'rep')), may hold values from 32 to 128, as said below
- adjoint_signal: bfloat16 [32, 128, 2048], P(('fsdp', 'rep')), may hold values from -6 to 6
- first_scaling_factor: float32 [2048], replicated, may hold values from 0.5 to 1.5
- first_scaling_shift: float32 [2048], replicated, may hold values from -1.5 to 1.5
- lerp_factors: float32 [6, 2048], replicated, may hold values from 0 to 1
- lerp_narrow_weights: float32 [2048, 160], replicated, may hold values from -0.125 to 0.125
- lerp_widen_weights: float32 [5, 32, 2048], replicated, may hold values from -0.5 to 0.5
- fading_baseline: float32 [2048], replicated, may hold values from -6 to -0.5
- fading_narrow_weights: float32 [2048, 64], replicated, may hold values from -0.125 to 0.125
- fading_widen_weights: float32 [64, 2048], replicated, may hold values from -1.5 to 1.5
- present_reward: float32 [2048], replicated, may hold values from -3 to 3
- acceptor_weights: bfloat16 [2048, 2048], P('fsdp'), may hold values from -0.125 to 0.125
- lookup_weights: bfloat16 [2048, 2048], P('fsdp'), may hold values from -0.125 to 0.125
- content_weights: bfloat16 [2048, 2048], P('fsdp'), may hold values from -0.125 to 0.125
- valve_weights: bfloat16 [2048, 2048], P('fsdp'), may hold values from -0.125 to 0.125
- emission_weights: bfloat16 [2048, 2048], P('fsdp'), may hold values from -0.25 to 0.25
- cluster_scaling_factor: float32 [2048], replicated, may hold values from 0.5 to 1.5
- cluster_scaling_shift: float32 [2048], replicated, may hold values from -1.5 to 1.5
- second_scaling_factor: float32 [2048], replicated, may hold values from 0.5 to 1.5
- second_scaling_shift_vec: float32 [2048], replicated, may hold values from -1.5 to 1.5
- feed_lerp_factors: float32 [2, 2048], replicated, may hold values from 0 to 1
- feed_lookup_weights: bfloat16 [2048, 7168], P('fsdp'), may hold values from -0.125 to 0.125
- feed_content_weights: bfloat16 [7168, 2048], P('fsdp'), may hold values from -0.0625 to 0.0625
- feed_acceptor_weights: bfloat16 [2048, 2048], P('fsdp'), may hold values from -0.125 to 0.125
Outputs:
- layer_output: float32 [32, 128, 2048], P(('fsdp', 'rep'))
- token_grad: float32 [32, 128, 2048], P(('fsdp', 'rep'))
- first_scaling_factor_grads: float32 [2048], replicated
- first_scaling_shift_grads: float32 [2048], replicated
- lerp_factors_grads: float32 [6, 2048], replicated
- lerp_narrow_grads: float32 [2048, 160], replicated
- lerp_widen_grads: float32 [5, 32, 2048], replicated
- fading_baseline_grads: float32 [2048], replicated
- fading_narrow_grads: float32 [2048, 64], replicated
- fading_widen_grads: float32 [64, 2048], replicated
- present_reward_grads: float32 [2048], replicated
- acceptor_weights_grads: float32 [2048, 2048], P('fsdp')
- lookup_weights_grads: float32 [2048, 2048], P('fsdp')
- content_weights_grads: float32 [2048, 2048], P('fsdp')
- valve_weights_grads: float32 [2048, 2048], P('fsdp')
- emission_weights_grads: float32 [2048, 2048], P('fsdp')
- cluster_scaling_factor_grads: float32 [2048], replicated
- cluster_scaling_shift_grads: float32 [2048], replicated
- second_scaling_factor_grads: float32 [2048], replicated
- second_scaling_shift_grads: float32 [2048], replicated
- feed_lerp_grads: float32 [2, 2048], replicated
- feed_lookup_grads: float32 [2048, 7168], P('fsdp')
- feed_content_grads: float32 [7168, 2048], P('fsdp')
- feed_acceptor_grads: float32 [2048, 2048], P('fsdp')
The draws below stay inside these ranges and needn't reach their ends.
Inputs may be any that keep to these rules, and one draw needn't show every extreme that they name: `string_extents`: at least one sequence has all 128 slots valid.
All inputs are finite; a program needn't handle non-finite values.
Results may differ from the reference program's by a relative error of at most 0.018.
Values may be sent and summed in bfloat16 or wider, within the bound.
No kernel may reach another device: no remote copies, remote signals or barrier semaphores. Data moves between devices by JAX's collectives and lax.ppermute only.
A program may use at most 576 MiB of HBM per device.

```python
import math
import jax
import jax.numpy as jnp
from jax import lax

EMBED_WIDTH = 2048
ATTENTION_PARTS = 32
FF = 7168
SHIFT_RANK = 32
DECAY_RANK = 64
PLACES_PER_STRING = 128
BLOCK = 32
STRING_COUNT = 32


def draw_string_extents(key, part):
    drawn_lengths = jax.random.randint(jax.random.fold_in(key, 11), (STRING_COUNT,), PLACES_PER_STRING // 4, PLACES_PER_STRING + 1, dtype=jnp.int32)
    chosen = jax.random.randint(jax.random.fold_in(key, 12), (), 0, STRING_COUNT, dtype=jnp.int32)
    return drawn_lengths.at[chosen].set(PLACES_PER_STRING).astype(jnp.int32)


def steps_of(stream_key, dims, cuts, low, high):
    def one(axis_at, blocks):
        heights = jax.random.uniform(jax.random.fold_in(jax.random.fold_in(stream_key, 6), axis_at), (blocks,), jnp.float32, low / len(cuts), high / len(cuts))
        return jnp.repeat(jnp.exp(heights), dims[axis_at] // blocks).reshape((-1,) + (1,) * (len(dims) - axis_at - 1))

    gain = one(*cuts[0])
    for cut in cuts[1:]:
        gain = gain * one(*cut)
    return gain


def gaussian(key, shape, scale, bound, split=(), held_as=jnp.bfloat16):
    values = scale * jax.random.normal(key, shape, jnp.float32)
    if split:
        values = values * steps_of(key, shape, split, -0.22, 0.18)
    return jnp.clip(values, -bound, bound).astype(held_as)


def setup_inputs(seed: int = 0) -> dict:
    streams_of = jax.random.split(jax.random.key(seed), 26)
    incoming_symbols = gaussian(streams_of[0], (STRING_COUNT, PLACES_PER_STRING, EMBED_WIDTH), 1.0, 6.0, ((0, 32),))
    string_extents = draw_string_extents(jax.random.fold_in(streams_of[25], 71), 0)
    adjoint_signal = gaussian(streams_of[2], (STRING_COUNT, PLACES_PER_STRING, EMBED_WIDTH), 1.0, 6.0, ((0, 32),))
    first_scaling_factor = jnp.clip(1.0 + 0.1 * jax.random.normal(streams_of[3], (EMBED_WIDTH,), jnp.float32), 0.5, 1.5)
    first_scaling_shift = gaussian(streams_of[4], (EMBED_WIDTH,), 0.3, 1.5, (), jnp.float32)
    lerp_factors = jnp.clip(jax.random.uniform(streams_of[5], (6, EMBED_WIDTH), jnp.float32, 0.0, 1.0), 0.0, 1.0)
    lerp_narrow_weights = gaussian(streams_of[6], (EMBED_WIDTH, 5 * SHIFT_RANK), EMBED_WIDTH ** -0.5, 0.125, (), jnp.float32)
    lerp_widen_weights = gaussian(streams_of[7], (5, SHIFT_RANK, EMBED_WIDTH), (4 * SHIFT_RANK) ** -0.5, 0.5, (), jnp.float32)
    fading_baseline = jnp.clip(jax.random.uniform(streams_of[8], (EMBED_WIDTH,), jnp.float32, -6.0, -0.5), -6.0, -0.5)
    fading_narrow_weights = gaussian(streams_of[9], (EMBED_WIDTH, DECAY_RANK), EMBED_WIDTH ** -0.5, 0.125, (), jnp.float32)
    fading_widen_weights = gaussian(streams_of[10], (DECAY_RANK, EMBED_WIDTH), (DECAY_RANK // 4) ** -0.5, 1.5, (), jnp.float32)
    present_reward = gaussian(streams_of[11], (EMBED_WIDTH,), 0.5, 3.0, (), jnp.float32)
    acceptor_weights = gaussian(streams_of[12], (EMBED_WIDTH, EMBED_WIDTH), EMBED_WIDTH ** -0.5, 0.125, ((0, 8),))
    lookup_weights = gaussian(streams_of[13], (EMBED_WIDTH, EMBED_WIDTH), EMBED_WIDTH ** -0.5, 0.125, ((0, 8),))
    content_weights = gaussian(streams_of[14], (EMBED_WIDTH, EMBED_WIDTH), EMBED_WIDTH ** -0.5, 0.125, ((0, 8),))
    valve_weights = gaussian(streams_of[15], (EMBED_WIDTH, EMBED_WIDTH), EMBED_WIDTH ** -0.5, 0.125, ((0, 8),))
    emission_weights = gaussian(streams_of[16], (EMBED_WIDTH, EMBED_WIDTH), (EMBED_WIDTH // 4) ** -0.5, 0.25, ((0, 8),))
    cluster_scaling_factor = jnp.clip(1.0 + 0.1 * jax.random.normal(streams_of[17], (EMBED_WIDTH,), jnp.float32), 0.5, 1.5)
    cluster_scaling_shift = gaussian(streams_of[18], (EMBED_WIDTH,), 0.3, 1.5, (), jnp.float32)
    second_scaling_factor = jnp.clip(1.0 + 0.1 * jax.random.normal(streams_of[19], (EMBED_WIDTH,), jnp.float32), 0.5, 1.5)
    second_scaling_shift_vec = gaussian(streams_of[20], (EMBED_WIDTH,), 0.3, 1.5, (), jnp.float32)
    feed_lerp_factors = jnp.clip(jax.random.uniform(streams_of[21], (2, EMBED_WIDTH), jnp.float32, 0.0, 1.0), 0.0, 1.0)
    feed_lookup_weights = gaussian(streams_of[22], (EMBED_WIDTH, FF), EMBED_WIDTH ** -0.5, 0.125, ((0, 8),))
    feed_content_weights = gaussian(streams_of[23], (FF, EMBED_WIDTH), FF ** -0.5, 0.0625, ((0, 8),))
    feed_acceptor_weights = gaussian(streams_of[24], (EMBED_WIDTH, EMBED_WIDTH), EMBED_WIDTH ** -0.5, 0.125, ((0, 8),))
    return {"incoming_symbols": incoming_symbols, "string_extents": string_extents, "adjoint_signal": adjoint_signal, "first_scaling_factor": first_scaling_factor, "first_scaling_shift": first_scaling_shift, "lerp_factors": lerp_factors, "lerp_narrow_weights": lerp_narrow_weights, "lerp_widen_weights": lerp_widen_weights, "fading_baseline": fading_baseline, "fading_narrow_weights": fading_narrow_weights, "fading_widen_weights": fading_widen_weights, "present_reward": present_reward, "acceptor_weights": acceptor_weights, "lookup_weights": lookup_weights, "content_weights": content_weights, "valve_weights": valve_weights, "emission_weights": emission_weights, "cluster_scaling_factor": cluster_scaling_factor, "cluster_scaling_shift": cluster_scaling_shift, "second_scaling_factor": second_scaling_factor, "second_scaling_shift_vec": second_scaling_shift_vec, "feed_lerp_factors": feed_lerp_factors, "feed_lookup_weights": feed_lookup_weights, "feed_content_weights": feed_content_weights, "feed_acceptor_weights": feed_acceptor_weights}


@jax.custom_vjp
def low(v):
    return lax.optimization_barrier(v.astype(jnp.bfloat16)).astype(jnp.float32)

@jax.custom_vjp
def low_back(v):
    return v

def low_keep(v):
    return (low(v), None)

def low_pass(kept, grad):
    return (grad,)

def back_keep(v):
    return (v, None)

def back_low(kept, grad):
    return (low(grad),)
low.defvjp(low_keep, low_pass)
low_back.defvjp(back_keep, back_low)
norm_eps = 1e-05
group_eps = 1.0
exactness_flag = lax.Precision.HIGHEST

def layer_norm(values, norm_gain, offset):
    center = values - lax.optimization_barrier(jnp.mean(values, axis=-1, keepdims=True))
    spread = lax.optimization_barrier(jnp.mean(center * center, axis=-1, keepdims=True))
    return center * lax.rsqrt(spread + norm_eps) * norm_gain + offset

def shifted_rows(values):
    return jnp.concatenate([jnp.zeros(values[:1].shape, values.dtype), values[:-1]], axis=0)

def time_mix_inputs(token_inputs, first_scaling_factor, first_scaling_shift, lerp_factors, lerp_narrow_weights, lerp_widen_weights, fading_baseline, fading_narrow_weights, fading_widen_weights):
    normed = layer_norm(token_inputs, first_scaling_factor, first_scaling_shift)
    shift_delta = shifted_rows(normed) - normed
    blended_rows = normed + shift_delta * lerp_factors[0]
    hidden_rows = jnp.tanh(jnp.dot(blended_rows, lerp_narrow_weights, precision=exactness_flag))
    hidden_rows = hidden_rows.reshape(hidden_rows.shape[0], lerp_widen_weights.shape[0], lerp_widen_weights.shape[1])
    start_offsets = jnp.einsum('dui,uiy->udy', hidden_rows, lerp_widen_weights, precision=exactness_flag)
    decay_in = normed + shift_delta * (lerp_factors[1] + start_offsets[0])
    key_input_rows = normed + shift_delta * (lerp_factors[2] + start_offsets[1])
    value_input_rows = normed + shift_delta * (lerp_factors[3] + start_offsets[2])
    receptance_input_rows = normed + shift_delta * (lerp_factors[4] + start_offsets[3])
    gate_input_rows = normed + shift_delta * (lerp_factors[5] + start_offsets[4])
    decay_low = jnp.tanh(jnp.dot(decay_in, fading_narrow_weights, precision=exactness_flag))
    decay_raw = fading_baseline + jnp.dot(decay_low, fading_widen_weights, precision=exactness_flag)
    fading_exponent = -jnp.exp(decay_raw)
    return (receptance_input_rows, key_input_rows, value_input_rows, gate_input_rows, fading_exponent)

def fading_cumulative(acceptor_lines, lookup_mapped, content_mapped, fading_exponent, present_reward):
    seq_len, model_width = acceptor_lines.shape
    value_type = acceptor_lines.dtype
    attention_part_width = model_width // ATTENTION_PARTS
    block_count = seq_len // BLOCK

    def to_blocks(values):
        return values.reshape(block_count, BLOCK, ATTENTION_PARTS, attention_part_width).transpose(0, 2, 1, 3)
    reward_each_part = present_reward.reshape(ATTENTION_PARTS, 1, attention_part_width)
    query_pos = lax.broadcasted_iota(jnp.int32, (BLOCK, BLOCK), 0)
    source_pos = lax.broadcasted_iota(jnp.int32, (BLOCK, BLOCK), 1)
    causal = (query_pos > source_pos)[None, :, :, None]

    def block_step(state, pieces):
        acceptor_slice, lookup_slice, value_part, decay_part = pieces
        before = jnp.cumsum(decay_part, axis=1) - decay_part
        after = before + decay_part
        block_total = after[:, -1:, :]
        carried_in = jnp.einsum('hti,hij->htj', acceptor_slice * jnp.exp(before), state, precision=exactness_flag)
        gap_raw = before[:, :, None, :] - after[:, None, :, :]
        log_gap = jnp.where(causal, gap_raw, jnp.zeros_like(gap_raw))
        weight = jnp.where(causal, jnp.exp(log_gap), jnp.zeros_like(log_gap))
        scores = jnp.einsum('hti,hsi,htsi->hts', acceptor_slice, lookup_slice, weight, precision=exactness_flag)
        diagonal_contribution = lax.optimization_barrier(jnp.sum(acceptor_slice * reward_each_part * lookup_slice, axis=-1, keepdims=True))
        result = carried_in + jnp.einsum('hts,hsj->htj', scores, value_part, precision=exactness_flag) + diagonal_contribution * value_part
        key_carried = lookup_slice * jnp.exp(block_total - after)
        fresh_state = jnp.einsum('hsi,hsj->hij', key_carried, value_part, precision=exactness_flag)
        new_state = jnp.exp(block_total)[:, 0, :, None] * state + fresh_state
        return (new_state, result)
    zero_state = jnp.zeros((ATTENTION_PARTS, attention_part_width, attention_part_width), value_type)
    last_state, outputs = lax.scan(jax.checkpoint(block_step), zero_state, (to_blocks(acceptor_lines), to_blocks(lookup_mapped), to_blocks(content_mapped), to_blocks(fading_exponent)))
    return outputs.transpose(0, 2, 1, 3).reshape(seq_len, model_width)

def attention_answers(acceptor_lines, lookup_mapped, content_mapped, valve_mapped, fading_exponent, present_reward, cluster_scaling_factor, cluster_scaling_shift):
    merged_lines = fading_cumulative(acceptor_lines, lookup_mapped, content_mapped, fading_exponent, present_reward)
    grouped = merged_lines.reshape(merged_lines.shape[0], ATTENTION_PARTS, -1)
    center = grouped - lax.optimization_barrier(jnp.mean(grouped, axis=-1, keepdims=True))
    spread = lax.optimization_barrier(jnp.mean(center * center, axis=-1, keepdims=True))
    normed = (center * lax.rsqrt(spread + group_eps)).reshape(merged_lines.shape)
    return (normed * cluster_scaling_factor + cluster_scaling_shift) * jax.nn.silu(valve_mapped)

def chan_inputs(residual, second_scaling_factor, second_scaling_shift_vec, feed_lerp_factors):
    normed = layer_norm(residual, second_scaling_factor, second_scaling_shift_vec)
    shift_delta = shifted_rows(normed) - normed
    return (normed + shift_delta * feed_lerp_factors[0], normed + shift_delta * feed_lerp_factors[1])

def matmul(first_op, second_op):
    return jnp.dot(first_op, second_op, precision=exactness_flag)

def forward_seq(token_inputs, mask_row, learned_bundle):
    first_scaling_factor, first_scaling_shift, lerp_factors, lerp_narrow_weights, lerp_widen_weights, fading_baseline, fading_narrow_weights, fading_widen_weights, present_reward, acceptor_weights, lookup_weights, content_weights, valve_weights, emission_weights, cluster_scaling_factor, cluster_scaling_shift, second_scaling_factor, second_scaling_shift_vec, feed_lerp_factors, feed_lookup_weights, feed_content_weights, feed_acceptor_weights = learned_bundle
    receptance_input_rows, key_input_rows, value_input_rows, gate_input_rows, fading_exponent = time_mix_inputs(token_inputs, first_scaling_factor, first_scaling_shift, lerp_factors, lerp_narrow_weights, lerp_widen_weights, fading_baseline, fading_narrow_weights, fading_widen_weights)
    acceptor_lines = low_back(matmul(low(receptance_input_rows), acceptor_weights))
    lookup_mapped = low_back(matmul(low(key_input_rows), lookup_weights))
    content_mapped = low_back(matmul(low(value_input_rows), content_weights))
    valve_mapped = low_back(matmul(low(gate_input_rows), valve_weights))
    merged_lines = attention_answers(acceptor_lines, lookup_mapped, content_mapped, valve_mapped, fading_exponent, present_reward, cluster_scaling_factor, cluster_scaling_shift)
    branch = low_back(matmul(low(merged_lines), emission_weights))
    residual = token_inputs + branch
    key_chan, recept_chan = chan_inputs(residual, second_scaling_factor, second_scaling_shift_vec, feed_lerp_factors)
    key_act = low_back(matmul(low(key_chan), feed_lookup_weights))
    softened = jax.nn.softplus(key_act)
    value_act = low_back(matmul(low(softened * softened), feed_content_weights))
    gate_act = low_back(matmul(low(recept_chan), feed_acceptor_weights))
    return (residual + jax.nn.sigmoid(gate_act) * value_act) * mask_row[:, None]

def reference(incoming_symbols, string_extents, adjoint_signal, first_scaling_factor, first_scaling_shift, lerp_factors, lerp_narrow_weights, lerp_widen_weights, fading_baseline, fading_narrow_weights, fading_widen_weights, present_reward, acceptor_weights, lookup_weights, content_weights, valve_weights, emission_weights, cluster_scaling_factor, cluster_scaling_shift, second_scaling_factor, second_scaling_shift_vec, feed_lerp_factors, feed_lookup_weights, feed_content_weights, feed_acceptor_weights):
    learned_bundle = tuple((element_pick.astype(jnp.float32) for element_pick in (first_scaling_factor, first_scaling_shift, lerp_factors, lerp_narrow_weights, lerp_widen_weights, fading_baseline, fading_narrow_weights, fading_widen_weights, present_reward, acceptor_weights, lookup_weights, content_weights, valve_weights, emission_weights, cluster_scaling_factor, cluster_scaling_shift, second_scaling_factor, second_scaling_shift_vec, feed_lerp_factors, feed_lookup_weights, feed_content_weights, feed_acceptor_weights)))
    value_type = learned_bundle[0].dtype
    group_size = math.gcd(STRING_COUNT, max(1, 4096 // PLACES_PER_STRING))
    group_steps = STRING_COUNT // group_size
    positions = lax.broadcasted_iota(jnp.int32, (STRING_COUNT, PLACES_PER_STRING), 1)
    extents = string_extents.astype(jnp.int32)[:, None]
    seq_masks = jnp.where(positions < extents, jnp.ones((), value_type), jnp.zeros((), value_type))

    def grouped(values):
        return values.astype(value_type).reshape(group_steps, group_size, PLACES_PER_STRING, EMBED_WIDTH)

    def run_group(cumulative_sums, pieces):
        token_inputs, cot_in, mask_in = pieces

        def batch_forward(tokens_all, *weights):
            return jax.vmap(lambda row_tokens, row_mask: forward_seq(row_tokens, row_mask, weights))(tokens_all, mask_in)
        result, pullback = jax.vjp(batch_forward, token_inputs, *learned_bundle)
        grads = pullback(cot_in)
        new_totals = tuple((running + piece_grad.astype(running.dtype) for running, piece_grad in zip(cumulative_sums, grads[1:])))
        return (new_totals, (result, grads[0]))
    zeros_init = tuple((jnp.zeros(element_pick.shape, value_type) for element_pick in learned_bundle))
    cumulative_sums, (block_answer, symbol_answer) = lax.scan(run_group, zeros_init, (grouped(incoming_symbols), grouped(adjoint_signal), seq_masks.reshape(group_steps, group_size, PLACES_PER_STRING)))
    first_scaling_factor_grads, first_scaling_shift_grads, lerp_factors_grads, lerp_narrow_grads, lerp_widen_grads, fading_baseline_grads, fading_narrow_grads, fading_widen_grads, present_reward_grads, acceptor_weights_grads, lookup_weights_grads, content_weights_grads, valve_weights_grads, emission_weights_grads, cluster_scaling_factor_grads, cluster_scaling_shift_grads, second_scaling_factor_grads, second_scaling_shift_grads, feed_lerp_grads, feed_lookup_grads, feed_content_grads, feed_acceptor_grads = cumulative_sums
    return (block_answer.reshape(STRING_COUNT, PLACES_PER_STRING, EMBED_WIDTH), symbol_answer.reshape(STRING_COUNT, PLACES_PER_STRING, EMBED_WIDTH), first_scaling_factor_grads, first_scaling_shift_grads, lerp_factors_grads, lerp_narrow_grads, lerp_widen_grads, fading_baseline_grads, fading_narrow_grads, fading_widen_grads, present_reward_grads, acceptor_weights_grads, lookup_weights_grads, content_weights_grads, valve_weights_grads, emission_weights_grads, cluster_scaling_factor_grads, cluster_scaling_shift_grads, second_scaling_factor_grads, second_scaling_shift_grads, feed_lerp_grads, feed_lookup_grads, feed_content_grads, feed_acceptor_grads)
```

```python
import functools

import jax
import jax.numpy as jnp
import numpy as np
from jax import lax
from jax.experimental import pallas as pl
from jax.experimental.pallas import tpu as pltpu
from jax.sharding import PartitionSpec as P

HEADS = 32
norm_eps = 1e-05
group_eps = 1.0
BF = jnp.bfloat16
F32 = jnp.float32
MIB = 1 << 20


def mm(a, b):
    return jnp.dot(a, b, preferred_element_type=F32)


def mm_nt(a, b):
    return lax.dot_general(a, b, (((1,), (1,)), ((), ())), preferred_element_type=F32)


def mm_tn(a, b):
    return lax.dot_general(a, b, (((0,), (0,)), ((), ())), preferred_element_type=F32)


def halves(v):
    high = v.astype(BF)
    return high, (v - high.astype(F32)).astype(BF)


def gather_rows(v):
    return lax.all_gather(v, "fsdp", axis=0, tiled=True)


def gather_cols(v):
    return lax.all_gather(v, "fsdp", axis=1, tiled=True)


def scatter_rows(v):
    return lax.psum_scatter(v, "fsdp", scatter_dimension=0, tiled=True)


def scatter_cols(v):
    return lax.psum_scatter(v, "fsdp", scatter_dimension=1, tiled=True)


def exchange(take, put, out):
    n = lax.axis_size("fsdp")
    me = lax.axis_index("fsdp")
    out = put(out, me, take(me))
    for m in range(1, n):
        got = lax.ppermute(take(me ^ m), "fsdp", [(i, i ^ m) for i in range(n)])
        out = put(out, me ^ m, got)
    return out


def rows_to_cols(v):
    n = lax.axis_size("fsdp")
    if n > 8:
        return lax.all_to_all(v, "fsdp", split_axis=1, concat_axis=0, tiled=True)
    r, c = v.shape[0], v.shape[1] // n
    return exchange(
        lambda j: lax.dynamic_slice_in_dim(v, j * c, c, 1),
        lambda out, j, b: lax.dynamic_update_slice_in_dim(out, b, j * r, 0),
        jnp.zeros((r * n, c), v.dtype),
    )


def cols_to_rows(v):
    n = lax.axis_size("fsdp")
    if n > 8:
        return lax.all_to_all(v, "fsdp", split_axis=0, concat_axis=1, tiled=True)
    r, c = v.shape[0] // n, v.shape[1]
    return exchange(
        lambda j: lax.dynamic_slice_in_dim(v, j * r, r, 0),
        lambda out, j, b: lax.dynamic_update_slice_in_dim(out, b, j * c, 1),
        jnp.zeros((r, c * n), v.dtype),
    )


def hold(*values):
    return lax.optimization_barrier(values)


def rep_scatter_rows(v):
    return lax.psum_scatter(v, "rep", scatter_dimension=0, tiled=True)


def rep_scatter_cols(v):
    n, z = lax.axis_size("fsdp"), lax.axis_size("rep")
    rows, c = v.shape
    v = v.reshape(n, z, rows // (n * z), c).transpose(1, 0, 2, 3).reshape(rows, c)
    return lax.psum_scatter(v, "rep", scatter_dimension=0, tiled=True)


def rep_gather(v):
    n = lax.axis_size("rep")
    z = lax.axis_index("rep")
    up, down = [v], [v]
    for s in range(1, n):
        up.append(lax.ppermute(up[-1], "rep", [(i, i + 1) for i in range(s - 1, n - 1)]))
        down.append(lax.ppermute(down[-1], "rep", [(i + 1, i) for i in range(n - s)]))
    out = jnp.zeros((n,) + v.shape, F32)
    out = lax.dynamic_update_index_in_dim(out, v.astype(F32), z, 0)
    for s in range(1, n):
        piece = jnp.where(z >= s, up[s], down[n - s]).astype(F32)
        out = lax.dynamic_update_index_in_dim(out, piece, lax.rem(z - s + n, n), 0)
    return out.reshape((n * v.shape[0],) + v.shape[1:])


def whole_block(a):
    return pl.BlockSpec(a.shape, lambda *_: (0,) * a.ndim, pipeline_mode=pl.Buffered(1))


def shifted(v):
    first = lax.broadcasted_iota(jnp.int32, v.shape, 0) == 0
    return jnp.where(first, 0.0, pltpu.roll(v, 1, 0))


def shifted_back(v):
    last = lax.broadcasted_iota(jnp.int32, v.shape, 0) == v.shape[0] - 1
    return jnp.where(last, 0.0, pltpu.roll(v, v.shape[0] - 1, 0))


def normal_rows(v):
    center = v - jnp.mean(v, axis=-1, keepdims=True)
    spread = jnp.mean(center * center, axis=-1, keepdims=True)
    return center * lax.rsqrt(spread + norm_eps)


def front_kernel(
    ranks, tok, gain, shift, lerp, narrow, widen, fnarrow, xk, xv, xr, xg, hid, low
):
    normed = normal_rows(tok[...].astype(F32)) * gain[...] + shift[...]
    delta = shifted(normed) - normed
    bh, bl = halves(normed + delta * lerp[0:1, :])
    wide = ranks * 5
    pre = mm(bh, narrow[...])
    hidden = jnp.tanh(pre[:, :wide] + pre[:, wide:] + mm(bl, narrow[:, :wide]))
    hid[...] = hidden
    hb = hidden.astype(BF)
    for f, out in ((1, xk), (2, xv), (3, xr), (4, xg), (0, None)):
        rows = slice(f * ranks, (f + 1) * ranks)
        x = normed + delta * (lerp[f + 1 : f + 2, :] + mm(hb[:, rows], widen[rows, :]))
        if out is not None:
            out[...] = x.astype(BF)
        else:
            dh, dl = halves(x)
            fd = low.shape[1]
            pre = mm(dh, fnarrow[...])
            low[...] = jnp.tanh(pre[:, :fd] + pre[:, fd:] + mm(dl, fnarrow[:, :fd]))


def front(seq_len, tokens, gain, shift, lerp, narrow, widen, fnarrow):
    g, d = tokens.shape
    ranks = widen.shape[0] // 5
    fd = fnarrow.shape[1] // 2
    per_seq = lambda w: pl.BlockSpec((seq_len, w), lambda s: (s, 0))
    return pl.pallas_call(
        functools.partial(front_kernel, ranks),
        grid=(g // seq_len,),
        in_specs=[per_seq(d)]
        + [whole_block(a) for a in (gain, shift, lerp, narrow, widen, fnarrow)],
        out_specs=[per_seq(d)] * 4 + [per_seq(5 * ranks), per_seq(fd)],
        out_shape=[jax.ShapeDtypeStruct((g, d), BF)] * 4
        + [
            jax.ShapeDtypeStruct((g, 5 * ranks), F32),
            jax.ShapeDtypeStruct((g, fd), F32),
        ],
        compiler_params=pltpu.CompilerParams(vmem_limit_bytes=48 * MIB),
        cost_estimate=pl.CostEstimate(
            flops=g * d * 2 * 5 * 256, bytes_accessed=g * d * 10, transcendentals=0
        ),
        name="token_shift",
    )(tokens, gain, shift, lerp, narrow, widen, fnarrow)


def back_kernel(
    ranks,
    tok,
    hid,
    low,
    dk,
    dv,
    dr,
    dg,
    draw,
    gain,
    shift,
    lerp,
    narrow,
    widen,
    fnarrow,
    fwiden,
    wk,
    wv,
    wr,
    wg,
    dn_out,
    vec_out,
    dwid_out,
    dnar_out,
    dfn_out,
):
    @pl.when(pl.program_id(0) == 0)
    def _():
        for ref in (vec_out, dwid_out, dnar_out, dfn_out):
            ref[...] = jnp.zeros_like(ref)

    unit = normal_rows(tok[...].astype(F32))
    normed = unit * gain[...] + shift[...]
    delta = shifted(normed) - normed
    hidden = hid[...]
    hb = hidden.astype(BF)
    lowv = low[...]
    colsum = lambda v: jnp.sum(v, axis=0, keepdims=True)
    dlow = mm_nt(draw[...].astype(BF), fwiden[...]) * (1.0 - lowv * lowv)
    dlow = dlow.astype(BF)
    total = jnp.zeros(normed.shape, F32)
    moved = jnp.zeros(normed.shape, F32)
    dhid = []
    for f, d_ref, w_ref in (
        (0, None, None),
        (1, dk, wk),
        (2, dv, wv),
        (3, dr, wr),
        (4, dg, wg),
    ):
        rows = slice(f * ranks, (f + 1) * ranks)
        mu = lerp[f + 1 : f + 2, :] + mm(hb[:, rows], widen[rows, :])
        if f == 0:
            dx = mm_nt(dlow, fnarrow[...])
            dfn_out[...] += mm_tn(dlow, (normed + delta * mu).astype(BF))
        else:
            dx = mm_nt(d_ref[...], w_ref[...])
        total = total + dx
        moved = moved + dx * mu
        doff = dx * delta
        vec_out[f + 1 : f + 2, :] += colsum(doff)
        db = doff.astype(BF)
        dwid_out[rows, :] += mm_tn(hb[:, rows], db)
        dhid.append(mm_nt(db, widen[rows, :]))
    dpre = (jnp.concatenate(dhid, axis=1) * (1.0 - hidden * hidden)).astype(BF)
    dblend = mm_nt(dpre, narrow[...])
    base = lerp[0:1, :]
    dnar_out[...] += mm_tn(dpre, (normed + delta * base).astype(BF))
    vec_out[0:1, :] += colsum(dblend * delta)
    total = total + dblend
    moved = moved + dblend * base
    dn = total - moved + shifted_back(moved)
    vec_out[6:7, :] += colsum(dn * unit)
    vec_out[7:8, :] += colsum(dn)
    dn_out[...] = dn.astype(BF)


def back(seq_len, tokens, hid, low, grads, draw, params, weights):
    g, d = tokens.shape
    c = draw.shape[1]
    gain, shift, lerp, narrow, widen, fnarrow, fwiden = params
    ranks = widen.shape[0] // 5
    fd = low.shape[1]
    per_seq = lambda w: pl.BlockSpec((seq_len, w), lambda s: (s, 0))
    kept = lambda r: pl.BlockSpec((r, d), lambda s: (0, 0))
    return pl.pallas_call(
        functools.partial(back_kernel, ranks),
        grid=(g // seq_len,),
        in_specs=[per_seq(d), per_seq(5 * ranks), per_seq(fd)]
        + [per_seq(c)] * 5
        + [whole_block(a) for a in params]
        + [whole_block(a) for a in weights],
        out_specs=[per_seq(d), kept(8), kept(5 * ranks), kept(5 * ranks), kept(fd)],
        out_shape=[
            jax.ShapeDtypeStruct((g, d), BF),
            jax.ShapeDtypeStruct((8, d), F32),
            jax.ShapeDtypeStruct((5 * ranks, d), F32),
            jax.ShapeDtypeStruct((5 * ranks, d), F32),
            jax.ShapeDtypeStruct((fd, d), F32),
        ],
        compiler_params=pltpu.CompilerParams(vmem_limit_bytes=56 * MIB),
        cost_estimate=pl.CostEstimate(
            flops=g * d * 2 * 18 * 256, bytes_accessed=g * d * 6, transcendentals=0
        ),
        name="token_shift_back",
    )(tokens, hid, low, *grads, draw, *params, *weights)


def level_tables(length):
    p = np.arange(length)[:, None]
    u = np.arange(length)[None, :]
    levels = int(length).bit_length() - 1
    spans = []
    for l in range(1, levels):
        b = 1 << l
        same = (p // b) == (u // b)
        upper = (p // b) % 2 == 1
        spans.append(same & np.where(upper, u < p, u > p))
    spans = np.concatenate(spans, 0).astype(np.float32)
    diff = p ^ u
    level = np.where(u < p, np.floor(np.log2(np.maximum(diff, 1))), -1)
    return levels, spans, level.astype(np.int32)


def per_head(lanes, width, count, v):
    out = jnp.sum(jnp.where(lanes == 0, v, 0.0), axis=1, keepdims=True)
    if count == 1:
        return jnp.broadcast_to(out, v.shape)
    for h in range(1, count):
        one = jnp.sum(jnp.where(lanes == h, v, 0.0), axis=1, keepdims=True)
        out = jnp.where(lanes == h, one, out)
    return out


def stack_heads(lanes, count, v):
    zero = jnp.zeros_like(v)
    return jnp.concatenate([jnp.where(lanes == h, v, zero) for h in range(count)], axis=0)


def side_by_side(length, count, v):
    return jnp.concatenate([v[h * length : (h + 1) * length] for h in range(count)], axis=1)


def mix_forward(levels, count, width, r, k, v, w, u, spans, level):
    length, lanes_n = r.shape
    lanes = lax.broadcasted_iota(jnp.int32, (length, lanes_n), 1) // width
    wh, wl = halves(w)
    gaps = mm(spans, wh) + mm(spans, wl)
    factors = [None] + [
        jnp.exp(gaps[l * length : (l + 1) * length]) for l in range(levels - 1)
    ]
    level2 = jnp.concatenate([level] * count, axis=0)
    scores = jnp.zeros((length * count, length), F32)
    parts = []
    for l in range(levels):
        e = factors[l]
        re = (r if e is None else r * e).astype(BF)
        ke = (k if e is None else k * e).astype(BF)
        parts.append((e, re, ke))
        scores = scores + jnp.where(
            level2 == l, mm_nt(stack_heads(lanes, count, re), ke), 0.0
        )
    vb = v.astype(BF)
    bonus = per_head(lanes, width, count, r * u * k)
    wkv = (
        mm(side_by_side(length, count, scores).astype(BF), stack_heads(lanes, count, vb))
        + bonus * v
    )
    center = wkv - per_head(lanes, width, count, wkv) * (1.0 / width)
    spread = per_head(lanes, width, count, center * center) * (1.0 / width)
    rstd = lax.rsqrt(spread + group_eps)
    return lanes, level2, parts, scores, bonus, vb, center * rstd, rstd


def wkv_kernel(levels, count, width, r, k, v, g, w, u, gain, bias, spans, level, out):
    unit = mix_forward(
        levels, count, width, r[...], k[...], v[...], w[...], u[...], spans[...], level[...]
    )[6]
    gate = g[...]
    out[...] = ((unit * gain[...] + bias[...]) * (gate * jax.nn.sigmoid(gate))).astype(BF)


def wkv_back_kernel(
    levels,
    count,
    width,
    r_ref,
    k_ref,
    v_ref,
    g_ref,
    w_ref,
    dm_ref,
    u_ref,
    gain_ref,
    bias_ref,
    spans,
    spans_t,
    level_ref,
    dr_out,
    dk_out,
    dv_out,
    dg_out,
    draw_out,
    vec_out,
):
    @pl.when(pl.program_id(1) == 0)
    def _():
        vec_out[...] = jnp.zeros_like(vec_out)

    r, k, v, w, u = r_ref[...], k_ref[...], v_ref[...], w_ref[...], u_ref[...]
    level = level_ref[...]
    lanes, level2, parts, scores, bonus, vb, unit, rstd = mix_forward(
        levels, count, width, r, k, v, w, u, spans[...], level
    )
    length = r.shape[0]
    heads = functools.partial(per_head, lanes, width, count)
    stack = functools.partial(stack_heads, lanes, count)
    beside = functools.partial(side_by_side, length, count)
    colsum = lambda x: jnp.sum(x, axis=0, keepdims=True)

    gate, dm, gain = g_ref[...], dm_ref[...], gain_ref[...]
    sig = jax.nn.sigmoid(gate)
    scaled = unit * gain + bias_ref[...]
    dg_out[...] = (dm * scaled * sig * (1.0 + gate * (1.0 - sig))).astype(BF)
    dscaled = dm * gate * sig
    dunit = dscaled * gain
    dwkv = rstd * (
        dunit - heads(dunit) * (1.0 / width) - unit * (heads(dunit * unit) * (1.0 / width))
    )
    db = dwkv.astype(BF)
    dbs = stack(db)
    dscores = mm_nt(dbs, vb)

    def turned(x):
        return jnp.concatenate(
            [jnp.transpose(x[h * length : (h + 1) * length]) for h in range(count)], axis=0
        )

    dscores_t = turned(dscores)
    level_t = jnp.transpose(level)
    level2_t = jnp.concatenate([level_t] * count, axis=0)
    dv = mm(beside(turned(scores)).astype(BF), dbs) + bonus * dwkv
    dbonus = heads(dwkv * v)
    dr = dbonus * u * k
    dk = dbonus * u * r
    flows = []
    for l in range(levels):
        e, re, ke = parts[l]
        dre = mm(beside(jnp.where(level2 == l, dscores, 0.0)).astype(BF), stack(ke))
        dke = mm(beside(jnp.where(level2_t == l, dscores_t, 0.0)).astype(BF), stack(re))
        if e is None:
            dr = dr + dre
            dk = dk + dke
        else:
            dre = dre * e
            dke = dke * e
            dr = dr + dre
            dk = dk + dke
            flows.append(dre * r + dke * k)
    fh, fl = halves(jnp.concatenate(flows, axis=0))
    dw = mm(spans_t[...], fh) + mm(spans_t[...], fl)
    draw = dw * w
    dr_out[...] = dr.astype(BF)
    dk_out[...] = dk.astype(BF)
    dv_out[...] = dv.astype(BF)
    draw_out[...] = draw
    vec_out[0:1, :] += colsum(dbonus * r * k)
    vec_out[1:2, :] += colsum(dscaled * unit)
    vec_out[2:3, :] += colsum(dscaled)
    vec_out[3:4, :] += colsum(draw)


def wkv(seq_len, r, k, v, g, w, u, gain, bias, dmixed=None):
    rows, c = r.shape
    heads_here = c * HEADS // D_OF(u, c)
    width = c // heads_here
    count = 2 if heads_here % 2 == 0 else 1
    lanes = count * width
    levels, spans, level = level_tables(seq_len)
    spans_a = jnp.asarray(spans, BF)
    level_a = jnp.asarray(level)
    cols = pl.BlockSpec((seq_len, lanes), lambda p, s: (s, p))
    vec = pl.BlockSpec((1, lanes), lambda p, s: (0, p))
    grid = (c // lanes, rows // seq_len)
    flops = rows * c * seq_len * 2 * 16
    params = pltpu.CompilerParams(vmem_limit_bytes=40 * MIB)
    if dmixed is None:
        return pl.pallas_call(
            functools.partial(wkv_kernel, levels, count, width),
            grid=grid,
            in_specs=[cols] * 5 + [vec] * 3 + [whole_block(spans_a), whole_block(level_a)],
            out_specs=cols,
            out_shape=jax.ShapeDtypeStruct((rows, c), BF),
            compiler_params=params,
            cost_estimate=pl.CostEstimate(
                flops=flops, bytes_accessed=rows * c * 22, transcendentals=rows * c * 7
            ),
            name="decay_mix",
        )(r, k, v, g, w, u, gain, bias, spans_a, level_a)
    spans_t = jnp.asarray(
        np.concatenate([s.T for s in spans.reshape(levels - 1, seq_len, seq_len)], 1), BF
    )
    return pl.pallas_call(
        functools.partial(wkv_back_kernel, levels, count, width),
        grid=grid,
        in_specs=[cols] * 6
        + [vec] * 3
        + [whole_block(spans_a), whole_block(spans_t), whole_block(level_a)],
        out_specs=[cols] * 5 + [pl.BlockSpec((4, lanes), lambda p, s: (0, p))],
        out_shape=[jax.ShapeDtypeStruct((rows, c), BF)] * 4
        + [jax.ShapeDtypeStruct((rows, c), F32), jax.ShapeDtypeStruct((4, c), F32)],
        compiler_params=params,
        cost_estimate=pl.CostEstimate(
            flops=flops * 4, bytes_accessed=rows * c * 36, transcendentals=rows * c * 7
        ),
        name="decay_mix_back",
    )(r, k, v, g, w, dmixed, u, gain, bias, spans_a, spans_t, level_a)


def D_OF(u, c):
    return c * lax.axis_size("fsdp")


def body(
    incoming_symbols,
    string_extents,
    adjoint_signal,
    first_scaling_factor,
    first_scaling_shift,
    lerp_factors,
    lerp_narrow_weights,
    lerp_widen_weights,
    fading_baseline,
    fading_narrow_weights,
    fading_widen_weights,
    present_reward,
    acceptor_weights,
    lookup_weights,
    content_weights,
    valve_weights,
    emission_weights,
    cluster_scaling_factor,
    cluster_scaling_shift,
    second_scaling_factor,
    second_scaling_shift_vec,
    feed_lerp_factors,
    feed_lookup_weights,
    feed_content_weights,
    feed_acceptor_weights,
):
    seqs, length, d = incoming_symbols.shape
    n = lax.axis_size("fsdp")
    me = lax.axis_index("fsdp")
    c = d // n
    home = seqs * length
    plane = home * n
    ranks = lerp_widen_weights.shape[1]
    fd = fading_narrow_weights.shape[1]

    tok_home = incoming_symbols.reshape(home, d)
    tokens = gather_rows(tok_home)
    weights = rows_to_cols(
        jnp.concatenate(
            [
                w.reshape(c, n, c)
                for w in (lookup_weights, content_weights, acceptor_weights, valve_weights)
            ],
            axis=2,
        ).reshape(c, 4 * d)
    )
    wk, wv, wr, wg = (weights[:, i * c : (i + 1) * c] for i in range(4))
    positions = lax.broadcasted_iota(jnp.int32, (seqs, length), 1)
    mask = (positions < string_extents[:, None]).astype(F32).reshape(home, 1)
    adj_low = adjoint_signal.reshape(home, d) * mask.astype(BF)
    d_out = adj_low.astype(F32)
    d_out_cols = rows_to_cols(adj_low).astype(F32)

    row = lambda v: v.reshape(1, -1)
    mine = lambda v: lax.dynamic_slice_in_dim(v, me * c, c, v.ndim - 1)
    gain1, shift1 = row(first_scaling_factor), row(first_scaling_shift)
    nh, nl = halves(lerp_narrow_weights)
    fh, fl = halves(fading_narrow_weights)
    widen_low = lerp_widen_weights.reshape(5 * ranks, d).astype(BF)
    xk, xv, xr, xg, hidden, low = front(
        length,
        tokens,
        gain1,
        shift1,
        lerp_factors,
        jnp.concatenate([nh, nl], axis=1),
        widen_low,
        jnp.concatenate([fh, fl], axis=1),
    )
    fwiden_mine = mine(fading_widen_weights)
    w = -jnp.exp(
        mine(row(fading_baseline))
        + jnp.dot(low, fwiden_mine, precision=lax.Precision.HIGHEST)
    )
    k, v, r, g = mm(xk, wk), mm(xv, wv), mm(xr, wr), mm(xg, wg)
    u, gn_gain, gn_bias = (
        mine(row(t)) for t in (present_reward, cluster_scaling_factor, cluster_scaling_shift)
    )
    mixed = wkv(length, r, k, v, g, w, u, gn_gain, gn_bias)
    branch = scatter_rows(mm(mixed, emission_weights).astype(BF))
    residual = tok_home.astype(F32) + branch.astype(F32)

    center = residual - jnp.mean(residual, axis=-1, keepdims=True)
    rstd2 = lax.rsqrt(jnp.mean(center * center, axis=-1, keepdims=True) + norm_eps)
    unit2 = center * rstd2
    normed2_home = unit2 * second_scaling_factor + second_scaling_shift_vec
    normed2 = gather_rows(normed2_home.astype(BF)).astype(F32)
    weights2 = rows_to_cols(
        jnp.concatenate(
            [feed_lookup_weights.reshape(c, n, -1), feed_acceptor_weights.reshape(c, n, -1)],
            axis=2,
        ).reshape(c, -1)
    )
    fc = feed_content_weights.shape[0]
    wl, wa = weights2[:, :fc], weights2[:, fc:]

    def before(t):
        t = t.reshape(-1, length, d)
        return jnp.concatenate([jnp.zeros_like(t[:, :1]), t[:, :-1]], axis=1).reshape(-1, d)

    def after(t):
        t = t.reshape(-1, length, d)
        return jnp.concatenate([t[:, 1:], jnp.zeros_like(t[:, :1])], axis=1).reshape(-1, d)

    delta2 = before(normed2) - normed2
    key_chan = (normed2 + delta2 * feed_lerp_factors[0]).astype(BF)
    recept_chan = (normed2 + delta2 * feed_lerp_factors[1]).astype(BF)
    key_act = mm(key_chan, wl)
    soft = jax.nn.softplus(key_act)
    squared = (soft * soft).astype(BF)
    value_act = scatter_cols(mm(squared, feed_content_weights).astype(BF)).astype(F32)
    gate = jax.nn.sigmoid(mm(recept_chan, wa))
    gated = gate * value_act
    layer_output = (residual + cols_to_rows(gated.astype(BF)).astype(F32)) * mask
    d_value = gather_cols((d_out_cols * gate).astype(BF))
    d_gate = (d_out_cols * gated * (1.0 - gate)).astype(BF)

    d_key = (mm_nt(d_value, feed_content_weights) * (2.0 * soft * jax.nn.sigmoid(key_act))).astype(BF)
    content_share = rep_scatter_rows(mm_tn(squared, d_value).astype(BF))
    d_key_chan = mm_nt(d_key, wl)
    d_recept_chan = mm_nt(d_gate, wa)
    moved = d_key_chan * feed_lerp_factors[0] + d_recept_chan * feed_lerp_factors[1]
    d_normed2 = d_key_chan + d_recept_chan - moved + after(moved)
    feed_lerp_part = jnp.stack(
        [jnp.sum(d_key_chan * delta2, axis=0), jnp.sum(d_recept_chan * delta2, axis=0)]
    )
    d_normed2 = scatter_rows(d_normed2.astype(BF)).astype(F32)
    lookup_share = rep_scatter_cols(mm_tn(key_chan, d_key).astype(BF))
    accept_share = rep_scatter_cols(mm_tn(recept_chan, d_gate).astype(BF))
    d_normed2, content_share = hold(d_normed2, content_share)

    def norm_back(unit, rstd, e):
        return rstd * (
            e
            - jnp.mean(e, axis=-1, keepdims=True)
            - unit * jnp.mean(e * unit, axis=-1, keepdims=True)
        )

    d_residual = d_out + norm_back(unit2, rstd2, d_normed2 * second_scaling_factor)
    norm2_part = jnp.stack([jnp.sum(d_normed2 * unit2, axis=0), jnp.sum(d_normed2, axis=0)])

    d_branch = gather_rows(d_residual.astype(BF))
    d_mixed = mm_nt(d_branch, emission_weights)
    emission_share = rep_scatter_rows(mm_tn(mixed, d_branch).astype(BF))
    d_mixed, lookup_share = hold(d_mixed, lookup_share)
    d_r, d_k, d_v, d_g, d_raw, mix_vec = wkv(
        length, r, k, v, g, w, u, gn_gain, gn_bias, d_mixed
    )
    d_r, accept_share, emission_share = hold(d_r, accept_share, emission_share)
    share_one = rep_scatter_cols(
        jnp.concatenate([mm_tn(xk, d_k), mm_tn(xv, d_v)], axis=1).astype(BF)
    )
    share_two = rep_scatter_cols(
        jnp.concatenate([mm_tn(xr, d_r), mm_tn(xg, d_g)], axis=1).astype(BF)
    )

    def settle(share, parts):
        total = rep_gather(cols_to_rows(share)).reshape(c, n, parts, -1)
        return [total[:, :, i].reshape(c, -1) for i in range(parts)]

    feed_content_grads = rep_gather(content_share)
    emission_weights_grads = rep_gather(emission_share)
    (feed_lookup_grads,) = settle(lookup_share, 1)
    (feed_acceptor_grads,) = settle(accept_share, 1)
    lookup_weights_grads, content_weights_grads = settle(share_one, 2)
    acceptor_weights_grads, valve_weights_grads = settle(share_two, 2)
    d_normed, vec_part, widen_part, narrow_part, fnarrow_part = back(
        length,
        tokens,
        hidden,
        low,
        (d_k, d_v, d_r, d_g),
        d_raw,
        (gain1, shift1, lerp_factors, nh, widen_low, fh, fwiden_mine.astype(BF)),
        (wk, wv, wr, wg),
    )
    d_normed = scatter_rows(d_normed).astype(F32)
    tok_f = tok_home.astype(F32)
    center1 = tok_f - jnp.mean(tok_f, axis=-1, keepdims=True)
    rstd1 = lax.rsqrt(jnp.mean(center1 * center1, axis=-1, keepdims=True) + norm_eps)
    token_grad = d_residual + norm_back(center1 * rstd1, rstd1, d_normed * first_scaling_factor)

    small = scatter_cols(
        jnp.concatenate(
            [vec_part, widen_part, narrow_part, fnarrow_part, norm2_part, feed_lerp_part], axis=0
        )
    )
    fwiden_part = lax.dot_general(
        low, d_raw, (((0,), (0,)), ((), ())), precision=lax.Precision.HIGHEST
    )
    small = lax.psum(jnp.concatenate([small, fwiden_part, mix_vec], axis=0), "rep")
    small = gather_cols(small)
    cuts = np.cumsum([8, 5 * ranks, 5 * ranks, fd, 2, 2, fd, 4])
    vec, widen_g, narrow_g, fnarrow_g, norm2_g, feed_lerp_g, fwiden_g, mix_g = (
        small[a:b] for a, b in zip([0, *cuts[:-1]], cuts)
    )
    return (
        layer_output.reshape(seqs, length, d),
        token_grad.reshape(seqs, length, d),
        vec[6],
        vec[7],
        vec[:6],
        narrow_g.T,
        widen_g.reshape(5, ranks, d),
        mix_g[3],
        fnarrow_g.T,
        fwiden_g,
        mix_g[0],
        acceptor_weights_grads,
        lookup_weights_grads,
        content_weights_grads,
        valve_weights_grads,
        emission_weights_grads,
        mix_g[1],
        mix_g[2],
        norm2_g[0],
        norm2_g[1],
        feed_lerp_g,
        feed_lookup_grads,
        feed_content_grads,
        feed_acceptor_grads,
    )


def solution(mesh):
    seq = P(("fsdp", "rep"), None, None)
    row = P("fsdp", None)
    in_specs = (
        (seq, P(("fsdp", "rep")), seq) + (P(),) * 9 + (row,) * 5 + (P(),) * 5 + (row,) * 3
    )
    out_specs = (seq, seq) + (P(),) * 9 + (row,) * 5 + (P(),) * 5 + (row,) * 3
    return jax.shard_map(body, mesh=mesh, in_specs=in_specs, out_specs=out_specs, check_vma=False)
```

```python
import functools

import jax
import jax.numpy as jnp
import numpy as np
from jax import lax
from jax.experimental import pallas as pl
from jax.experimental.pallas import tpu as pltpu
from jax.sharding import PartitionSpec as P

HEADS = 32
norm_eps = 1e-05
group_eps = 1.0
BF = jnp.bfloat16
F32 = jnp.float32
MIB = 1 << 20
SHORT = pl.CostEstimate(flops=1, bytes_accessed=1, transcendentals=0)


def lasts(us):
    return pl.CostEstimate(flops=int(us * 1e9), bytes_accessed=1, transcendentals=0)


def mm(a, b):
    return jnp.dot(a, b, preferred_element_type=F32)


def mm_nt(a, b):
    return lax.dot_general(a, b, (((1,), (1,)), ((), ())), preferred_element_type=F32)


def mm_tn(a, b):
    return lax.dot_general(a, b, (((0,), (0,)), ((), ())), preferred_element_type=F32)


def halves(v):
    high = v.astype(BF)
    return high, (v - high.astype(F32)).astype(BF)


def hold(*values):
    return lax.optimization_barrier(values)


def paired():
    return lax.axis_size("fsdp") == 8


def swap(v, m):
    return lax.ppermute(v, "fsdp", [(i, i ^ m) for i in range(8)])


def place():
    me = lax.axis_index("fsdp")
    return me // 2, lax.rem(me, 2)


def by_core(core, mine, other, axis):
    return jnp.where(
        core == 0,
        jnp.concatenate([mine, other], axis=axis),
        jnp.concatenate([other, mine], axis=axis),
    )


def gather_tokens(v, *later):
    if not paired():
        return (lax.all_gather(v, "fsdp", axis=0, tiled=True), *later)
    r = v.shape[0] // 2
    a, b = v[:r], v[r:]
    a1, b1 = swap(a, 2), swap(b, 4)
    a2 = swap(jnp.concatenate([a, a1], axis=0), 4)
    b2 = swap(jnp.concatenate([b, b1], axis=0), 2)
    if later:
        a2, b2, *later = hold(a2, b2, *later)
    near = jnp.concatenate([v, a1, b2[:r], a2[:r], b1, a2[r:], b2[r:]], axis=0)
    return (jnp.concatenate([near, swap(near, 1)], axis=0), *later)


def scatter_tokens(v):
    if not paired():
        return lax.psum_scatter(v, "fsdp", scatter_dimension=0, tiled=True).astype(F32)
    r = v.shape[0] // 8
    got = swap(v[4 * r :], 1)
    pair = lambda q: v[q * r : (q + 1) * r].astype(F32) + got[q * r : (q + 1) * r].astype(F32)
    far = [swap(pair(q).astype(BF), 2 * q) for q in (1, 2, 3)]
    return pair(0) + (far[0].astype(F32) + far[1].astype(F32)) + far[2].astype(F32)


def chip_exchange(take, put, out):
    chip, _ = place()
    out = put(out, chip, take(chip))
    for q in (1, 2, 3):
        out = put(out, chip ^ q, swap(take(chip ^ q), 2 * q))
    return out


def home_features(v, beside):
    if not paired():
        return lax.all_to_all(v, "fsdp", split_axis=0, concat_axis=1, tiled=True), beside()
    chip, core = place()
    r, c = v.shape[0] // 8, v.shape[1]
    both = by_core(core, v[: 4 * r], swap(v[4 * r :], 1), 1)
    pieces = [both[:r]] + [swap(both[q * r : (q + 1) * r], 2 * q) for q in (1, 2, 3)]
    held = hold(*pieces, *beside())
    pieces, others = held[:4], held[4:]
    out = jnp.zeros((r, 8 * c), v.dtype)
    for q in range(4):
        out = lax.dynamic_update_slice_in_dim(out, pieces[q], (chip ^ q) * (2 * c), 1)
    return out, others


def spread_features(v):
    if not paired():
        return lax.all_to_all(v, "fsdp", split_axis=1, concat_axis=0, tiled=True)
    chip, core = place()
    c = v.shape[1] // 8
    near = []
    for q in range(4):
        piece = lax.dynamic_slice_in_dim(v, (chip ^ q) * (2 * c), 2 * c, 1)
        near.append(piece if q == 0 else swap(piece, 2 * q))
    near = jnp.concatenate(near, axis=0)
    cut = lambda which: lax.dynamic_slice_in_dim(near, which * c, c, 1)
    return jnp.concatenate([cut(core), swap(cut(1 - core), 1)], axis=0)


def orders():
    me = lax.axis_index("fsdp")
    return jnp.stack([me ^ m for m in (0, 2, 4, 6, 1, 3, 5, 7)]).astype(jnp.int32)


def pack_kernel(count, order, *refs):
    parts, (near, far) = refs[:count], refs[count:]
    for half, out in enumerate((near, far)):

        @pl.when(pl.program_id(0) // 4 == half)
        def _():
            at = 0
            for p in parts:
                out[0, :, at : at + p.shape[1]] = p[...]
                at += p.shape[1]


def unpack_kernel(widths, order, *refs):
    pieces, outs = refs[:8], refs[8:]
    for m, piece in enumerate(pieces):

        @pl.when(pl.program_id(0) == m)
        def _():
            at = 0
            for w, out in zip(widths, outs):
                out[...] = piece[0, :, at : at + w]
                at += w


class Exchange:
    def __init__(self, parts, side):
        self.side = side
        self.parts = parts
        if not paired():
            return
        if side == 1:
            r, self.widths = parts[0].shape[0], [p.shape[1] // 8 for p in parts]
            at = lambda m, o: (0, o[m])
        else:
            r, self.widths = parts[0].shape[0] // 8, [p.shape[1] for p in parts]
            at = lambda m, o: (o[m], 0)
        total = sum(self.widths)
        out = jax.ShapeDtypeStruct((4, r, total), parts[0].dtype)
        self.near, self.far = pl.pallas_call(
            functools.partial(pack_kernel, len(parts)),
            grid_spec=pltpu.PrefetchScalarGridSpec(
                num_scalar_prefetch=1,
                grid=(8,),
                in_specs=[pl.BlockSpec((r, w), at) for w in self.widths],
                out_specs=[
                    pl.BlockSpec((1, r, total), lambda m, o: (jnp.minimum(m, 3), 0, 0)),
                    pl.BlockSpec((1, r, total), lambda m, o: (jnp.maximum(m - 4, 0), 0, 0)),
                ],
            ),
            out_shape=[out, out],
            compiler_params=pltpu.CompilerParams(vmem_limit_bytes=32 * MIB),
            name="pack",
        )(orders(), *parts)

    def across_cores(self):
        if paired():
            self.far = swap(self.far, 1)

    def after(self, *values):
        if not paired():
            return values
        *values, self.near, self.far = hold(*values, self.near, self.far)
        return values

    def parcels(self):
        if not paired():
            return []
        return [
            jnp.concatenate([self.near[q : q + 1], self.far[q : q + 1]], axis=0) for q in (1, 2, 3)
        ]

    def got_parcels(self):
        return self.got if paired() else []

    def across_chips(self, parcels=None):
        if paired():
            parcels = parcels or self.parcels()
            self.got = [swap(p, 2 * q) for q, p in zip((1, 2, 3), parcels)]

    def arrived(self, *values):
        if not paired():
            return values
        *values, g1, g2, g3 = hold(*values, *self.got)
        self.got = [g1, g2, g3]
        return values

    def results(self):
        if not paired():
            split, concat = (1, 0) if self.side == 1 else (0, 1)
            return [
                lax.all_to_all(p, "fsdp", split_axis=split, concat_axis=concat, tiled=True)
                for p in self.parts
            ]
        _, r, total = self.near.shape
        block = lambda i: pl.BlockSpec((1, r, total), lambda m, o: (i, 0, 0))
        if self.side == 1:
            at = lambda m, o: (o[m], 0)
            shape = lambda w: (8 * r, w)
        else:
            at = lambda m, o: (0, o[m])
            shape = lambda w: (r, 8 * w)
        return pl.pallas_call(
            functools.partial(unpack_kernel, self.widths),
            grid_spec=pltpu.PrefetchScalarGridSpec(
                num_scalar_prefetch=1,
                grid=(8,),
                in_specs=[block(0)] * 4 + [block(0)] + [block(1)] * 3,
                out_specs=[pl.BlockSpec((r, w), at) for w in self.widths],
            ),
            out_shape=[jax.ShapeDtypeStruct(shape(w), self.near.dtype) for w in self.widths],
            compiler_params=pltpu.CompilerParams(vmem_limit_bytes=32 * MIB),
            name="unpack",
        )(orders(), self.near, *self.got, self.far, *self.got)


def rep_scatter(v):
    return lax.psum_scatter(v, "rep", scatter_dimension=0, tiled=True)


def rep_gather(v):
    return lax.all_gather(v, "rep", axis=0, tiled=True)


def share_kernel(shares, *refs):
    *parts, out = refs
    at = 0
    for p in parts:
        rows, w = p.shape[0] // shares, p.shape[1]
        for i in range(shares):
            out[i, 0, :, at : at + w] = p[i * rows : (i + 1) * rows, :]
        at += w


def rep_scatter_cols(parts):
    n, z = lax.axis_size("fsdp"), lax.axis_size("rep")
    rows = parts[0].shape[0]
    c = sum(p.shape[1] for p in parts)
    v = pl.pallas_call(
        functools.partial(share_kernel, z),
        grid=(n,),
        in_specs=[pl.BlockSpec((rows // n, p.shape[1]), lambda i: (i, 0)) for p in parts],
        out_specs=pl.BlockSpec((z, 1, rows // (n * z), c), lambda i: (0, i, 0, 0)),
        out_shape=jax.ShapeDtypeStruct((z, n, rows // (n * z), c), parts[0].dtype),
        compiler_params=pltpu.CompilerParams(vmem_limit_bytes=32 * MIB),
        cost_estimate=SHORT,
        name="shares",
    )(*parts)
    return rep_scatter(v.reshape(rows, c))


def widen_kernel(*refs):
    joined, *outs = refs
    at = 0
    for out in outs:
        w = out.shape[1]
        out[...] = joined[:, at : at + w].astype(F32)
        at += w


def widened(v, widths):
    r = v.shape[0]
    rows = min(r, 32)
    return pl.pallas_call(
        widen_kernel,
        grid=(r // rows,),
        in_specs=[pl.BlockSpec((rows, v.shape[1]), lambda i: (i, 0))],
        out_specs=[pl.BlockSpec((rows, w), lambda i: (i, 0)) for w in widths],
        out_shape=[jax.ShapeDtypeStruct((r, w), F32) for w in widths],
        compiler_params=pltpu.CompilerParams(vmem_limit_bytes=32 * MIB),
        cost_estimate=SHORT,
        name="widened",
    )(v)


def rep_sum(v):
    n = lax.axis_size("rep")
    total = v.astype(F32)
    for s in range(1, n):
        total = total + lax.ppermute(v, "rep", [(i, (i + s) % n) for i in range(n)]).astype(F32)
    return total


def scatter_features(v):
    if not paired():
        return lax.psum_scatter(v, "fsdp", scatter_dimension=1, tiled=True).astype(F32)
    chip, core = place()
    r = v.shape[0]
    v = v.reshape(r, 4, 2, -1)
    cut = lambda which: lax.dynamic_index_in_dim(v, which, 2, keepdims=False).transpose(1, 0, 2)
    pair = cut(core).astype(F32) + swap(cut(1 - core), 1).astype(F32)
    low = pair.astype(BF)
    total = lax.dynamic_index_in_dim(pair, chip, 0, keepdims=False)
    for q in (1, 2, 3):
        got = swap(lax.dynamic_index_in_dim(low, chip ^ q, 0, keepdims=False), 2 * q)
        total = total + got.astype(F32)
    return total


def gather_features(v):
    if not paired():
        return lax.all_gather(v, "fsdp", axis=1, tiled=True)
    chip, core = place()
    r, c = v.shape
    both = by_core(core, v, swap(v, 1), 1)
    out = jnp.zeros((r, 8 * c), v.dtype)
    for q in range(4):
        got = both if q == 0 else swap(both, 2 * q)
        out = lax.dynamic_update_slice_in_dim(out, got, (chip ^ q) * (2 * c), 1)
    return out


def whole_block(a):
    return pl.BlockSpec(a.shape, lambda *_: (0,) * a.ndim, pipeline_mode=pl.Buffered(1))


def shifted(v):
    first = lax.broadcasted_iota(jnp.int32, v.shape, 0) == 0
    return jnp.where(first, 0.0, pltpu.roll(v, 1, 0))


def shifted_back(v):
    last = lax.broadcasted_iota(jnp.int32, v.shape, 0) == v.shape[0] - 1
    return jnp.where(last, 0.0, pltpu.roll(v, v.shape[0] - 1, 0))


def normal_rows(v):
    center = v - jnp.mean(v, axis=-1, keepdims=True)
    spread = jnp.mean(center * center, axis=-1, keepdims=True)
    return center * lax.rsqrt(spread + norm_eps)


def front_kernel(
    ranks, tok, gain, shift, lerp, narrow, widen, fnarrow, xk, xv, xr, xg, hid, low, nh, nl, wb, fh, fl
):
    @pl.when(pl.program_id(0) == 0)
    def _():
        nh[...], nl[...] = halves(jnp.transpose(narrow[...]))
        fh[...], fl[...] = halves(jnp.transpose(fnarrow[...]))
        wb[...] = widen[...].astype(BF)

    normed = normal_rows(tok[...].astype(F32)) * gain[...] + shift[...]
    delta = shifted(normed) - normed
    bh, bl = halves(normed + delta * lerp[0:1, :])
    hidden = jnp.tanh(mm(bh, nh[...]) + mm(bh, nl[...]) + mm(bl, nh[...]))
    hid[...] = hidden
    hb = hidden.astype(BF)
    for f, out in ((1, xk), (2, xv), (3, xr), (4, xg), (0, None)):
        rows = slice(f * ranks, (f + 1) * ranks)
        x = normed + delta * (lerp[f + 1 : f + 2, :] + mm(hb[:, rows], wb[rows, :]))
        if out is not None:
            out[...] = x.astype(BF)
        else:
            dh, dl = halves(x)
            low[...] = jnp.tanh(mm(dh, fh[...]) + mm(dh, fl[...]) + mm(dl, fh[...]))


def front(seq_len, tokens, gain, shift, lerp, narrow, widen, fnarrow):
    g, d = tokens.shape
    ranks = widen.shape[0] // 5
    fd = fnarrow.shape[0]
    per_seq = lambda w: pl.BlockSpec((seq_len, w), lambda s: (s, 0))
    return pl.pallas_call(
        functools.partial(front_kernel, ranks),
        grid=(g // seq_len,),
        in_specs=[per_seq(d)]
        + [whole_block(a) for a in (gain, shift, lerp, narrow, widen, fnarrow)],
        out_specs=[per_seq(d)] * 4 + [per_seq(5 * ranks), per_seq(fd)],
        out_shape=[jax.ShapeDtypeStruct((g, d), BF)] * 4
        + [
            jax.ShapeDtypeStruct((g, 5 * ranks), F32),
            jax.ShapeDtypeStruct((g, fd), F32),
        ],
        scratch_shapes=[
            pltpu.VMEM((d, 5 * ranks), BF),
            pltpu.VMEM((d, 5 * ranks), BF),
            pltpu.VMEM((5 * ranks, d), BF),
            pltpu.VMEM((d, fd), BF),
            pltpu.VMEM((d, fd), BF),
        ],
        compiler_params=pltpu.CompilerParams(vmem_limit_bytes=48 * MIB),
        cost_estimate=lasts(22),
        name="token_shift",
    )(tokens, gain, shift, lerp, narrow, widen, fnarrow)


def back_kernel(
    ranks,
    tok,
    hid,
    low,
    dk,
    dv,
    dr,
    dg,
    draw,
    gain,
    shift,
    lerp,
    narrow,
    widen,
    fnarrow,
    fwiden,
    wk,
    wv,
    wr,
    wg,
    dn_out,
    vec_out,
    dwid_out,
    dnar_out,
    dfn_out,
    narrow_low,
    widen_low,
    fnarrow_low,
    fwiden_low,
):
    @pl.when(pl.program_id(0) == 0)
    def _():
        narrow_low[...] = narrow[...].astype(BF)
        widen_low[...] = widen[...].astype(BF)
        fnarrow_low[...] = fnarrow[...].astype(BF)
        fwiden_low[...] = fwiden[...].astype(BF)
        for ref in (vec_out, dwid_out, dnar_out, dfn_out):
            ref[...] = jnp.zeros_like(ref)

    unit = normal_rows(tok[...].astype(F32))
    normed = unit * gain[...] + shift[...]
    delta = shifted(normed) - normed
    hidden = hid[...]
    hb = hidden.astype(BF)
    lowv = low[...]
    colsum = lambda v: jnp.sum(v, axis=0, keepdims=True)
    dlow = mm_nt(draw[...].astype(BF), fwiden_low[...]) * (1.0 - lowv * lowv)
    dlow = dlow.astype(BF)
    total = jnp.zeros(normed.shape, F32)
    moved = jnp.zeros(normed.shape, F32)
    dhid = []
    for f, d_ref, w_ref in (
        (0, None, None),
        (1, dk, wk),
        (2, dv, wv),
        (3, dr, wr),
        (4, dg, wg),
    ):
        rows = slice(f * ranks, (f + 1) * ranks)
        mu = lerp[f + 1 : f + 2, :] + mm(hb[:, rows], widen_low[rows, :])
        if f == 0:
            dx = mm(dlow, fnarrow_low[...])
            dfn_out[...] += mm_tn(dlow, (normed + delta * mu).astype(BF))
        else:
            dx = mm_nt(d_ref[...], w_ref[...])
        total = total + dx
        moved = moved + dx * mu
        doff = dx * delta
        vec_out[f + 1 : f + 2, :] += colsum(doff)
        db = doff.astype(BF)
        dwid_out[rows, :] += mm_tn(hb[:, rows], db)
        dhid.append(mm_nt(db, widen_low[rows, :]))
    dpre = (jnp.concatenate(dhid, axis=1) * (1.0 - hidden * hidden)).astype(BF)
    dblend = mm(dpre, narrow_low[...])
    base = lerp[0:1, :]
    dnar_out[...] += mm_tn(dpre, (normed + delta * base).astype(BF))
    vec_out[0:1, :] += colsum(dblend * delta)
    total = total + dblend
    moved = moved + dblend * base
    dn = total - moved + shifted_back(moved)
    vec_out[6:7, :] += colsum(dn * unit)
    vec_out[7:8, :] += colsum(dn)
    dn_out[...] = dn.astype(BF)


def back(seq_len, tokens, hid, low, grads, draw, params, weights):
    g, d = tokens.shape
    c = draw.shape[1]
    gain, shift, lerp, narrow, widen, fnarrow, fwiden = params
    ranks = widen.shape[0] // 5
    fd = low.shape[1]
    per_seq = lambda w: pl.BlockSpec((seq_len, w), lambda s: (s, 0))
    kept = lambda r: pl.BlockSpec((r, d), lambda s: (0, 0))
    return pl.pallas_call(
        functools.partial(back_kernel, ranks),
        grid=(g // seq_len,),
        in_specs=[per_seq(d), per_seq(5 * ranks), per_seq(fd)]
        + [per_seq(c)] * 5
        + [whole_block(a) for a in params]
        + [whole_block(a) for a in weights],
        out_specs=[per_seq(d), kept(8), kept(5 * ranks), kept(5 * ranks), kept(fd)],
        out_shape=[
            jax.ShapeDtypeStruct((g, d), BF),
            jax.ShapeDtypeStruct((8, d), F32),
            jax.ShapeDtypeStruct((5 * ranks, d), F32),
            jax.ShapeDtypeStruct((5 * ranks, d), F32),
            jax.ShapeDtypeStruct((fd, d), F32),
        ],
        scratch_shapes=[
            pltpu.VMEM((5 * ranks, d), BF),
            pltpu.VMEM((5 * ranks, d), BF),
            pltpu.VMEM((fd, d), BF),
            pltpu.VMEM((fd, c), BF),
        ],
        compiler_params=pltpu.CompilerParams(vmem_limit_bytes=56 * MIB),
        cost_estimate=SHORT,
        name="token_shift_back",
    )(tokens, hid, low, *grads, draw, *params, *weights)


def level_tables(length):
    p = np.arange(length)[:, None]
    u = np.arange(length)[None, :]
    levels = int(length).bit_length() - 1
    spans = []
    for l in range(1, levels):
        b = 1 << l
        same = (p // b) == (u // b)
        upper = (p // b) % 2 == 1
        spans.append(same & np.where(upper, u < p, u > p))
    spans = np.concatenate(spans, 0).astype(np.float32)
    diff = p ^ u
    level = np.where(u < p, np.floor(np.log2(np.maximum(diff, 1))), -1)
    return levels, spans, level.astype(np.int32)


def per_head(lanes, width, count, v):
    out = jnp.sum(jnp.where(lanes == 0, v, 0.0), axis=1, keepdims=True)
    if count == 1:
        return jnp.broadcast_to(out, v.shape)
    for h in range(1, count):
        one = jnp.sum(jnp.where(lanes == h, v, 0.0), axis=1, keepdims=True)
        out = jnp.where(lanes == h, one, out)
    return out


def stack_heads(lanes, count, v):
    zero = jnp.zeros_like(v)
    return jnp.concatenate([jnp.where(lanes == h, v, zero) for h in range(count)], axis=0)


def side_by_side(length, count, v):
    return jnp.concatenate([v[h * length : (h + 1) * length] for h in range(count)], axis=1)


def mix_forward(levels, count, width, r, k, v, w, u, spans, level):
    length, lanes_n = r.shape
    lanes = lax.broadcasted_iota(jnp.int32, (length, lanes_n), 1) // width
    wh, wl = halves(w)
    gaps = mm(spans, wh) + mm(spans, wl)
    factors = [None] + [
        jnp.exp(gaps[l * length : (l + 1) * length]) for l in range(levels - 1)
    ]
    level2 = jnp.concatenate([level] * count, axis=0)
    scores = jnp.zeros((length * count, length), F32)
    parts = []
    for l in range(levels):
        e = factors[l]
        re = (r if e is None else r * e).astype(BF)
        ke = (k if e is None else k * e).astype(BF)
        parts.append((e, re, ke))
        scores = scores + jnp.where(
            level2 == l, mm_nt(stack_heads(lanes, count, re), ke), 0.0
        )
    vb = v.astype(BF)
    bonus = per_head(lanes, width, count, r * u * k)
    wkv = (
        mm(side_by_side(length, count, scores).astype(BF), stack_heads(lanes, count, vb))
        + bonus * v
    )
    center = wkv - per_head(lanes, width, count, wkv) * (1.0 / width)
    spread = per_head(lanes, width, count, center * center) * (1.0 / width)
    rstd = lax.rsqrt(spread + group_eps)
    return lanes, level2, parts, scores, bonus, vb, center * rstd, rstd


def wkv_kernel(levels, count, width, r, k, v, g, w, u, gain, bias, spans, level, out):
    unit = mix_forward(
        levels, count, width, r[...], k[...], v[...], w[...], u[...], spans[...], level[...]
    )[6]
    gate = g[...]
    out[...] = ((unit * gain[...] + bias[...]) * (gate * jax.nn.sigmoid(gate))).astype(BF)


def wkv_back_kernel(
    levels,
    count,
    width,
    r_ref,
    k_ref,
    v_ref,
    g_ref,
    w_ref,
    dm_ref,
    u_ref,
    gain_ref,
    bias_ref,
    spans,
    spans_t,
    level_ref,
    dr_out,
    dk_out,
    dv_out,
    dg_out,
    draw_out,
    vec_out,
):
    @pl.when(pl.program_id(1) == 0)
    def _():
        vec_out[...] = jnp.zeros_like(vec_out)

    r, k, v, w, u = r_ref[...], k_ref[...], v_ref[...], w_ref[...], u_ref[...]
    level = level_ref[...]
    lanes, level2, parts, scores, bonus, vb, unit, rstd = mix_forward(
        levels, count, width, r, k, v, w, u, spans[...], level
    )
    length = r.shape[0]
    heads = functools.partial(per_head, lanes, width, count)
    stack = functools.partial(stack_heads, lanes, count)
    beside = functools.partial(side_by_side, length, count)
    colsum = lambda x: jnp.sum(x, axis=0, keepdims=True)

    gate, dm, gain = g_ref[...], dm_ref[...], gain_ref[...]
    sig = jax.nn.sigmoid(gate)
    scaled = unit * gain + bias_ref[...]
    dg_out[...] = (dm * scaled * sig * (1.0 + gate * (1.0 - sig))).astype(BF)
    dscaled = dm * gate * sig
    dunit = dscaled * gain
    dwkv = rstd * (
        dunit - heads(dunit) * (1.0 / width) - unit * (heads(dunit * unit) * (1.0 / width))
    )
    db = dwkv.astype(BF)
    dbs = stack(db)
    dscores = mm_nt(dbs, vb)

    def turned(x):
        return jnp.concatenate(
            [jnp.transpose(x[h * length : (h + 1) * length]) for h in range(count)], axis=0
        )

    dscores_t = turned(dscores)
    level_t = jnp.transpose(level)
    level2_t = jnp.concatenate([level_t] * count, axis=0)
    dv = mm(beside(turned(scores)).astype(BF), dbs) + bonus * dwkv
    dbonus = heads(dwkv * v)
    dr = dbonus * u * k
    dk = dbonus * u * r
    flows = []
    for l in range(levels):
        e, re, ke = parts[l]
        dre = mm(beside(jnp.where(level2 == l, dscores, 0.0)).astype(BF), stack(ke))
        dke = mm(beside(jnp.where(level2_t == l, dscores_t, 0.0)).astype(BF), stack(re))
        if e is None:
            dr = dr + dre
            dk = dk + dke
        else:
            dre = dre * e
            dke = dke * e
            dr = dr + dre
            dk = dk + dke
            flows.append(dre * r + dke * k)
    fh, fl = halves(jnp.concatenate(flows, axis=0))
    dw = mm(spans_t[...], fh) + mm(spans_t[...], fl)
    draw = dw * w
    dr_out[...] = dr.astype(BF)
    dk_out[...] = dk.astype(BF)
    dv_out[...] = dv.astype(BF)
    draw_out[...] = draw
    vec_out[0:1, :] += colsum(dbonus * r * k)
    vec_out[1:2, :] += colsum(dscaled * unit)
    vec_out[2:3, :] += colsum(dscaled)
    vec_out[3:4, :] += colsum(draw)


def wkv(seq_len, r, k, v, g, w, u, gain, bias, dmixed=None):
    rows, c = r.shape
    heads_here = c * HEADS // D_OF(u, c)
    width = c // heads_here
    count = 2 if heads_here % 2 == 0 else 1
    lanes = count * width
    levels, spans, level = level_tables(seq_len)
    spans_a = jnp.asarray(spans, BF)
    level_a = jnp.asarray(level)
    cols = pl.BlockSpec((seq_len, lanes), lambda p, s: (s, p))
    vec = pl.BlockSpec((1, lanes), lambda p, s: (0, p))
    grid = (c // lanes, rows // seq_len)
    flops = rows * c * seq_len * 2 * 16
    params = pltpu.CompilerParams(vmem_limit_bytes=40 * MIB)
    if dmixed is None:
        return pl.pallas_call(
            functools.partial(wkv_kernel, levels, count, width),
            grid=grid,
            in_specs=[cols] * 5 + [vec] * 3 + [whole_block(spans_a), whole_block(level_a)],
            out_specs=cols,
            out_shape=jax.ShapeDtypeStruct((rows, c), BF),
            compiler_params=params,
            cost_estimate=SHORT,
            name="decay_mix",
        )(r, k, v, g, w, u, gain, bias, spans_a, level_a)
    spans_t = jnp.asarray(
        np.concatenate([s.T for s in spans.reshape(levels - 1, seq_len, seq_len)], 1), BF
    )
    return pl.pallas_call(
        functools.partial(wkv_back_kernel, levels, count, width),
        grid=grid,
        in_specs=[cols] * 6
        + [vec] * 3
        + [whole_block(spans_a), whole_block(spans_t), whole_block(level_a)],
        out_specs=[cols] * 5 + [pl.BlockSpec((4, lanes), lambda p, s: (0, p))],
        out_shape=[jax.ShapeDtypeStruct((rows, c), BF)] * 4
        + [jax.ShapeDtypeStruct((rows, c), F32), jax.ShapeDtypeStruct((4, c), F32)],
        compiler_params=params,
        cost_estimate=SHORT,
        name="decay_mix_back",
    )(r, k, v, g, w, dmixed, u, gain, bias, spans_a, spans_t, level_a)


def D_OF(u, c):
    return c * lax.axis_size("fsdp")


def step_shift(length, v, back=False):
    rows = v.shape[0]
    at = lax.rem(lax.broadcasted_iota(jnp.int32, v.shape, 0), length)
    edge = at == (length - 1 if back else 0)
    return jnp.where(edge, 0.0, pltpu.roll(v, rows - 1 if back else 1, 0))


def feed_kernel(length, n2, lerp, wla, wc, *refs):
    kc_out, sq_out, fac_out, va_out = refs[-4:]
    n = n2[...].astype(F32)
    delta = step_shift(length, n) - n
    kc = (n + delta * lerp[0:1, :]).astype(BF)
    kc_out[...] = kc
    act = mm(kc, wla[:, : wc.shape[0]])
    soft = jnp.maximum(act, 0.0) + jnp.log1p(jnp.exp(-jnp.abs(act)))
    fac_out[...] = 2.0 * soft * jax.nn.sigmoid(act)
    sq = (soft * soft).astype(BF)
    sq_out[...] = sq
    va_out[...] = mm(sq, wc[...]).astype(BF)


def feed(length, n2, lerp, wla, wc, part, earlier=()):
    g, d = n2.shape
    f = wc.shape[0]
    half = g // 2
    rows = 2 * length if half % (2 * length) == 0 else length
    if half % rows:
        rows = half
    first = part * (half // rows)
    block = lambda w: pl.BlockSpec((rows, w), lambda s: (first + s, 0))
    shape = lambda w, t: jax.ShapeDtypeStruct((g, w), t)
    return pl.pallas_call(
        functools.partial(feed_kernel, length),
        grid=(half // rows,),
        in_specs=[block(d)]
        + [whole_block(a) for a in (lerp, wla, wc)]
        + [pl.BlockSpec(memory_space=pl.ANY)] * len(earlier),
        out_specs=[block(d), block(f), block(f), block(d)],
        out_shape=[shape(d, BF), shape(f, BF), shape(f, F32), shape(d, BF)],
        input_output_aliases={4 + i: i for i in range(len(earlier))},
        compiler_params=pltpu.CompilerParams(vmem_limit_bytes=52 * MIB),
        cost_estimate=lasts(8),
        name="feed",
    )(n2, lerp, wla, wc, *earlier)


def gate_kernel(length, n2, lerp, wla, rc_out, gate_out):
    n = n2[...].astype(F32)
    rc = (n + (step_shift(length, n) - n) * lerp[1:2, :]).astype(BF)
    rc_out[...] = rc
    gate_out[...] = jax.nn.sigmoid(mm(rc, wla[:, wla.shape[1] - gate_out.shape[1] :])).astype(BF)


def feed_gate(length, n2, lerp, wla):
    g, d = n2.shape
    c = d // lax.axis_size("fsdp")
    rows = 2 * length if g % (2 * length) == 0 else length
    block = lambda w: pl.BlockSpec((rows, w), lambda s: (s, 0))
    return pl.pallas_call(
        functools.partial(gate_kernel, length),
        grid=(g // rows,),
        in_specs=[block(d), whole_block(lerp), whole_block(wla)],
        out_specs=[block(d), block(c)],
        out_shape=[jax.ShapeDtypeStruct((g, d), BF), jax.ShapeDtypeStruct((g, c), BF)],
        compiler_params=pltpu.CompilerParams(vmem_limit_bytes=32 * MIB),
        cost_estimate=SHORT,
        name="feed_gate",
    )(n2, lerp, wla)


def feed_back_kernel(length, dv, n2, fac, dgate, lerp, wla, wc, dkey_out, dn_out, vec_out):
    @pl.when(pl.program_id(0) == 0)
    def _():
        vec_out[...] = jnp.zeros_like(vec_out)

    dkey = (mm_nt(dv[...], wc[...]) * fac[...]).astype(BF)
    dkey_out[...] = dkey
    n = n2[...].astype(F32)
    delta = step_shift(length, n) - n
    f = wc.shape[0]
    dk = mm_nt(dkey, wla[:, :f])
    dr = mm_nt(dgate[...], wla[:, f:])
    vec_out[0:1, :] += jnp.sum(dk * delta, axis=0, keepdims=True)
    vec_out[1:2, :] += jnp.sum(dr * delta, axis=0, keepdims=True)
    moved = dk * lerp[0:1, :] + dr * lerp[1:2, :]
    dn_out[...] = (dk + dr - moved + step_shift(length, moved, True)).astype(BF)


def feed_back(length, dv, n2, fac, dgate, lerp, wla, wc):
    g, d = n2.shape
    f, c = wc.shape[0], dgate.shape[1]
    rows = 2 * length if g % (2 * length) == 0 else length
    block = lambda w: pl.BlockSpec((rows, w), lambda s: (s, 0))
    return pl.pallas_call(
        functools.partial(feed_back_kernel, length),
        grid=(g // rows,),
        in_specs=[block(d), block(d), block(f), block(c)]
        + [whole_block(a) for a in (lerp, wla, wc)],
        out_specs=[block(f), block(d), pl.BlockSpec((2, d), lambda s: (0, 0))],
        out_shape=[
            jax.ShapeDtypeStruct((g, f), BF),
            jax.ShapeDtypeStruct((g, d), BF),
            jax.ShapeDtypeStruct((2, d), F32),
        ],
        compiler_params=pltpu.CompilerParams(vmem_limit_bytes=52 * MIB),
        cost_estimate=SHORT,
        name="feed_back",
    )(dv, n2, fac, dgate, lerp, wla, wc)


def body(
    incoming_symbols,
    string_extents,
    adjoint_signal,
    first_scaling_factor,
    first_scaling_shift,
    lerp_factors,
    lerp_narrow_weights,
    lerp_widen_weights,
    fading_baseline,
    fading_narrow_weights,
    fading_widen_weights,
    present_reward,
    acceptor_weights,
    lookup_weights,
    content_weights,
    valve_weights,
    emission_weights,
    cluster_scaling_factor,
    cluster_scaling_shift,
    second_scaling_factor,
    second_scaling_shift_vec,
    feed_lerp_factors,
    feed_lookup_weights,
    feed_content_weights,
    feed_acceptor_weights,
):
    seqs, length, d = incoming_symbols.shape
    n = lax.axis_size("fsdp")
    me = lax.axis_index("fsdp")
    c = d // n
    home = seqs * length
    plane = home * n
    ranks = lerp_widen_weights.shape[1]
    fd = fading_narrow_weights.shape[1]

    tok_home = incoming_symbols.reshape(home, d)
    z = lax.axis_index("rep")
    share = c // lax.axis_size("rep")
    feed_weights = Exchange(
        [
            lax.dynamic_slice_in_dim(t, z * share, share, 0)
            for t in (feed_lookup_weights, feed_acceptor_weights)
        ],
        1,
    )
    feed_weights.across_cores()
    feed_weights.across_chips()
    mix_weights = Exchange(
        (lookup_weights, content_weights, acceptor_weights, valve_weights), 1
    )
    mix_weights.across_cores()
    parcels = mix_weights.parcels()
    tokens, *held = gather_tokens(tok_home, *parcels, *feed_weights.got_parcels())
    mix_weights.across_chips(held[: len(parcels)])
    feed_weights.got = held[len(parcels) :]
    positions = lax.broadcasted_iota(jnp.int32, (seqs, length), 1)
    mask = (positions < string_extents[:, None]).astype(F32).reshape(home, 1)
    d_out = adjoint_signal.reshape(home, d).astype(F32) * mask

    row = lambda v: v.reshape(1, -1)
    mine = lambda v: lax.dynamic_slice_in_dim(v, me * c, c, v.ndim - 1)
    gain1, shift1 = row(first_scaling_factor), row(first_scaling_shift)
    narrow, fnarrow = lerp_narrow_weights.T, fading_narrow_weights.T
    widen = lerp_widen_weights.reshape(5 * ranks, d)
    feed_shares = jnp.concatenate(feed_weights.results(), axis=1).reshape(n, share, -1)
    tokens, feed_shares = hold(tokens, feed_shares)
    feed_full = lax.all_gather(feed_shares, "rep", axis=1, tiled=True).reshape(d, -1)
    xk, xv, xr, xg, hidden, low = front(
        length, tokens, gain1, shift1, lerp_factors, narrow, widen, fnarrow
    )
    (low,) = mix_weights.arrived(low)
    wk, wv, wr, wg = mix_weights.results()
    fwiden_mine = mine(fading_widen_weights)
    w = -jnp.exp(
        mine(row(fading_baseline))
        + jnp.dot(low, fwiden_mine, precision=lax.Precision.HIGHEST)
    )
    k, v, r, g = mm(xk, wk), mm(xv, wv), mm(xr, wr), mm(xg, wg)
    u, gn_gain, gn_bias = (
        mine(row(t)) for t in (present_reward, cluster_scaling_factor, cluster_scaling_shift)
    )
    mixed = wkv(length, r, k, v, g, w, u, gn_gain, gn_bias)
    mixed, feed_full = hold(mixed, feed_full)
    branch = scatter_tokens(mm(mixed, emission_weights).astype(BF))
    residual = tok_home.astype(F32) + branch

    center = residual - jnp.mean(residual, axis=-1, keepdims=True)
    rstd2 = lax.rsqrt(jnp.mean(center * center, axis=-1, keepdims=True) + norm_eps)
    unit2 = center * rstd2
    (normed2,) = gather_tokens((unit2 * second_scaling_factor + second_scaling_shift_vec).astype(BF))
    fc = feed_content_weights.shape[0]
    recept_chan, gate = feed_gate(length, normed2, feed_lerp_factors, feed_full)
    feed_part = lambda *t: feed(length, normed2, feed_lerp_factors, feed_full, feed_content_weights, *t)
    gate, earlier = home_features(gate, lambda: feed_part(0))
    gate = gate.astype(F32)
    (d_value,) = gather_tokens((d_out * gate).astype(BF))
    key_chan, squared, factor, value_part = feed_part(1, earlier)
    d_content = mm_tn(squared, d_value).astype(BF)
    d_value, d_content, value_part = hold(d_value, d_content, value_part)
    content_share = lax.psum_scatter(d_content, "rep", scatter_dimension=0, tiled=True)
    value_act = scatter_tokens(value_part)
    gated = gate * value_act
    layer_output = (residual + gated) * mask
    d_gate = spread_features((d_out * gated * (1.0 - gate)).astype(BF))

    d_key, d_normed2, feed_lerp_part = feed_back(
        length, d_value, normed2, factor, d_gate, feed_lerp_factors, feed_full, feed_content_weights
    )
    d_normed2, content_share = hold(d_normed2, content_share)
    feed_share = rep_scatter_cols(
        (mm_tn(key_chan, d_key).astype(BF), mm_tn(recept_chan, d_gate).astype(BF))
    )
    d_normed2 = scatter_tokens(d_normed2)
    content_sum = rep_gather(content_share)

    def norm_back(unit, rstd, e):
        return rstd * (
            e
            - jnp.mean(e, axis=-1, keepdims=True)
            - unit * jnp.mean(e * unit, axis=-1, keepdims=True)
        )

    d_residual = d_out + norm_back(unit2, rstd2, d_normed2 * second_scaling_factor)
    norm2_part = jnp.stack([jnp.sum(d_normed2 * unit2, axis=0), jnp.sum(d_normed2, axis=0)])

    (d_branch,) = gather_tokens(d_residual.astype(BF))
    d_mixed = mm_nt(d_branch, emission_weights)
    emission_share = rep_scatter(mm_tn(mixed, d_branch).astype(BF))
    d_r, d_k, d_v, d_g, d_raw, mix_vec = wkv(
        length, r, k, v, g, w, u, gn_gain, gn_bias, d_mixed
    )
    d_r, d_k, d_v, d_g, feed_share = hold(d_r, d_k, d_v, d_g, feed_share)
    time_share = rep_scatter_cols(
        [mm_tn(x, t).astype(BF) for x, t in ((xk, d_k), (xv, d_v), (xr, d_r), (xg, d_g))]
    )
    feed_sums = Exchange([feed_share[:, :fc], feed_share[:, fc:]], 0)
    feed_sums.across_cores()
    feed_sums.across_chips()
    d_normed, vec_part, widen_part, narrow_part, fnarrow_part = back(
        length,
        tokens,
        hidden,
        low,
        (d_k, d_v, d_r, d_g),
        d_raw,
        (gain1, shift1, lerp_factors, narrow, widen, fnarrow, fwiden_mine),
        (wk, wv, wr, wg),
    )
    d_normed, content_sum, emission_share = feed_sums.arrived(
        *hold(d_normed, content_sum, emission_share)
    )
    feed_sum = rep_gather(jnp.concatenate(feed_sums.results(), axis=1))
    d_normed = scatter_tokens(d_normed)
    small = scatter_features(
        jnp.concatenate(
            [vec_part, widen_part, narrow_part, fnarrow_part, norm2_part, feed_lerp_part], axis=0
        ).astype(BF)
    )
    fwiden_part = mm_tn(low.astype(BF), d_raw.astype(BF))
    small = rep_sum(jnp.concatenate([small, fwiden_part, mix_vec], axis=0).astype(BF))
    small = gather_features(small.astype(BF)).astype(F32)
    small, time_share = hold(small, time_share)
    time_sums = Exchange([time_share[:, i * c : (i + 1) * c] for i in range(4)], 0)
    time_sums.across_cores()
    time_sums.across_chips()
    time_sum = rep_gather(jnp.concatenate([*time_sums.results(), emission_share], axis=1))
    (feed_content_grads,) = widened(content_sum, (d,))
    feed_lookup_grads, feed_acceptor_grads = widened(feed_sum, (n * fc, n * c))
    (
        lookup_weights_grads,
        content_weights_grads,
        acceptor_weights_grads,
        valve_weights_grads,
        emission_weights_grads,
    ) = widened(time_sum, (d,) * 5)
    tok_f = tok_home.astype(F32)
    center1 = tok_f - jnp.mean(tok_f, axis=-1, keepdims=True)
    rstd1 = lax.rsqrt(jnp.mean(center1 * center1, axis=-1, keepdims=True) + norm_eps)
    token_grad = d_residual + norm_back(center1 * rstd1, rstd1, d_normed * first_scaling_factor)
    cuts = np.cumsum([8, 5 * ranks, 5 * ranks, fd, 2, 2, fd, 4])
    vec, widen_g, narrow_g, fnarrow_g, norm2_g, feed_lerp_g, fwiden_g, mix_g = (
        small[a:b] for a, b in zip([0, *cuts[:-1]], cuts)
    )
    return (
        layer_output.reshape(seqs, length, d),
        token_grad.reshape(seqs, length, d),
        vec[6],
        vec[7],
        vec[:6],
        narrow_g.T,
        widen_g.reshape(5, ranks, d),
        mix_g[3],
        fnarrow_g.T,
        fwiden_g,
        mix_g[0],
        acceptor_weights_grads,
        lookup_weights_grads,
        content_weights_grads,
        valve_weights_grads,
        emission_weights_grads,
        mix_g[1],
        mix_g[2],
        norm2_g[0],
        norm2_g[1],
        feed_lerp_g,
        feed_lookup_grads,
        feed_content_grads,
        feed_acceptor_grads,
    )


def solution(mesh):
    seq = P(("fsdp", "rep"), None, None)
    row = P("fsdp", None)
    in_specs = (
        (seq, P(("fsdp", "rep")), seq) + (P(),) * 9 + (row,) * 5 + (P(),) * 5 + (row,) * 3
    )
    out_specs = (seq, seq) + (P(),) * 9 + (row,) * 5 + (P(),) * 5 + (row,) * 3
    return jax.shard_map(body, mesh=mesh, in_specs=in_specs, out_specs=out_specs, check_vma=False)
```

```python
import functools

import jax
import jax.numpy as jnp
import numpy as np
from jax import lax
from jax.experimental import pallas as pl
from jax.experimental.pallas import tpu as pltpu
from jax.sharding import PartitionSpec as P

HEADS = 32
norm_eps = 1e-05
group_eps = 1.0
BF = jnp.bfloat16
F32 = jnp.float32
MIB = 1 << 20
SHORT = pl.CostEstimate(flops=1, bytes_accessed=1, transcendentals=0)


def lasts(us):
    return pl.CostEstimate(flops=int(us * 1e9), bytes_accessed=1, transcendentals=0)


def mm(a, b):
    return jnp.dot(a, b, preferred_element_type=F32)


def mm_nt(a, b):
    return lax.dot_general(a, b, (((1,), (1,)), ((), ())), preferred_element_type=F32)


def mm_tn(a, b):
    return lax.dot_general(a, b, (((0,), (0,)), ((), ())), preferred_element_type=F32)


def halves(v):
    high = v.astype(BF)
    return high, (v - high.astype(F32)).astype(BF)


def hold(*values):
    return lax.optimization_barrier(values)


def paired():
    return lax.axis_size("fsdp") == 8


def swap(v, m):
    return lax.ppermute(v, "fsdp", [(i, i ^ m) for i in range(8)])


def place():
    me = lax.axis_index("fsdp")
    return me // 2, lax.rem(me, 2)


def by_core(core, mine, other, axis):
    return jnp.where(
        core == 0,
        jnp.concatenate([mine, other], axis=axis),
        jnp.concatenate([other, mine], axis=axis),
    )


def gather_tokens(v, beside=tuple):
    if not paired():
        return lax.all_gather(v, "fsdp", axis=0, tiled=True), beside()
    r = v.shape[0] // 2
    a, b = v[:r], v[r:]
    a1, b1 = swap(a, 2), swap(b, 4)
    a2 = swap(jnp.concatenate([a, a1], axis=0), 4)
    b2 = swap(jnp.concatenate([b, b1], axis=0), 2)
    held = beside()
    if held:
        a2, b2, *held = hold(a2, b2, *held)
    near = jnp.concatenate([v, a1, b2[:r], a2[:r], b1, a2[r:], b2[r:]], axis=0)
    return jnp.concatenate([near, swap(near, 1)], axis=0), held


def scatter_tokens(near, far):
    if not paired():
        v = jnp.concatenate([near, far], axis=0)
        return lax.psum_scatter(v, "fsdp", scatter_dimension=0, tiled=True).astype(F32)
    r = near.shape[0] // 4
    got = swap(far, 1)
    pair = lambda q: near[q * r : (q + 1) * r].astype(F32) + got[q * r : (q + 1) * r].astype(F32)
    far = [swap(pair(q).astype(BF), 2 * q) for q in (1, 2, 3)]
    return pair(0) + (far[0].astype(F32) + far[1].astype(F32)) + far[2].astype(F32)


def home_features(v):
    if not paired():
        return lax.all_to_all(v, "fsdp", split_axis=0, concat_axis=1, tiled=True)
    chip, core = place()
    r, c = v.shape[0] // 8, v.shape[1]
    both = by_core(core, v[: 4 * r], swap(v[4 * r :], 1), 1)
    out = jnp.zeros((r, 8 * c), v.dtype)
    for q in range(4):
        piece = both[q * r : (q + 1) * r]
        piece = piece if q == 0 else swap(piece, 2 * q)
        out = lax.dynamic_update_slice_in_dim(out, piece, (chip ^ q) * (2 * c), 1)
    return out


ORDER = (0, 2, 4, 6, 1, 3, 5, 7)


def line_up_kernel(order, near, far, out):
    rows = near.shape[1] // 8
    for i, m in enumerate(ORDER):

        @pl.when(pl.program_id(0) == i)
        def _():
            source = near if i < 4 else far
            for q, own in enumerate(ORDER):
                p = ORDER.index(m ^ own)
                out[q * rows : (q + 1) * rows, :] = source[0, p * rows : (p + 1) * rows, :]


def gather_features_of_tokens(v, beside):
    first, second = beside
    if not paired():
        return lax.all_gather(v, "fsdp", axis=1, tiled=True), second(*first())
    g, c = v.shape
    r = g // 2
    a, b = v[:r], v[r:]
    a1, b1 = swap(a, 2), swap(b, 4)
    a1, b1, *held = hold(a1, b1, *first())
    a2 = swap(jnp.concatenate([a, a1], axis=0), 4)
    b2 = swap(jnp.concatenate([b, b1], axis=0), 2)
    a2, b2, *held = hold(a2, b2, *second(*held))
    near = jnp.concatenate([v, a1, b2[:r], a2[:r], b1, a2[r:], b2[r:]], axis=0).reshape(4, g, c)
    far = swap(near, 1)
    lined = pl.pallas_call(
        line_up_kernel,
        grid_spec=pltpu.PrefetchScalarGridSpec(
            num_scalar_prefetch=1,
            grid=(8,),
            in_specs=[
                pl.BlockSpec((1, g, c), lambda i, o: (jnp.minimum(i, 3), 0, 0)),
                pl.BlockSpec((1, g, c), lambda i, o: (jnp.maximum(i - 4, 0), 0, 0)),
            ],
            out_specs=pl.BlockSpec((g, c), lambda i, o: (0, o[i])),
        ),
        out_shape=jax.ShapeDtypeStruct((g, 8 * c), v.dtype),
        compiler_params=pltpu.CompilerParams(vmem_limit_bytes=32 * MIB),
        cost_estimate=SHORT,
        name="line_up",
    )(orders(), near, far)
    return lined, held


def spread_features(v):
    if not paired():
        return lax.all_to_all(v, "fsdp", split_axis=1, concat_axis=0, tiled=True)
    chip, core = place()
    c = v.shape[1] // 8
    near = []
    for q in range(4):
        piece = lax.dynamic_slice_in_dim(v, (chip ^ q) * (2 * c), 2 * c, 1)
        near.append(piece if q == 0 else swap(piece, 2 * q))
    near = jnp.concatenate(near, axis=0)
    cut = lambda which: lax.dynamic_slice_in_dim(near, which * c, c, 1)
    return jnp.concatenate([cut(core), swap(cut(1 - core), 1)], axis=0)


def orders():
    me = lax.axis_index("fsdp")
    if not paired():
        return jnp.arange(lax.axis_size("fsdp"), dtype=jnp.int32)
    return jnp.stack([me ^ m for m in ORDER]).astype(jnp.int32)


def pack_kernel(count, order, *refs):
    parts, (near, far) = refs[:count], refs[count:]
    for half, out in enumerate((near, far)):

        @pl.when(pl.program_id(0) // 4 == half)
        def _():
            at = 0
            for p in parts:
                out[0, :, at : at + p.shape[1]] = p[...]
                at += p.shape[1]


def unpack_kernel(widths, order, *refs):
    pieces, outs = refs[:8], refs[8:]
    for m, piece in enumerate(pieces):

        @pl.when(pl.program_id(0) == m)
        def _():
            at = 0
            for w, out in zip(widths, outs):
                out[...] = piece[0, :, at : at + w]
                at += w


class Exchange:
    def __init__(self, parts, side):
        self.side = side
        self.parts = parts
        if not paired():
            return
        if side == 1:
            r, self.widths = parts[0].shape[0], [p.shape[1] // 8 for p in parts]
            at = lambda m, o: (0, o[m])
        else:
            r, self.widths = parts[0].shape[0] // 8, [p.shape[1] for p in parts]
            at = lambda m, o: (o[m], 0)
        total = sum(self.widths)
        out = jax.ShapeDtypeStruct((4, r, total), parts[0].dtype)
        self.near, self.far = pl.pallas_call(
            functools.partial(pack_kernel, len(parts)),
            grid_spec=pltpu.PrefetchScalarGridSpec(
                num_scalar_prefetch=1,
                grid=(8,),
                in_specs=[pl.BlockSpec((r, w), at) for w in self.widths],
                out_specs=[
                    pl.BlockSpec((1, r, total), lambda m, o: (jnp.minimum(m, 3), 0, 0)),
                    pl.BlockSpec((1, r, total), lambda m, o: (jnp.maximum(m - 4, 0), 0, 0)),
                ],
            ),
            out_shape=[out, out],
            compiler_params=pltpu.CompilerParams(vmem_limit_bytes=32 * MIB),
            name="pack",
        )(orders(), *parts)

    def across_cores(self):
        if paired():
            self.far = swap(self.far, 1)

    def after(self, *values):
        if not paired():
            return values
        *values, self.near, self.far = hold(*values, self.near, self.far)
        return values

    def across_chips(self):
        if paired():
            self.got = [
                swap(jnp.concatenate([self.near[q : q + 1], self.far[q : q + 1]], axis=0), 2 * q)
                for q in (1, 2, 3)
            ]

    def moving(self):
        return self.got if paired() else []

    def waiting(self):
        return [self.near, self.far] if paired() else []

    def resume(self, held):
        if not paired():
            return held
        if hasattr(self, "got"):
            self.got, held = list(held[:3]), held[3:]
        else:
            (self.near, self.far), held = held[:2], held[2:]
        return held

    def arrived(self, *values, count=3):
        if not paired():
            return values
        held = hold(*values, *self.got[:count])
        self.got[:count] = held[len(values) :]
        return held[: len(values)]

    def results(self):
        if not paired():
            split, concat = (1, 0) if self.side == 1 else (0, 1)
            return [
                lax.all_to_all(p, "fsdp", split_axis=split, concat_axis=concat, tiled=True)
                for p in self.parts
            ]
        _, r, total = self.near.shape
        block = lambda i: pl.BlockSpec((1, r, total), lambda m, o: (i, 0, 0))
        if self.side == 1:
            at = lambda m, o: (o[m], 0)
            shape = lambda w: (8 * r, w)
        else:
            at = lambda m, o: (0, o[m])
            shape = lambda w: (r, 8 * w)
        return pl.pallas_call(
            functools.partial(unpack_kernel, self.widths),
            grid_spec=pltpu.PrefetchScalarGridSpec(
                num_scalar_prefetch=1,
                grid=(8,),
                in_specs=[block(0)] * 4 + [block(0)] + [block(1)] * 3,
                out_specs=[pl.BlockSpec((r, w), at) for w in self.widths],
            ),
            out_shape=[jax.ShapeDtypeStruct(shape(w), self.near.dtype) for w in self.widths],
            compiler_params=pltpu.CompilerParams(vmem_limit_bytes=32 * MIB),
            name="unpack",
        )(orders(), self.near, *self.got, self.far, *self.got)


def rep_scatter(v):
    return lax.psum_scatter(v, "rep", scatter_dimension=0, tiled=True)


def rep_gather(v):
    return lax.all_gather(v, "rep", axis=0, tiled=True)


def share_kernel(blocks, shares, rows_at_end, *refs):
    *parts, out = refs
    rows = out.shape[2]

    def put(some):
        at = 0
        for p in some:
            w = p.shape[1]
            for i in range(shares):
                out[i, 0, :, at : at + w] = p[i * rows : (i + 1) * rows, :]
            at += w

    if not rows_at_end:
        put(parts)
        return

    @pl.when(pl.program_id(0) < blocks)
    def _():
        put(parts[:-1])

    @pl.when(pl.program_id(0) >= blocks)
    def _():
        put(parts[-1:])


def rep_scatter_cols(parts, last=None):
    n, z = lax.axis_size("fsdp"), lax.axis_size("rep")
    rows, c = parts[0].shape[0], sum(p.shape[1] for p in parts)
    share = rows // (n * z)
    extra = 0 if last is None else last.shape[1] // c
    specs = [
        pl.BlockSpec((rows // n, p.shape[1]), lambda i: (jnp.minimum(i, n - 1), 0)) for p in parts
    ]
    if extra:
        specs.append(pl.BlockSpec((rows // n, c), lambda i: (0, jnp.maximum(i - n, 0))))
        parts = [*parts, last]
    v = pl.pallas_call(
        functools.partial(share_kernel, n, z, extra > 0),
        grid=(n + extra,),
        in_specs=specs,
        out_specs=pl.BlockSpec((z, 1, share, c), lambda i: (0, i, 0, 0)),
        out_shape=jax.ShapeDtypeStruct((z, n + extra, share, c), parts[0].dtype),
        compiler_params=pltpu.CompilerParams(vmem_limit_bytes=32 * MIB),
        cost_estimate=SHORT,
        name="shares",
    )(*parts)
    v = rep_scatter(v.reshape(z * (n + extra) * share, c))
    if last is None:
        return v
    tail = v[n * share :].reshape(extra, share, c).transpose(1, 0, 2).reshape(share, extra * c)
    return v[: n * share], tail


def widen_kernel(*refs):
    joined, *outs = refs
    at = 0
    for out in outs:
        w = out.shape[1]
        out[...] = joined[:, at : at + w].astype(F32)
        at += w


def widened(v, widths):
    r = v.shape[0]
    rows = min(r, 32)
    return pl.pallas_call(
        widen_kernel,
        grid=(r // rows,),
        in_specs=[pl.BlockSpec((rows, v.shape[1]), lambda i: (i, 0))],
        out_specs=[pl.BlockSpec((rows, w), lambda i: (i, 0)) for w in widths],
        out_shape=[jax.ShapeDtypeStruct((r, w), F32) for w in widths],
        compiler_params=pltpu.CompilerParams(vmem_limit_bytes=32 * MIB),
        cost_estimate=SHORT,
        name="widened",
    )(v)


def rep_sum(v):
    n = lax.axis_size("rep")
    total = v.astype(F32)
    for s in range(1, n):
        total = total + lax.ppermute(v, "rep", [(i, (i + s) % n) for i in range(n)]).astype(F32)
    return total


def scatter_features(v):
    if not paired():
        return lax.psum_scatter(v, "fsdp", scatter_dimension=1, tiled=True).astype(F32)
    chip, core = place()
    r = v.shape[0]
    v = v.reshape(r, 4, 2, -1)
    cut = lambda which: lax.dynamic_index_in_dim(v, which, 2, keepdims=False).transpose(1, 0, 2)
    pair = cut(core).astype(F32) + swap(cut(1 - core), 1).astype(F32)
    low = pair.astype(BF)
    total = lax.dynamic_index_in_dim(pair, chip, 0, keepdims=False)
    for q in (1, 2, 3):
        got = swap(lax.dynamic_index_in_dim(low, chip ^ q, 0, keepdims=False), 2 * q)
        total = total + got.astype(F32)
    return total


def gather_features(v):
    if not paired():
        return lax.all_gather(v, "fsdp", axis=1, tiled=True)
    chip, core = place()
    r, c = v.shape
    both = by_core(core, v, swap(v, 1), 1)
    out = jnp.zeros((r, 8 * c), v.dtype)
    for q in range(4):
        got = both if q == 0 else swap(both, 2 * q)
        out = lax.dynamic_update_slice_in_dim(out, got, (chip ^ q) * (2 * c), 1)
    return out


def whole_block(a):
    return pl.BlockSpec(a.shape, lambda *_: (0,) * a.ndim, pipeline_mode=pl.Buffered(1))


def shifted(v):
    first = lax.broadcasted_iota(jnp.int32, v.shape, 0) == 0
    return jnp.where(first, 0.0, pltpu.roll(v, 1, 0))


def shifted_back(v):
    last = lax.broadcasted_iota(jnp.int32, v.shape, 0) == v.shape[0] - 1
    return jnp.where(last, 0.0, pltpu.roll(v, v.shape[0] - 1, 0))


def normal_rows(v):
    center = v - jnp.mean(v, axis=-1, keepdims=True)
    spread = jnp.mean(center * center, axis=-1, keepdims=True)
    return center * lax.rsqrt(spread + norm_eps)


def front_kernel(
    ranks, order, tok, gain, shift, lerp, narrow, widen, fnarrow, xk, xv, xr, xg, hid, low, nh, nl, wb, fh, fl
):
    @pl.when(pl.program_id(0) == 0)
    def _():
        nh[...], nl[...] = halves(jnp.transpose(narrow[...]))
        fh[...], fl[...] = halves(jnp.transpose(fnarrow[...]))
        wb[...] = widen[...].astype(BF)

    normed = normal_rows(tok[...].astype(F32)) * gain[...] + shift[...]
    delta = shifted(normed) - normed
    bh, bl = halves(normed + delta * lerp[0:1, :])
    hidden = jnp.tanh(mm(bh, nh[...]) + mm(bh, nl[...]) + mm(bl, nh[...]))
    hid[...] = hidden
    hb = hidden.astype(BF)
    for f, out in ((1, xk), (2, xv), (3, xr), (4, xg), (0, None)):
        rows = slice(f * ranks, (f + 1) * ranks)
        x = normed + delta * (lerp[f + 1 : f + 2, :] + mm(hb[:, rows], wb[rows, :]))
        if out is not None:
            out[...] = x.astype(BF)
        else:
            dh, dl = halves(x)
            low[...] = jnp.tanh(mm(dh, fh[...]) + mm(dh, fl[...]) + mm(dl, fh[...]))


def ordered_rows(seq_len, d, seqs):
    return pl.BlockSpec((seq_len, d), lambda s, o: (o[s // seqs] * seqs + lax.rem(s, seqs), 0))


def front(seq_len, tokens, gain, shift, lerp, narrow, widen, fnarrow):
    g, d = tokens.shape
    ranks = widen.shape[0] // 5
    fd = fnarrow.shape[0]
    order = orders()
    per_seq = lambda w: pl.BlockSpec((seq_len, w), lambda s, o: (s, 0))
    return pl.pallas_call(
        functools.partial(front_kernel, ranks),
        grid_spec=pltpu.PrefetchScalarGridSpec(
            num_scalar_prefetch=1,
            grid=(g // seq_len,),
            in_specs=[ordered_rows(seq_len, d, g // seq_len // order.shape[0])]
            + [whole_block(a) for a in (gain, shift, lerp, narrow, widen, fnarrow)],
            out_specs=[per_seq(d)] * 4 + [per_seq(5 * ranks), per_seq(fd)],
            scratch_shapes=[
                pltpu.VMEM((d, 5 * ranks), BF),
                pltpu.VMEM((d, 5 * ranks), BF),
                pltpu.VMEM((5 * ranks, d), BF),
                pltpu.VMEM((d, fd), BF),
                pltpu.VMEM((d, fd), BF),
            ],
        ),
        out_shape=[jax.ShapeDtypeStruct((g, d), BF)] * 4
        + [
            jax.ShapeDtypeStruct((g, 5 * ranks), F32),
            jax.ShapeDtypeStruct((g, fd), F32),
        ],
        compiler_params=pltpu.CompilerParams(vmem_limit_bytes=48 * MIB),
        cost_estimate=SHORT,
        name="token_shift",
    )(order, tokens, gain, shift, lerp, narrow, widen, fnarrow)


def back_kernel(
    ranks,
    order,
    tok,
    hid,
    low,
    dk,
    dv,
    dr,
    dg,
    draw,
    gain,
    shift,
    lerp,
    narrow,
    widen,
    fnarrow,
    fwiden,
    wk,
    wv,
    wr,
    wg,
    dn_out,
    vec_out,
    dwid_out,
    dnar_out,
    dfn_out,
    narrow_low,
    widen_low,
    fnarrow_low,
    fwiden_low,
):
    @pl.when(pl.program_id(0) == 0)
    def _():
        narrow_low[...] = narrow[...].astype(BF)
        widen_low[...] = widen[...].astype(BF)
        fnarrow_low[...] = fnarrow[...].astype(BF)
        fwiden_low[...] = fwiden[...].astype(BF)
        for ref in (vec_out, dwid_out, dnar_out, dfn_out):
            ref[...] = jnp.zeros_like(ref)

    unit = normal_rows(tok[...].astype(F32))
    normed = unit * gain[...] + shift[...]
    delta = shifted(normed) - normed
    hidden = hid[...]
    hb = hidden.astype(BF)
    lowv = low[...]
    colsum = lambda v: jnp.sum(v, axis=0, keepdims=True)
    dlow = mm_nt(draw[...].astype(BF), fwiden_low[...]) * (1.0 - lowv * lowv)
    dlow = dlow.astype(BF)
    total = jnp.zeros(normed.shape, F32)
    moved = jnp.zeros(normed.shape, F32)
    dhid = []
    for f, d_ref, w_ref in (
        (0, None, None),
        (1, dk, wk),
        (2, dv, wv),
        (3, dr, wr),
        (4, dg, wg),
    ):
        rows = slice(f * ranks, (f + 1) * ranks)
        mu = lerp[f + 1 : f + 2, :] + mm(hb[:, rows], widen_low[rows, :])
        if f == 0:
            dx = mm(dlow, fnarrow_low[...])
            dfn_out[...] += mm_tn(dlow, (normed + delta * mu).astype(BF))
        else:
            dx = mm_nt(d_ref[...], w_ref[...])
        total = total + dx
        moved = moved + dx * mu
        doff = dx * delta
        vec_out[f + 1 : f + 2, :] += colsum(doff)
        db = doff.astype(BF)
        dwid_out[rows, :] += mm_tn(hb[:, rows], db)
        dhid.append(mm_nt(db, widen_low[rows, :]))
    dpre = (jnp.concatenate(dhid, axis=1) * (1.0 - hidden * hidden)).astype(BF)
    dblend = mm(dpre, narrow_low[...])
    base = lerp[0:1, :]
    dnar_out[...] += mm_tn(dpre, (normed + delta * base).astype(BF))
    vec_out[0:1, :] += colsum(dblend * delta)
    total = total + dblend
    moved = moved + dblend * base
    dn = total - moved + shifted_back(moved)
    vec_out[6:7, :] += colsum(dn * unit)
    vec_out[7:8, :] += colsum(dn)
    dn_out[...] = dn.astype(BF)


def back(seq_len, tokens, hid, low, grads, draw, params, weights):
    g, d = tokens.shape
    c = draw.shape[1]
    gain, shift, lerp, narrow, widen, fnarrow, fwiden = params
    ranks = widen.shape[0] // 5
    fd = low.shape[1]
    order = orders()
    per_seq = lambda w: pl.BlockSpec((seq_len, w), lambda s, o: (s, 0))
    kept = lambda r: pl.BlockSpec((r, d), lambda s, o: (0, 0))
    return pl.pallas_call(
        functools.partial(back_kernel, ranks),
        grid_spec=pltpu.PrefetchScalarGridSpec(
            num_scalar_prefetch=1,
            grid=(g // seq_len,),
            in_specs=[
                ordered_rows(seq_len, d, g // seq_len // order.shape[0]),
                per_seq(5 * ranks),
                per_seq(fd),
            ]
            + [per_seq(c)] * 5
            + [whole_block(a) for a in params]
            + [whole_block(a) for a in weights],
            out_specs=[per_seq(d), kept(8), kept(5 * ranks), kept(5 * ranks), kept(fd)],
            scratch_shapes=[
                pltpu.VMEM((5 * ranks, d), BF),
                pltpu.VMEM((5 * ranks, d), BF),
                pltpu.VMEM((fd, d), BF),
                pltpu.VMEM((fd, c), BF),
            ],
        ),
        out_shape=[
            jax.ShapeDtypeStruct((g, d), BF),
            jax.ShapeDtypeStruct((8, d), F32),
            jax.ShapeDtypeStruct((5 * ranks, d), F32),
            jax.ShapeDtypeStruct((5 * ranks, d), F32),
            jax.ShapeDtypeStruct((fd, d), F32),
        ],
        compiler_params=pltpu.CompilerParams(vmem_limit_bytes=56 * MIB),
        cost_estimate=SHORT,
        name="token_shift_back",
    )(order, tokens, hid, low, *grads, draw, *params, *weights)


def level_tables(length):
    p = np.arange(length)[:, None]
    u = np.arange(length)[None, :]
    levels = int(length).bit_length() - 1
    spans = []
    for l in range(1, levels):
        b = 1 << l
        same = (p // b) == (u // b)
        upper = (p // b) % 2 == 1
        spans.append(same & np.where(upper, u < p, u > p))
    spans = np.concatenate(spans, 0).astype(np.float32)
    diff = p ^ u
    level = np.where(u < p, np.floor(np.log2(np.maximum(diff, 1))), -1)
    return levels, spans, level.astype(np.int32)


def per_head(lanes, width, count, v):
    out = jnp.sum(jnp.where(lanes == 0, v, 0.0), axis=1, keepdims=True)
    if count == 1:
        return jnp.broadcast_to(out, v.shape)
    for h in range(1, count):
        one = jnp.sum(jnp.where(lanes == h, v, 0.0), axis=1, keepdims=True)
        out = jnp.where(lanes == h, one, out)
    return out


def stack_heads(lanes, count, v):
    zero = jnp.zeros_like(v)
    return jnp.concatenate([jnp.where(lanes == h, v, zero) for h in range(count)], axis=0)


def side_by_side(length, count, v):
    return jnp.concatenate([v[h * length : (h + 1) * length] for h in range(count)], axis=1)


def mix_forward(levels, count, width, r, k, v, w, u, spans, level):
    length, lanes_n = r.shape
    lanes = lax.broadcasted_iota(jnp.int32, (length, lanes_n), 1) // width
    wh, wl = halves(w)
    gaps = mm(spans, wh) + mm(spans, wl)
    factors = [None] + [
        jnp.exp(gaps[l * length : (l + 1) * length]) for l in range(levels - 1)
    ]
    level2 = jnp.concatenate([level] * count, axis=0)
    scores = jnp.zeros((length * count, length), F32)
    parts = []
    for l in range(levels):
        e = factors[l]
        re = (r if e is None else r * e).astype(BF)
        ke = (k if e is None else k * e).astype(BF)
        parts.append((e, re, ke))
        scores = scores + jnp.where(
            level2 == l, mm_nt(stack_heads(lanes, count, re), ke), 0.0
        )
    vb = v.astype(BF)
    bonus = per_head(lanes, width, count, r * u * k)
    wkv = (
        mm(side_by_side(length, count, scores).astype(BF), stack_heads(lanes, count, vb))
        + bonus * v
    )
    center = wkv - per_head(lanes, width, count, wkv) * (1.0 / width)
    spread = per_head(lanes, width, count, center * center) * (1.0 / width)
    rstd = lax.rsqrt(spread + group_eps)
    return lanes, level2, parts, scores, bonus, vb, center * rstd, rstd


def mix_kernel(levels, count, width, *refs):
    xk, xv, xr, xg, low, wk, wv, wr, wg, we, base, fwiden, u, gain, bias, spans, level = refs[:17]
    k_out, v_out, r_out, g_out, w_out, mixed_out, near_out, far_out = refs[17:]
    for x, weights, out in ((xk, wk, k_out), (xv, wv, v_out), (xr, wr, r_out), (xg, wg, g_out)):
        out[...] = mm(x[...], weights[...])
    lh, ll = halves(low[...])
    fh, fl = halves(fwiden[...])
    w_out[...] = -jnp.exp(base[...] + (mm(lh, fh) + mm(lh, fl) + mm(ll, fh)))
    lanes = count * width
    for p in range(u.shape[1] // lanes):
        at = slice(p * lanes, (p + 1) * lanes)
        unit = mix_forward(
            levels,
            count,
            width,
            r_out[:, at],
            k_out[:, at],
            v_out[:, at],
            w_out[:, at],
            u[:, at],
            spans[...],
            level[...],
        )[6]
        gate = g_out[:, at]
        mixed_out[:, at] = (
            (unit * gain[:, at] + bias[:, at]) * (gate * jax.nn.sigmoid(gate))
        ).astype(BF)
    product = mm(mixed_out[...], we[...]).astype(BF)
    step, steps = pl.program_id(0), pl.num_programs(0)

    @pl.when(step < steps // 2)
    def _():
        near_out[...] = product

    @pl.when(step >= steps // 2)
    def _():
        far_out[...] = product


def mix(seq_len, xs, low, weights, we, vectors, fwiden):
    rows, d = xs[0].shape
    c = we.shape[0]
    half = rows // 2
    heads_here = c * HEADS // d
    width = c // heads_here
    count = 2 if heads_here % 2 == 0 else 1
    levels, spans, level = level_tables(seq_len)
    spans_a, level_a = jnp.asarray(spans, BF), jnp.asarray(level)
    steps = half // seq_len
    block = lambda w: pl.BlockSpec((seq_len, w), lambda s: (s, 0))
    base, u, gain, bias = vectors
    kept = (*weights, we, base, fwiden, u, gain, bias, spans_a, level_a)
    shape = lambda w, t: jax.ShapeDtypeStruct((rows, w), t)
    return pl.pallas_call(
        functools.partial(mix_kernel, levels, count, width),
        grid=(2 * steps,),
        in_specs=[block(d)] * 4 + [block(low.shape[1])] + [whole_block(t) for t in kept],
        out_specs=[block(c)] * 6
        + [
            pl.BlockSpec((seq_len, d), lambda s: (jnp.minimum(s, steps - 1), 0)),
            pl.BlockSpec((seq_len, d), lambda s: (jnp.maximum(s - steps, 0), 0)),
        ],
        out_shape=[shape(c, F32)] * 5
        + [shape(c, BF)]
        + [jax.ShapeDtypeStruct((half, d), BF)] * 2,
        compiler_params=pltpu.CompilerParams(vmem_limit_bytes=48 * MIB),
        cost_estimate=lasts(20),
        name="decay_mix",
    )(*xs, low, *kept)


def wkv_back_kernel(
    levels,
    count,
    width,
    r_ref,
    k_ref,
    v_ref,
    g_ref,
    w_ref,
    dm_ref,
    u_ref,
    gain_ref,
    bias_ref,
    spans,
    spans_t,
    level_ref,
    dr_out,
    dk_out,
    dv_out,
    dg_out,
    draw_out,
    vec_out,
):
    @pl.when(pl.program_id(1) == 0)
    def _():
        vec_out[...] = jnp.zeros_like(vec_out)

    r, k, v, w, u = r_ref[...], k_ref[...], v_ref[...], w_ref[...], u_ref[...]
    level = level_ref[...]
    lanes, level2, parts, scores, bonus, vb, unit, rstd = mix_forward(
        levels, count, width, r, k, v, w, u, spans[...], level
    )
    length = r.shape[0]
    heads = functools.partial(per_head, lanes, width, count)
    stack = functools.partial(stack_heads, lanes, count)
    beside = functools.partial(side_by_side, length, count)
    colsum = lambda x: jnp.sum(x, axis=0, keepdims=True)

    gate, dm, gain = g_ref[...], dm_ref[...], gain_ref[...]
    sig = jax.nn.sigmoid(gate)
    scaled = unit * gain + bias_ref[...]
    dg_out[...] = (dm * scaled * sig * (1.0 + gate * (1.0 - sig))).astype(BF)
    dscaled = dm * gate * sig
    dunit = dscaled * gain
    dwkv = rstd * (
        dunit - heads(dunit) * (1.0 / width) - unit * (heads(dunit * unit) * (1.0 / width))
    )
    db = dwkv.astype(BF)
    dbs = stack(db)
    dscores = mm_nt(dbs, vb)

    def turned(x):
        return jnp.concatenate(
            [jnp.transpose(x[h * length : (h + 1) * length]) for h in range(count)], axis=0
        )

    dscores_t = turned(dscores)
    level_t = jnp.transpose(level)
    level2_t = jnp.concatenate([level_t] * count, axis=0)
    dv = mm(beside(turned(scores)).astype(BF), dbs) + bonus * dwkv
    dbonus = heads(dwkv * v)
    dr = dbonus * u * k
    dk = dbonus * u * r
    flows = []
    for l in range(levels):
        e, re, ke = parts[l]
        dre = mm(beside(jnp.where(level2 == l, dscores, 0.0)).astype(BF), stack(ke))
        dke = mm(beside(jnp.where(level2_t == l, dscores_t, 0.0)).astype(BF), stack(re))
        if e is None:
            dr = dr + dre
            dk = dk + dke
        else:
            dre = dre * e
            dke = dke * e
            dr = dr + dre
            dk = dk + dke
            flows.append(dre * r + dke * k)
    fh, fl = halves(jnp.concatenate(flows, axis=0))
    dw = mm(spans_t[...], fh) + mm(spans_t[...], fl)
    draw = dw * w
    dr_out[...] = dr.astype(BF)
    dk_out[...] = dk.astype(BF)
    dv_out[...] = dv.astype(BF)
    draw_out[...] = draw
    vec_out[0:1, :] += colsum(dbonus * r * k)
    vec_out[1:2, :] += colsum(dscaled * unit)
    vec_out[2:3, :] += colsum(dscaled)
    vec_out[3:4, :] += colsum(draw)


def mix_back(seq_len, r, k, v, g, w, u, gain, bias, dmixed):
    rows, c = r.shape
    heads_here = HEADS // lax.axis_size("fsdp")
    width = c // heads_here
    count = 2 if heads_here % 2 == 0 else 1
    lanes = count * width
    levels, spans, level = level_tables(seq_len)
    spans_a = jnp.asarray(spans, BF)
    level_a = jnp.asarray(level)
    cols = pl.BlockSpec((seq_len, lanes), lambda p, s: (s, p))
    vec = pl.BlockSpec((1, lanes), lambda p, s: (0, p))
    grid = (c // lanes, rows // seq_len)
    params = pltpu.CompilerParams(vmem_limit_bytes=40 * MIB)
    spans_t = jnp.asarray(
        np.concatenate([s.T for s in spans.reshape(levels - 1, seq_len, seq_len)], 1), BF
    )
    return pl.pallas_call(
        functools.partial(wkv_back_kernel, levels, count, width),
        grid=grid,
        in_specs=[cols] * 6
        + [vec] * 3
        + [whole_block(spans_a), whole_block(spans_t), whole_block(level_a)],
        out_specs=[cols] * 5 + [pl.BlockSpec((4, lanes), lambda p, s: (0, p))],
        out_shape=[jax.ShapeDtypeStruct((rows, c), BF)] * 4
        + [jax.ShapeDtypeStruct((rows, c), F32), jax.ShapeDtypeStruct((4, c), F32)],
        compiler_params=params,
        cost_estimate=SHORT,
        name="decay_mix_back",
    )(r, k, v, g, w, dmixed, u, gain, bias, spans_a, spans_t, level_a)


def step_shift(length, v, back=False):
    rows = v.shape[0]
    at = lax.rem(lax.broadcasted_iota(jnp.int32, v.shape, 0), length)
    edge = at == (length - 1 if back else 0)
    return jnp.where(edge, 0.0, pltpu.roll(v, rows - 1 if back else 1, 0))


def feed_kernel(length, own_order, order, n2, lerp, wl, wc, *refs):
    kc_out, sq_out, fac_out, near_out, far_out = refs[-5:]
    n = n2[...].astype(F32)
    delta = step_shift(length, n) - n
    kc = (n + delta * lerp[0:1, :]).astype(BF)
    kc_out[...] = kc
    act = mm(kc, wl[...])
    soft = jnp.maximum(act, 0.0) + jnp.log1p(jnp.exp(-jnp.abs(act)))
    fac_out[...] = 2.0 * soft * jax.nn.sigmoid(act)
    sq = (soft * soft).astype(BF)
    sq_out[...] = sq
    some, _, c = near_out.shape
    for i in range(2 * some):
        at = pl.ds(pl.multiple_of(order[i] * c, c), c) if own_order else slice(i * c, (i + 1) * c)
        out = near_out if i < some else far_out
        out[i % some] = mm(sq, wc[:, at]).astype(BF)


def feed(length, n2, lerp, wl, wc, part, earlier=()):
    g, d = n2.shape
    f = wc.shape[0]
    n = lax.axis_size("fsdp")
    half = g // 2
    rows = 2 * length if half % (2 * length) == 0 else length
    first = part * (half // rows)
    block = lambda w: pl.BlockSpec((rows, w), lambda s, o: (first + s, 0))
    shape = lambda w, t: jax.ShapeDtypeStruct((g, w), t)
    return pl.pallas_call(
        functools.partial(feed_kernel, length, paired()),
        grid_spec=pltpu.PrefetchScalarGridSpec(
            num_scalar_prefetch=1,
            grid=(half // rows,),
            in_specs=[block(d)]
            + [whole_block(a) for a in (lerp, wl, wc)]
            + [pl.BlockSpec(memory_space=pl.ANY)] * len(earlier),
            out_specs=[block(d), block(f), block(f)]
            + [pl.BlockSpec((n // 2, rows, d // n), lambda s, o: (0, s, 0))] * 2,
        ),
        out_shape=[shape(d, BF), shape(f, BF), shape(f, F32)]
        + [jax.ShapeDtypeStruct((n // 2, half, d // n), BF)] * 2,
        input_output_aliases={5 + i: i for i in range(len(earlier))},
        compiler_params=pltpu.CompilerParams(vmem_limit_bytes=52 * MIB),
        cost_estimate=lasts(8),
        name="feed",
    )(orders(), n2, lerp, wl, wc, *earlier)


def pair_kernel(near0, near1, got0, got1, *outs):
    half = near0.shape[1]
    for q, out in enumerate(outs):

        @pl.when(pl.program_id(0) == q)
        def _():
            out[:half, :] = (near0[0].astype(F32) + got1[0].astype(F32)).astype(BF)
            out[half:, :] = (near1[0].astype(F32) + got0[0].astype(F32)).astype(BF)


def gated_kernel(paired_order, adj, gate, *refs):
    *parts, gated_out, dgate_out = refs
    rows = adj.shape[0] // (8 if paired_order else 1)
    for i, own in enumerate(ORDER if paired_order else (0,)):
        at = slice(i * rows, (i + 1) * rows)
        value = parts[0][at, :].astype(F32)
        for q, part in enumerate(parts[1:]):
            p = ORDER.index((2 * q + 2) ^ own)
            value = value + part[p * rows : (p + 1) * rows, :].astype(F32)
        g = gate[at, :].astype(F32)
        gated = g * value
        gated_out[at, :] = gated.astype(BF)
        dgate_out[at, :] = (adj[at, :].astype(F32) * gated * (1.0 - g)).astype(BF)


def gated_value(adj, gate, halves_of_value):
    (near0, far0), (near1, far1) = halves_of_value
    g, c = gate.shape
    if paired():
        got0, got1 = swap(far0, 1), swap(far1, 1)
        block = pl.BlockSpec((1, g // 2, c), lambda q: (q, 0, 0))
        parts = pl.pallas_call(
            pair_kernel,
            grid=(4,),
            in_specs=[block] * 4,
            out_specs=[pl.BlockSpec((g, c), lambda q: (0, 0))] * 4,
            out_shape=[jax.ShapeDtypeStruct((g, c), BF)] * 4,
            compiler_params=pltpu.CompilerParams(vmem_limit_bytes=32 * MIB),
            cost_estimate=SHORT,
            name="pairs",
        )(near0, near1, got0, got1)
        parts = [parts[0]] + [swap(parts[q], 2 * q) for q in (1, 2, 3)]
        rows = g
    else:
        sums = [
            lax.psum_scatter(
                jnp.concatenate(t, axis=0), "fsdp", scatter_dimension=0, tiled=True
            )[0]
            for t in halves_of_value
        ]
        parts = [jnp.concatenate(sums, axis=0)]
        rows = g // lax.axis_size("fsdp")
    block = pl.BlockSpec((rows, c), lambda s: (s, 0))
    return pl.pallas_call(
        functools.partial(gated_kernel, paired()),
        grid=(g // rows,),
        in_specs=[block] * (2 + len(parts)),
        out_specs=[block] * 2,
        out_shape=[jax.ShapeDtypeStruct((g, c), BF)] * 2,
        compiler_params=pltpu.CompilerParams(vmem_limit_bytes=32 * MIB),
        cost_estimate=SHORT,
        name="gated_value",
    )(adj, gate, *parts)


def gate_kernel(length, n2, adj, lerp, wa, rc_out, gate_out, dv_out):
    n = n2[...].astype(F32)
    rc = (n + (step_shift(length, n) - n) * lerp[1:2, :]).astype(BF)
    rc_out[...] = rc
    gate = jax.nn.sigmoid(mm(rc, wa[...]))
    gate_out[...] = gate.astype(BF)
    dv_out[...] = (adj[...].astype(F32) * gate).astype(BF)


def feed_gate(length, n2, adj, lerp, wa):
    g, d = n2.shape
    c = wa.shape[1]
    rows = 2 * length if g % (2 * length) == 0 else length
    block = lambda w: pl.BlockSpec((rows, w), lambda s: (s, 0))
    return pl.pallas_call(
        functools.partial(gate_kernel, length),
        grid=(g // rows,),
        in_specs=[block(d), block(c), whole_block(lerp), whole_block(wa)],
        out_specs=[block(d), block(c), block(c)],
        out_shape=[jax.ShapeDtypeStruct((g, w), BF) for w in (d, c, c)],
        compiler_params=pltpu.CompilerParams(vmem_limit_bytes=32 * MIB),
        cost_estimate=SHORT,
        name="feed_gate",
    )(n2, adj, lerp, wa)


def feed_back_kernel(length, dv, n2, fac, dgate, lerp, wl, wa, wc, dkey_out, dn_out, vec_out):
    @pl.when(pl.program_id(0) == 0)
    def _():
        vec_out[...] = jnp.zeros_like(vec_out)

    dkey = (mm_nt(dv[...], wc[...]) * fac[...]).astype(BF)
    dkey_out[...] = dkey
    n = n2[...].astype(F32)
    delta = step_shift(length, n) - n
    dk = mm_nt(dkey, wl[...])
    dr = mm_nt(dgate[...], wa[...])
    vec_out[0:1, :] += jnp.sum(dk * delta, axis=0, keepdims=True)
    vec_out[1:2, :] += jnp.sum(dr * delta, axis=0, keepdims=True)
    moved = dk * lerp[0:1, :] + dr * lerp[1:2, :]
    dn_out[...] = (dk + dr - moved + step_shift(length, moved, True)).astype(BF)


def feed_back(length, dv, n2, fac, dgate, lerp, wl, wa, wc):
    g, d = n2.shape
    f, c = wc.shape[0], dgate.shape[1]
    rows = 2 * length if g % (2 * length) == 0 else length
    block = lambda w: pl.BlockSpec((rows, w), lambda s: (s, 0))
    return pl.pallas_call(
        functools.partial(feed_back_kernel, length),
        grid=(g // rows,),
        in_specs=[block(d), block(d), block(f), block(c)]
        + [whole_block(a) for a in (lerp, wl, wa, wc)],
        out_specs=[block(f), block(d), pl.BlockSpec((2, d), lambda s: (0, 0))],
        out_shape=[
            jax.ShapeDtypeStruct((g, f), BF),
            jax.ShapeDtypeStruct((g, d), BF),
            jax.ShapeDtypeStruct((2, d), F32),
        ],
        compiler_params=pltpu.CompilerParams(vmem_limit_bytes=52 * MIB),
        cost_estimate=SHORT,
        name="feed_back",
    )(dv, n2, fac, dgate, lerp, wl, wa, wc)


def body(
    incoming_symbols,
    string_extents,
    adjoint_signal,
    first_scaling_factor,
    first_scaling_shift,
    lerp_factors,
    lerp_narrow_weights,
    lerp_widen_weights,
    fading_baseline,
    fading_narrow_weights,
    fading_widen_weights,
    present_reward,
    acceptor_weights,
    lookup_weights,
    content_weights,
    valve_weights,
    emission_weights,
    cluster_scaling_factor,
    cluster_scaling_shift,
    second_scaling_factor,
    second_scaling_shift_vec,
    feed_lerp_factors,
    feed_lookup_weights,
    feed_content_weights,
    feed_acceptor_weights,
):
    seqs, length, d = incoming_symbols.shape
    n = lax.axis_size("fsdp")
    me = lax.axis_index("fsdp")
    c = d // n
    home = seqs * length
    plane = home * n
    ranks = lerp_widen_weights.shape[1]
    fd = fading_narrow_weights.shape[1]

    tok_home = incoming_symbols.reshape(home, d)
    z = lax.axis_index("rep")
    share = c // lax.axis_size("rep")
    lookup_quarter = Exchange(
        [lax.dynamic_slice_in_dim(feed_lookup_weights, z * share, share, 0)], 1
    )
    lookup_quarter.across_cores()
    lookup_quarter.across_chips()
    tokens = lax.all_gather(tok_home, "fsdp", axis=0, tiled=True)
    mix_weights = Exchange(
        (
            lookup_weights,
            content_weights,
            acceptor_weights,
            valve_weights,
            feed_acceptor_weights,
        ),
        1,
    )
    mix_weights.across_cores()
    mix_weights.across_chips()
    positions = lax.broadcasted_iota(jnp.int32, (seqs, length), 1)
    mask = (positions < string_extents[:, None]).astype(F32).reshape(home, 1)
    adjoint = adjoint_signal.reshape(home, d) * mask.astype(BF)
    d_out = adjoint.astype(F32)

    row = lambda v: v.reshape(1, -1)
    mine = lambda v: lax.dynamic_slice_in_dim(v, me * c, c, v.ndim - 1)
    gain1, shift1 = row(first_scaling_factor), row(first_scaling_shift)
    narrow, fnarrow = lerp_narrow_weights.T, fading_narrow_weights.T
    widen = lerp_widen_weights.reshape(5 * ranks, d)
    (tokens,) = mix_weights.arrived(tokens, count=2)
    xk, xv, xr, xg, hidden, low = front(
        length, tokens, gain1, shift1, lerp_factors, narrow, widen, fnarrow
    )
    (low,) = mix_weights.arrived(*lookup_quarter.arrived(low))
    (lookup_share,) = lookup_quarter.results()
    low, lookup_share = hold(low, lookup_share)
    wl = lax.all_gather(lookup_share.reshape(n, share, -1), "rep", axis=1, tiled=True)
    wl = wl.reshape(d, -1)
    wk, wv, wr, wg, wa = mix_weights.results()
    fwiden_mine = mine(fading_widen_weights)
    base, u, gn_gain, gn_bias = (
        mine(row(t))
        for t in (
            fading_baseline,
            present_reward,
            cluster_scaling_factor,
            cluster_scaling_shift,
        )
    )
    k, v, r, g, w, mixed, near, far = mix(
        length,
        (xk, xv, xr, xg),
        low,
        (wk, wv, wr, wg),
        emission_weights,
        (base, u, gn_gain, gn_bias),
        fwiden_mine,
    )
    branch = scatter_tokens(near, far)
    branch, wl, wa = hold(branch, wl, wa)
    branch, adjoint = hold(branch, adjoint)
    adjoint_cols = spread_features(adjoint)
    residual = tok_home.astype(F32) + branch

    center = residual - jnp.mean(residual, axis=-1, keepdims=True)
    rstd2 = lax.rsqrt(jnp.mean(center * center, axis=-1, keepdims=True) + norm_eps)
    unit2 = center * rstd2
    normed2, _ = gather_tokens(
        (unit2 * second_scaling_factor + second_scaling_shift_vec).astype(BF)
    )
    fc = feed_content_weights.shape[0]
    recept_chan, gate, d_value_mine = feed_gate(
        length, normed2, adjoint_cols, feed_lerp_factors, wa
    )
    feed_part = lambda *t: feed(length, normed2, feed_lerp_factors, wl, feed_content_weights, *t)

    def second_part(*done):
        return (*feed_part(1, done[:3]), *done[3:])

    d_value, held = gather_features_of_tokens(d_value_mine, (lambda: feed_part(0), second_part))
    key_chan, squared, factor, *values = held
    d_content = mm_tn(squared, d_value).astype(BF)
    d_value, d_content, *values = hold(d_value, d_content, *values)
    content_share = lax.psum_scatter(d_content, "rep", scatter_dimension=0, tiled=True)
    gated, d_gate = gated_value(adjoint_cols, gate, (values[2:], values[:2]))

    d_key, d_normed2, feed_lerp_part = feed_back(
        length, d_value, normed2, factor, d_gate, feed_lerp_factors, wl, wa, feed_content_weights
    )
    d_normed2, content_share = hold(d_normed2, content_share)
    feed_share = rep_scatter_cols(
        (mm_tn(key_chan, d_key).astype(BF), mm_tn(recept_chan, d_gate).astype(BF))
    )
    d_normed2 = scatter_tokens(d_normed2[: plane // 2], d_normed2[plane // 2 :])
    content_sum = rep_gather(content_share)

    def norm_back(unit, rstd, e):
        return rstd * (
            e
            - jnp.mean(e, axis=-1, keepdims=True)
            - unit * jnp.mean(e * unit, axis=-1, keepdims=True)
        )

    layer_output = (residual + home_features(gated).astype(F32)) * mask
    d_residual = d_out + norm_back(unit2, rstd2, d_normed2 * second_scaling_factor)
    norm2_part = jnp.stack([jnp.sum(d_normed2 * unit2, axis=0), jnp.sum(d_normed2, axis=0)])

    d_branch, _ = gather_tokens(d_residual.astype(BF))
    d_mixed = mm_nt(d_branch, emission_weights)
    d_emission = mm_tn(mixed, d_branch).astype(BF)
    d_r, d_k, d_v, d_g, d_raw, mix_vec = mix_back(
        length, r, k, v, g, w, u, gn_gain, gn_bias, d_mixed
    )
    d_r, d_k, d_v, d_g, feed_share = hold(d_r, d_k, d_v, d_g, feed_share)
    time_share, emission_share = rep_scatter_cols(
        [mm_tn(x, t).astype(BF) for x, t in ((xk, d_k), (xv, d_v), (xr, d_r), (xg, d_g))],
        d_emission,
    )
    feed_sums = Exchange([feed_share[:, :fc], feed_share[:, fc:]], 0)
    feed_sums.across_cores()
    feed_sums.across_chips()
    d_normed, vec_part, widen_part, narrow_part, fnarrow_part = back(
        length,
        tokens,
        hidden,
        low,
        (d_k, d_v, d_r, d_g),
        d_raw,
        (gain1, shift1, lerp_factors, narrow, widen, fnarrow, fwiden_mine),
        (wk, wv, wr, wg),
    )
    d_normed, content_sum = feed_sums.arrived(*hold(d_normed, content_sum))
    feed_sum = rep_gather(jnp.concatenate(feed_sums.results(), axis=1))
    d_normed = scatter_tokens(d_normed[: plane // 2], d_normed[plane // 2 :])
    small = scatter_features(
        jnp.concatenate(
            [vec_part, widen_part, narrow_part, fnarrow_part, norm2_part, feed_lerp_part], axis=0
        ).astype(BF)
    )
    fwiden_part = mm_tn(low.astype(BF), d_raw.astype(BF))
    small = rep_sum(jnp.concatenate([small, fwiden_part, mix_vec], axis=0).astype(BF))
    small = gather_features(small.astype(BF)).astype(F32)
    small, time_share = hold(small, time_share)
    time_sums = Exchange([time_share[:, i * c : (i + 1) * c] for i in range(4)], 0)
    time_sums.across_cores()
    time_sums.across_chips()
    time_sum = rep_gather(jnp.concatenate([*time_sums.results(), emission_share], axis=1))
    (feed_content_grads,) = widened(content_sum, (d,))
    feed_lookup_grads, feed_acceptor_grads = widened(feed_sum, (n * fc, n * c))
    (
        lookup_weights_grads,
        content_weights_grads,
        acceptor_weights_grads,
        valve_weights_grads,
        emission_weights_grads,
    ) = widened(time_sum, (d,) * 5)
    tok_f = tok_home.astype(F32)
    center1 = tok_f - jnp.mean(tok_f, axis=-1, keepdims=True)
    rstd1 = lax.rsqrt(jnp.mean(center1 * center1, axis=-1, keepdims=True) + norm_eps)
    token_grad = d_residual + norm_back(center1 * rstd1, rstd1, d_normed * first_scaling_factor)
    cuts = np.cumsum([8, 5 * ranks, 5 * ranks, fd, 2, 2, fd, 4])
    vec, widen_g, narrow_g, fnarrow_g, norm2_g, feed_lerp_g, fwiden_g, mix_g = (
        small[a:b] for a, b in zip([0, *cuts[:-1]], cuts)
    )
    return (
        layer_output.reshape(seqs, length, d),
        token_grad.reshape(seqs, length, d),
        vec[6],
        vec[7],
        vec[:6],
        narrow_g.T,
        widen_g.reshape(5, ranks, d),
        mix_g[3],
        fnarrow_g.T,
        fwiden_g,
        mix_g[0],
        acceptor_weights_grads,
        lookup_weights_grads,
        content_weights_grads,
        valve_weights_grads,
        emission_weights_grads,
        mix_g[1],
        mix_g[2],
        norm2_g[0],
        norm2_g[1],
        feed_lerp_g,
        feed_lookup_grads,
        feed_content_grads,
        feed_acceptor_grads,
    )


def solution(mesh):
    seq = P(("fsdp", "rep"), None, None)
    row = P("fsdp", None)
    in_specs = (
        (seq, P(("fsdp", "rep")), seq) + (P(),) * 9 + (row,) * 5 + (P(),) * 5 + (row,) * 3
    )
    out_specs = (seq, seq) + (P(),) * 9 + (row,) * 5 + (P(),) * 5 + (row,) * 3
    return jax.shard_map(body, mesh=mesh, in_specs=in_specs, out_specs=out_specs, check_vma=False)
```

```python
import functools

import jax
import jax.numpy as jnp
import numpy as np
from jax import lax
from jax.experimental import pallas as pl
from jax.experimental.pallas import tpu as pltpu
from jax.sharding import PartitionSpec as P

HEADS = 32
norm_eps = 1e-05
group_eps = 1.0
BF = jnp.bfloat16
F32 = jnp.float32
MIB = 1 << 20
SHORT = pl.CostEstimate(flops=1, bytes_accessed=1, transcendentals=0)


def lasts(us):
    return pl.CostEstimate(flops=int(us * 1e9), bytes_accessed=1, transcendentals=0)


def mm(a, b):
    return jnp.dot(a, b, preferred_element_type=F32)


def mm_nt(a, b):
    return lax.dot_general(a, b, (((1,), (1,)), ((), ())), preferred_element_type=F32)


def mm_tn(a, b):
    return lax.dot_general(a, b, (((0,), (0,)), ((), ())), preferred_element_type=F32)


def halves(v):
    high = v.astype(BF)
    return high, (v - high.astype(F32)).astype(BF)


def hold(*values):
    return lax.optimization_barrier(values)


def paired():
    return lax.axis_size("fsdp") == 8


def swap(v, m):
    return lax.ppermute(v, "fsdp", [(i, i ^ m) for i in range(8)])


def place():
    me = lax.axis_index("fsdp")
    return me // 2, lax.rem(me, 2)


def by_core(core, mine, other, axis):
    return jnp.where(
        core == 0,
        jnp.concatenate([mine, other], axis=axis),
        jnp.concatenate([other, mine], axis=axis),
    )


def gather_tokens(v, beside=tuple):
    if not paired():
        return lax.all_gather(v, "fsdp", axis=0, tiled=True), beside()
    r = v.shape[0] // 2
    a, b = v[:r], v[r:]
    a1, b1 = swap(a, 2), swap(b, 4)
    a2 = swap(jnp.concatenate([a, a1], axis=0), 4)
    b2 = swap(jnp.concatenate([b, b1], axis=0), 2)
    held = beside()
    if held:
        a2, b2, *held = hold(a2, b2, *held)
    near = jnp.concatenate([v, a1, b2[:r], a2[:r], b1, a2[r:], b2[r:]], axis=0)
    return jnp.concatenate([near, swap(near, 1)], axis=0), held


def scatter_tokens(near, far):
    if not paired():
        v = jnp.concatenate([near, far], axis=0)
        return lax.psum_scatter(v, "fsdp", scatter_dimension=0, tiled=True).astype(F32)
    r = near.shape[0] // 4
    got = swap(far, 1)
    pair = lambda q: near[q * r : (q + 1) * r].astype(F32) + got[q * r : (q + 1) * r].astype(F32)
    far = [swap(pair(q).astype(BF), 2 * q) for q in (1, 2, 3)]
    return pair(0) + (far[0].astype(F32) + far[1].astype(F32)) + far[2].astype(F32)


def home_features(v):
    if not paired():
        return lax.all_to_all(v, "fsdp", split_axis=0, concat_axis=1, tiled=True)
    chip, core = place()
    r, c = v.shape[0] // 8, v.shape[1]
    both = by_core(core, v[: 4 * r], swap(v[4 * r :], 1), 1)
    out = jnp.zeros((r, 8 * c), v.dtype)
    for q in range(4):
        piece = both[q * r : (q + 1) * r]
        piece = piece if q == 0 else swap(piece, 2 * q)
        out = lax.dynamic_update_slice_in_dim(out, piece, (chip ^ q) * (2 * c), 1)
    return out


ORDER = (0, 2, 4, 6, 1, 3, 5, 7)


def line_up_kernel(order, near, far, out):
    rows = near.shape[1] // 8
    for i, m in enumerate(ORDER):

        @pl.when(pl.program_id(0) == i)
        def _():
            source = near if i < 4 else far
            for q, own in enumerate(ORDER):
                p = ORDER.index(m ^ own)
                out[q * rows : (q + 1) * rows, :] = source[0, p * rows : (p + 1) * rows, :]


def gather_features_of_tokens(v, beside):
    first, second = beside
    if not paired():
        return lax.all_gather(v, "fsdp", axis=1, tiled=True), second(*first())
    g, c = v.shape
    r = g // 2
    a, b = v[:r], v[r:]
    a1, b1 = swap(a, 2), swap(b, 4)
    a1, b1, *held = hold(a1, b1, *first())
    a2 = swap(jnp.concatenate([a, a1], axis=0), 4)
    b2 = swap(jnp.concatenate([b, b1], axis=0), 2)
    a2, b2, *held = hold(a2, b2, *second(*held))
    near = jnp.concatenate([v, a1, b2[:r], a2[:r], b1, a2[r:], b2[r:]], axis=0).reshape(4, g, c)
    far = swap(near, 1)
    lined = pl.pallas_call(
        line_up_kernel,
        grid_spec=pltpu.PrefetchScalarGridSpec(
            num_scalar_prefetch=1,
            grid=(8,),
            in_specs=[
                pl.BlockSpec((1, g, c), lambda i, o: (jnp.minimum(i, 3), 0, 0)),
                pl.BlockSpec((1, g, c), lambda i, o: (jnp.maximum(i - 4, 0), 0, 0)),
            ],
            out_specs=pl.BlockSpec((g, c), lambda i, o: (0, o[i])),
        ),
        out_shape=jax.ShapeDtypeStruct((g, 8 * c), v.dtype),
        compiler_params=pltpu.CompilerParams(vmem_limit_bytes=32 * MIB),
        cost_estimate=SHORT,
        name="line_up",
    )(orders(), near, far)
    return lined, held


def spread_features(v):
    if not paired():
        return lax.all_to_all(v, "fsdp", split_axis=1, concat_axis=0, tiled=True)
    chip, core = place()
    c = v.shape[1] // 8
    near = []
    for q in range(4):
        piece = lax.dynamic_slice_in_dim(v, (chip ^ q) * (2 * c), 2 * c, 1)
        near.append(piece if q == 0 else swap(piece, 2 * q))
    near = jnp.concatenate(near, axis=0)
    cut = lambda which: lax.dynamic_slice_in_dim(near, which * c, c, 1)
    return jnp.concatenate([cut(core), swap(cut(1 - core), 1)], axis=0)


def orders():
    me = lax.axis_index("fsdp")
    if not paired():
        return jnp.arange(lax.axis_size("fsdp"), dtype=jnp.int32)
    return jnp.stack([me ^ m for m in ORDER]).astype(jnp.int32)


def pack_kernel(count, order, *refs):
    parts, (near, far) = refs[:count], refs[count:]
    for half, out in enumerate((near, far)):

        @pl.when(pl.program_id(0) // 4 == half)
        def _():
            at = 0
            for p in parts:
                out[0, :, at : at + p.shape[1]] = p[...]
                at += p.shape[1]


def unpack_kernel(widths, order, *refs):
    pieces, outs = refs[:8], refs[8:]
    for m, piece in enumerate(pieces):

        @pl.when(pl.program_id(0) == m)
        def _():
            at = 0
            for w, out in zip(widths, outs):
                out[...] = piece[0, :, at : at + w]
                at += w


class Exchange:
    def __init__(self, parts, side):
        self.side = side
        self.parts = parts
        if not paired():
            return
        if side == 1:
            r, self.widths = parts[0].shape[0], [p.shape[1] // 8 for p in parts]
            at = lambda m, o: (0, o[m])
        else:
            r, self.widths = parts[0].shape[0] // 8, [p.shape[1] for p in parts]
            at = lambda m, o: (o[m], 0)
        total = sum(self.widths)
        out = jax.ShapeDtypeStruct((4, r, total), parts[0].dtype)
        self.near, self.far = pl.pallas_call(
            functools.partial(pack_kernel, len(parts)),
            grid_spec=pltpu.PrefetchScalarGridSpec(
                num_scalar_prefetch=1,
                grid=(8,),
                in_specs=[pl.BlockSpec((r, w), at) for w in self.widths],
                out_specs=[
                    pl.BlockSpec((1, r, total), lambda m, o: (jnp.minimum(m, 3), 0, 0)),
                    pl.BlockSpec((1, r, total), lambda m, o: (jnp.maximum(m - 4, 0), 0, 0)),
                ],
            ),
            out_shape=[out, out],
            compiler_params=pltpu.CompilerParams(vmem_limit_bytes=32 * MIB),
            name="pack",
        )(orders(), *parts)

    def across_cores(self):
        if paired():
            self.far = swap(self.far, 1)

    def after(self, *values):
        if not paired():
            return values
        *values, self.near, self.far = hold(*values, self.near, self.far)
        return values

    def across_chips(self):
        if paired():
            self.got = [
                swap(jnp.concatenate([self.near[q : q + 1], self.far[q : q + 1]], axis=0), 2 * q)
                for q in (1, 2, 3)
            ]

    def moving(self):
        return self.got if paired() else []

    def waiting(self):
        return [self.near, self.far] if paired() else []

    def resume(self, held):
        if not paired():
            return held
        if hasattr(self, "got"):
            self.got, held = list(held[:3]), held[3:]
        else:
            (self.near, self.far), held = held[:2], held[2:]
        return held

    def arrived(self, *values, count=3):
        if not paired():
            return values
        held = hold(*values, *self.got[:count])
        self.got[:count] = held[len(values) :]
        return held[: len(values)]

    def results(self):
        if not paired():
            split, concat = (1, 0) if self.side == 1 else (0, 1)
            return [
                lax.all_to_all(p, "fsdp", split_axis=split, concat_axis=concat, tiled=True)
                for p in self.parts
            ]
        _, r, total = self.near.shape
        block = lambda i: pl.BlockSpec((1, r, total), lambda m, o: (i, 0, 0))
        if self.side == 1:
            at = lambda m, o: (o[m], 0)
            shape = lambda w: (8 * r, w)
        else:
            at = lambda m, o: (0, o[m])
            shape = lambda w: (r, 8 * w)
        return pl.pallas_call(
            functools.partial(unpack_kernel, self.widths),
            grid_spec=pltpu.PrefetchScalarGridSpec(
                num_scalar_prefetch=1,
                grid=(8,),
                in_specs=[block(0)] * 4 + [block(0)] + [block(1)] * 3,
                out_specs=[pl.BlockSpec((r, w), at) for w in self.widths],
            ),
            out_shape=[jax.ShapeDtypeStruct(shape(w), self.near.dtype) for w in self.widths],
            compiler_params=pltpu.CompilerParams(vmem_limit_bytes=32 * MIB),
            name="unpack",
        )(orders(), self.near, *self.got, self.far, *self.got)


def rep_scatter(v):
    return lax.psum_scatter(v, "rep", scatter_dimension=0, tiled=True)


def rep_gather(v):
    return lax.all_gather(v, "rep", axis=0, tiled=True)


def share_kernel(blocks, shares, rows_at_end, *refs):
    *parts, out = refs
    rows = out.shape[2]

    def put(some):
        at = 0
        for p in some:
            w = p.shape[1]
            for i in range(shares):
                out[i, 0, :, at : at + w] = p[i * rows : (i + 1) * rows, :]
            at += w

    if not rows_at_end:
        put(parts)
        return

    @pl.when(pl.program_id(0) < blocks)
    def _():
        put(parts[:-1])

    @pl.when(pl.program_id(0) >= blocks)
    def _():
        put(parts[-1:])


def rep_scatter_cols(parts, last=None):
    n, z = lax.axis_size("fsdp"), lax.axis_size("rep")
    rows, c = parts[0].shape[0], sum(p.shape[1] for p in parts)
    share = rows // (n * z)
    extra = 0 if last is None else last.shape[1] // c
    specs = [
        pl.BlockSpec((rows // n, p.shape[1]), lambda i: (jnp.minimum(i, n - 1), 0)) for p in parts
    ]
    if extra:
        specs.append(pl.BlockSpec((rows // n, c), lambda i: (0, jnp.maximum(i - n, 0))))
        parts = [*parts, last]
    v = pl.pallas_call(
        functools.partial(share_kernel, n, z, extra > 0),
        grid=(n + extra,),
        in_specs=specs,
        out_specs=pl.BlockSpec((z, 1, share, c), lambda i: (0, i, 0, 0)),
        out_shape=jax.ShapeDtypeStruct((z, n + extra, share, c), parts[0].dtype),
        compiler_params=pltpu.CompilerParams(vmem_limit_bytes=32 * MIB),
        cost_estimate=SHORT,
        name="shares",
    )(*parts)
    v = rep_scatter(v.reshape(z * (n + extra) * share, c))
    if last is None:
        return v
    tail = v[n * share :].reshape(extra, share, c).transpose(1, 0, 2).reshape(share, extra * c)
    return v[: n * share], tail


def widen_kernel(*refs):
    joined, *outs = refs
    at = 0
    for out in outs:
        w = out.shape[1]
        out[...] = joined[:, at : at + w].astype(F32)
        at += w


def widened(v, widths):
    r = v.shape[0]
    rows = min(r, 32)
    return pl.pallas_call(
        widen_kernel,
        grid=(r // rows,),
        in_specs=[pl.BlockSpec((rows, v.shape[1]), lambda i: (i, 0))],
        out_specs=[pl.BlockSpec((rows, w), lambda i: (i, 0)) for w in widths],
        out_shape=[jax.ShapeDtypeStruct((r, w), F32) for w in widths],
        compiler_params=pltpu.CompilerParams(vmem_limit_bytes=32 * MIB),
        cost_estimate=SHORT,
        name="widened",
    )(v)


def rep_sum(v):
    n = lax.axis_size("rep")
    if n & (n - 1):
        return lax.psum(v, "rep").astype(F32)
    total, step = v.astype(F32), 1
    while step < n:
        got = lax.ppermute(total.astype(v.dtype), "rep", [(i, i ^ step) for i in range(n)])
        total, step = total + got.astype(F32), step * 2
    return total


def scatter_features(v):
    if not paired():
        return lax.psum_scatter(v, "fsdp", scatter_dimension=1, tiled=True).astype(F32)
    chip, core = place()
    r = v.shape[0]
    v = v.reshape(r, 4, 2, -1)
    cut = lambda which: lax.dynamic_index_in_dim(v, which, 2, keepdims=False).transpose(1, 0, 2)
    pair = cut(core).astype(F32) + swap(cut(1 - core), 1).astype(F32)
    low = pair.astype(BF)
    total = lax.dynamic_index_in_dim(pair, chip, 0, keepdims=False)
    for q in (1, 2, 3):
        got = swap(lax.dynamic_index_in_dim(low, chip ^ q, 0, keepdims=False), 2 * q)
        total = total + got.astype(F32)
    return total


def gather_features(v):
    if not paired():
        return lax.all_gather(v, "fsdp", axis=1, tiled=True)
    chip, core = place()
    r, c = v.shape
    both = by_core(core, v, swap(v, 1), 1)
    out = jnp.zeros((r, 8 * c), v.dtype)
    for q in range(4):
        got = both if q == 0 else swap(both, 2 * q)
        out = lax.dynamic_update_slice_in_dim(out, got, (chip ^ q) * (2 * c), 1)
    return out


def whole_block(a):
    return pl.BlockSpec(a.shape, lambda *_: (0,) * a.ndim, pipeline_mode=pl.Buffered(1))


def shifted(v):
    first = lax.broadcasted_iota(jnp.int32, v.shape, 0) == 0
    return jnp.where(first, 0.0, pltpu.roll(v, 1, 0))


def shifted_back(v):
    last = lax.broadcasted_iota(jnp.int32, v.shape, 0) == v.shape[0] - 1
    return jnp.where(last, 0.0, pltpu.roll(v, v.shape[0] - 1, 0))


def normal_rows(v):
    center = v - jnp.mean(v, axis=-1, keepdims=True)
    spread = jnp.mean(center * center, axis=-1, keepdims=True)
    return center * lax.rsqrt(spread + norm_eps)


def front_kernel(ranks, length, count, order, *refs):
    tokens, (gain, shift, lerp, narrow, widen, fnarrow) = refs[:count], refs[count : count + 6]
    xk, xv, xr, xg, hid, low, nw, wb, fw = refs[count + 6 :]
    fd = low.shape[1]

    @pl.when(pl.program_id(0) == 0)
    def _():
        nw[...] = jnp.transpose(narrow[...]).astype(BF)
        wb[...] = widen[...].astype(BF)
        fw[:, :fd], fw[:, fd:] = halves(jnp.transpose(fnarrow[...]))

    tok = jnp.concatenate([t[...].astype(F32) for t in tokens], axis=0)
    normed = normal_rows(tok) * gain[...] + shift[...]
    delta = step_shift(length, normed) - normed
    hidden = jnp.tanh(mm((normed + delta * lerp[0:1, :]).astype(BF), nw[...]))
    hid[...] = hidden
    hb = hidden.astype(BF)
    for f, out in ((1, xk), (2, xv), (3, xr), (4, xg), (0, None)):
        rows = slice(f * ranks, (f + 1) * ranks)
        x = normed + delta * (lerp[f + 1 : f + 2, :] + mm(hb[:, rows], wb[rows, :]))
        if out is not None:
            out[...] = x.astype(BF)
        else:
            dh, dl = halves(x)
            pre = mm(dh, fw[...])
            low[...] = jnp.tanh(pre[:, :fd] + pre[:, fd:] + mm(dl, fw[:, :fd]))


def ordered_rows(seq_len, d, seqs):
    return pl.BlockSpec((seq_len, d), lambda s, o: (o[s // seqs] * seqs + lax.rem(s, seqs), 0))


def front(seq_len, tokens, gain, shift, lerp, narrow, widen, fnarrow):
    g, d = tokens.shape
    ranks = widen.shape[0] // 5
    fd = fnarrow.shape[0]
    order = orders()
    seqs = g // seq_len // order.shape[0]
    count = 2 if g % (2 * seq_len) == 0 else 1
    rows = count * seq_len
    block = lambda w: pl.BlockSpec((rows, w), lambda s, o: (s, 0))

    def sequence(i):
        def at(s, o):
            q = s * count + i
            return (o[q // seqs] * seqs + lax.rem(q, seqs), 0)

        return pl.BlockSpec((seq_len, d), at)

    return pl.pallas_call(
        functools.partial(front_kernel, ranks, seq_len, count),
        grid_spec=pltpu.PrefetchScalarGridSpec(
            num_scalar_prefetch=1,
            grid=(g // rows,),
            in_specs=[sequence(i) for i in range(count)]
            + [whole_block(a) for a in (gain, shift, lerp, narrow, widen, fnarrow)],
            out_specs=[block(d)] * 4 + [block(5 * ranks), block(fd)],
            scratch_shapes=[
                pltpu.VMEM((d, 5 * ranks), BF),
                pltpu.VMEM((5 * ranks, d), BF),
                pltpu.VMEM((d, 2 * fd), BF),
            ],
        ),
        out_shape=[jax.ShapeDtypeStruct((g, d), BF)] * 4
        + [
            jax.ShapeDtypeStruct((g, 5 * ranks), F32),
            jax.ShapeDtypeStruct((g, fd), F32),
        ],
        compiler_params=pltpu.CompilerParams(vmem_limit_bytes=48 * MIB),
        cost_estimate=SHORT,
        name="token_shift",
    )(order, *[tokens] * count, gain, shift, lerp, narrow, widen, fnarrow)


def back_kernel(
    ranks,
    order,
    tok,
    hid,
    low,
    dk,
    dv,
    dr,
    dg,
    draw,
    gain,
    shift,
    lerp,
    narrow,
    widen,
    fnarrow,
    fwiden,
    wk,
    wv,
    wr,
    wg,
    dn_out,
    vec_out,
    dwid_out,
    dnar_out,
    dfn_out,
    narrow_low,
    widen_low,
    fnarrow_low,
    fwiden_low,
):
    @pl.when(pl.program_id(0) == 0)
    def _():
        narrow_low[...] = narrow[...].astype(BF)
        widen_low[...] = widen[...].astype(BF)
        fnarrow_low[...] = fnarrow[...].astype(BF)
        fwiden_low[...] = fwiden[...].astype(BF)
        for ref in (vec_out, dwid_out, dnar_out, dfn_out):
            ref[...] = jnp.zeros_like(ref)

    unit = normal_rows(tok[...].astype(F32))
    normed = unit * gain[...] + shift[...]
    delta = shifted(normed) - normed
    hidden = hid[...]
    hb = hidden.astype(BF)
    lowv = low[...]
    colsum = lambda v: jnp.sum(v, axis=0, keepdims=True)
    dlow = mm_nt(draw[...].astype(BF), fwiden_low[...]) * (1.0 - lowv * lowv)
    dlow = dlow.astype(BF)
    total = jnp.zeros(normed.shape, F32)
    moved = jnp.zeros(normed.shape, F32)
    dhid = []
    for f, d_ref, w_ref in (
        (0, None, None),
        (1, dk, wk),
        (2, dv, wv),
        (3, dr, wr),
        (4, dg, wg),
    ):
        rows = slice(f * ranks, (f + 1) * ranks)
        mu = lerp[f + 1 : f + 2, :] + mm(hb[:, rows], widen_low[rows, :])
        if f == 0:
            dx = mm(dlow, fnarrow_low[...])
            dfn_out[...] += mm_tn(dlow, (normed + delta * mu).astype(BF))
        else:
            dx = mm_nt(d_ref[...], w_ref[...])
        total = total + dx
        moved = moved + dx * mu
        doff = dx * delta
        vec_out[f + 1 : f + 2, :] += colsum(doff)
        db = doff.astype(BF)
        dwid_out[rows, :] += mm_tn(hb[:, rows], db)
        dhid.append(mm_nt(db, widen_low[rows, :]))
    dpre = (jnp.concatenate(dhid, axis=1) * (1.0 - hidden * hidden)).astype(BF)
    dblend = mm(dpre, narrow_low[...])
    base = lerp[0:1, :]
    dnar_out[...] += mm_tn(dpre, (normed + delta * base).astype(BF))
    vec_out[0:1, :] += colsum(dblend * delta)
    total = total + dblend
    moved = moved + dblend * base
    dn = total - moved + shifted_back(moved)
    vec_out[6:7, :] += colsum(dn * unit)
    vec_out[7:8, :] += colsum(dn)
    dn_out[...] = dn.astype(BF)


def back(seq_len, tokens, hid, low, grads, draw, params, weights):
    g, d = tokens.shape
    c = draw.shape[1]
    gain, shift, lerp, narrow, widen, fnarrow, fwiden = params
    ranks = widen.shape[0] // 5
    fd = low.shape[1]
    order = orders()
    per_seq = lambda w: pl.BlockSpec((seq_len, w), lambda s, o: (s, 0))
    kept = lambda r: pl.BlockSpec((r, d), lambda s, o: (0, 0))
    return pl.pallas_call(
        functools.partial(back_kernel, ranks),
        grid_spec=pltpu.PrefetchScalarGridSpec(
            num_scalar_prefetch=1,
            grid=(g // seq_len,),
            in_specs=[
                ordered_rows(seq_len, d, g // seq_len // order.shape[0]),
                per_seq(5 * ranks),
                per_seq(fd),
            ]
            + [per_seq(c)] * 5
            + [whole_block(a) for a in params]
            + [whole_block(a) for a in weights],
            out_specs=[per_seq(d), kept(8), kept(5 * ranks), kept(5 * ranks), kept(fd)],
            scratch_shapes=[
                pltpu.VMEM((5 * ranks, d), BF),
                pltpu.VMEM((5 * ranks, d), BF),
                pltpu.VMEM((fd, d), BF),
                pltpu.VMEM((fd, c), BF),
            ],
        ),
        out_shape=[
            jax.ShapeDtypeStruct((g, d), BF),
            jax.ShapeDtypeStruct((8, d), F32),
            jax.ShapeDtypeStruct((5 * ranks, d), F32),
            jax.ShapeDtypeStruct((5 * ranks, d), F32),
            jax.ShapeDtypeStruct((fd, d), F32),
        ],
        compiler_params=pltpu.CompilerParams(vmem_limit_bytes=56 * MIB),
        cost_estimate=SHORT,
        name="token_shift_back",
    )(order, tokens, hid, low, *grads, draw, *params, *weights)


def level_tables(length):
    p = np.arange(length)[:, None]
    u = np.arange(length)[None, :]
    levels = int(length).bit_length() - 1
    spans = []
    for l in range(1, levels):
        b = 1 << l
        same = (p // b) == (u // b)
        upper = (p // b) % 2 == 1
        spans.append(same & np.where(upper, u < p, u > p))
    spans = np.concatenate(spans, 0).astype(np.float32)
    diff = p ^ u
    level = np.where(u < p, np.floor(np.log2(np.maximum(diff, 1))), -1)
    return levels, spans, level.astype(np.int32)


def per_head(lanes, width, count, v):
    out = jnp.sum(jnp.where(lanes == 0, v, 0.0), axis=1, keepdims=True)
    if count == 1:
        return jnp.broadcast_to(out, v.shape)
    for h in range(1, count):
        one = jnp.sum(jnp.where(lanes == h, v, 0.0), axis=1, keepdims=True)
        out = jnp.where(lanes == h, one, out)
    return out


def stack_heads(lanes, count, v):
    zero = jnp.zeros_like(v)
    return jnp.concatenate([jnp.where(lanes == h, v, zero) for h in range(count)], axis=0)


def side_by_side(length, count, v):
    return jnp.concatenate([v[h * length : (h + 1) * length] for h in range(count)], axis=1)


def mix_forward(levels, count, width, r, k, v, w, u, spans, level):
    length, lanes_n = r.shape
    lanes = lax.broadcasted_iota(jnp.int32, (length, lanes_n), 1) // width
    gaps = mm(spans, jnp.concatenate(halves(w), axis=0))
    factors = [None] + [
        jnp.exp(gaps[l * length : (l + 1) * length]) for l in range(levels - 1)
    ]
    level2 = jnp.concatenate([level] * count, axis=0)
    scores = jnp.zeros((length * count, length), F32)
    parts = []
    for l in range(levels):
        e = factors[l]
        re = (r if e is None else r * e).astype(BF)
        ke = (k if e is None else k * e).astype(BF)
        parts.append((e, re, ke))
        scores = scores + jnp.where(
            level2 == l, mm_nt(stack_heads(lanes, count, re), ke), 0.0
        )
    vb = v.astype(BF)
    bonus = per_head(lanes, width, count, r * u * k)
    wkv = (
        mm(side_by_side(length, count, scores).astype(BF), stack_heads(lanes, count, vb))
        + bonus * v
    )
    center = wkv - per_head(lanes, width, count, wkv) * (1.0 / width)
    spread = per_head(lanes, width, count, center * center) * (1.0 / width)
    rstd = lax.rsqrt(spread + group_eps)
    return lanes, level2, parts, scores, bonus, vb, center * rstd, rstd


def mix_kernel(levels, count, width, *refs):
    xk, xv, xr, xg, low, wk, wv, wr, wg, we, base, fwiden, u, gain, bias, spans, level = refs[:17]
    k_out, v_out, r_out, g_out, w_out, mixed_out, near_out, far_out = refs[17:]
    for x, weights, out in ((xk, wk, k_out), (xv, wv, v_out), (xr, wr, r_out), (xg, wg, g_out)):
        out[...] = mm(x[...], weights[...])
    lh, ll = halves(low[...])
    fh, fl = halves(fwiden[...])
    w_out[...] = -jnp.exp(base[...] + (mm(lh, fh) + mm(lh, fl) + mm(ll, fh)))
    lanes = count * width
    for p in range(u.shape[1] // lanes):
        at = slice(p * lanes, (p + 1) * lanes)
        unit = mix_forward(
            levels,
            count,
            width,
            r_out[:, at],
            k_out[:, at],
            v_out[:, at],
            w_out[:, at],
            u[:, at],
            spans[...],
            level[...],
        )[6]
        gate = g_out[:, at]
        mixed_out[:, at] = (
            (unit * gain[:, at] + bias[:, at]) * (gate * jax.nn.sigmoid(gate))
        ).astype(BF)
    product = mm(mixed_out[...], we[...]).astype(BF)
    step, steps = pl.program_id(0), pl.num_programs(0)

    @pl.when(step < steps // 2)
    def _():
        near_out[...] = product

    @pl.when(step >= steps // 2)
    def _():
        far_out[...] = product


def mix(seq_len, xs, low, weights, we, vectors, fwiden):
    rows, d = xs[0].shape
    c = we.shape[0]
    half = rows // 2
    heads_here = c * HEADS // d
    width = c // heads_here
    count = 2 if heads_here % 2 == 0 else 1
    levels, spans, level = level_tables(seq_len)
    spans_a = jnp.asarray(np.concatenate([spans, spans], axis=1), BF)
    level_a = jnp.asarray(level)
    steps = half // seq_len
    block = lambda w: pl.BlockSpec((seq_len, w), lambda s: (s, 0))
    base, u, gain, bias = vectors
    kept = (*weights, we, base, fwiden, u, gain, bias, spans_a, level_a)
    shape = lambda w, t: jax.ShapeDtypeStruct((rows, w), t)
    return pl.pallas_call(
        functools.partial(mix_kernel, levels, count, width),
        grid=(2 * steps,),
        in_specs=[block(d)] * 4 + [block(low.shape[1])] + [whole_block(t) for t in kept],
        out_specs=[block(c)] * 6
        + [
            pl.BlockSpec((seq_len, d), lambda s: (jnp.minimum(s, steps - 1), 0)),
            pl.BlockSpec((seq_len, d), lambda s: (jnp.maximum(s - steps, 0), 0)),
        ],
        out_shape=[shape(c, F32)] * 5
        + [shape(c, BF)]
        + [jax.ShapeDtypeStruct((half, d), BF)] * 2,
        compiler_params=pltpu.CompilerParams(vmem_limit_bytes=28 * MIB),
        cost_estimate=lasts(20),
        name="decay_mix",
    )(*xs, low, *kept)


def wkv_back_kernel(
    levels,
    count,
    width,
    r_ref,
    k_ref,
    v_ref,
    g_ref,
    w_ref,
    dm_ref,
    u_ref,
    gain_ref,
    bias_ref,
    spans,
    spans_t,
    level_ref,
    dr_out,
    dk_out,
    dv_out,
    dg_out,
    draw_out,
    vec_out,
):
    @pl.when(pl.program_id(1) == 0)
    def _():
        vec_out[...] = jnp.zeros_like(vec_out)

    r, k, v, w, u = r_ref[...], k_ref[...], v_ref[...], w_ref[...], u_ref[...]
    level = level_ref[...]
    lanes, level2, parts, scores, bonus, vb, unit, rstd = mix_forward(
        levels, count, width, r, k, v, w, u, spans[...], level
    )
    length = r.shape[0]
    heads = functools.partial(per_head, lanes, width, count)
    stack = functools.partial(stack_heads, lanes, count)
    beside = functools.partial(side_by_side, length, count)
    colsum = lambda x: jnp.sum(x, axis=0, keepdims=True)

    gate, dm, gain = g_ref[...], dm_ref[...], gain_ref[...]
    sig = jax.nn.sigmoid(gate)
    scaled = unit * gain + bias_ref[...]
    dg_out[...] = (dm * scaled * sig * (1.0 + gate * (1.0 - sig))).astype(BF)
    dscaled = dm * gate * sig
    dunit = dscaled * gain
    dwkv = rstd * (
        dunit - heads(dunit) * (1.0 / width) - unit * (heads(dunit * unit) * (1.0 / width))
    )
    db = dwkv.astype(BF)
    dbs = stack(db)
    dscores = mm_nt(dbs, vb)

    def turned(x):
        return jnp.concatenate(
            [jnp.transpose(x[h * length : (h + 1) * length]) for h in range(count)], axis=0
        )

    dscores_t = turned(dscores)
    level_t = jnp.transpose(level)
    level2_t = jnp.concatenate([level_t] * count, axis=0)
    dv = mm(beside(turned(scores)).astype(BF), dbs) + bonus * dwkv
    dbonus = heads(dwkv * v)
    dr = dbonus * u * k
    dk = dbonus * u * r
    flows = []
    for l in range(levels):
        e, re, ke = parts[l]
        dre = mm(beside(jnp.where(level2 == l, dscores, 0.0)).astype(BF), stack(ke))
        dke = mm(beside(jnp.where(level2_t == l, dscores_t, 0.0)).astype(BF), stack(re))
        if e is None:
            dr = dr + dre
            dk = dk + dke
        else:
            dre = dre * e
            dke = dke * e
            dr = dr + dre
            dk = dk + dke
            flows.append(dre * r + dke * k)
    fh, fl = halves(jnp.concatenate(flows, axis=0))
    dw = mm(spans_t[...], fh) + mm(spans_t[...], fl)
    draw = dw * w
    dr_out[...] = dr.astype(BF)
    dk_out[...] = dk.astype(BF)
    dv_out[...] = dv.astype(BF)
    draw_out[...] = draw
    vec_out[0:1, :] += colsum(dbonus * r * k)
    vec_out[1:2, :] += colsum(dscaled * unit)
    vec_out[2:3, :] += colsum(dscaled)
    vec_out[3:4, :] += colsum(draw)


def mix_back(seq_len, r, k, v, g, w, u, gain, bias, dmixed):
    rows, c = r.shape
    heads_here = HEADS // lax.axis_size("fsdp")
    width = c // heads_here
    count = 2 if heads_here % 2 == 0 else 1
    lanes = count * width
    levels, spans, level = level_tables(seq_len)
    spans_a = jnp.asarray(np.concatenate([spans, spans], axis=1), BF)
    level_a = jnp.asarray(level)
    cols = pl.BlockSpec((seq_len, lanes), lambda p, s: (s, p))
    vec = pl.BlockSpec((1, lanes), lambda p, s: (0, p))
    grid = (c // lanes, rows // seq_len)
    params = pltpu.CompilerParams(vmem_limit_bytes=40 * MIB)
    spans_t = jnp.asarray(
        np.concatenate([s.T for s in spans.reshape(levels - 1, seq_len, seq_len)], 1), BF
    )
    return pl.pallas_call(
        functools.partial(wkv_back_kernel, levels, count, width),
        grid=grid,
        in_specs=[cols] * 6
        + [vec] * 3
        + [whole_block(spans_a), whole_block(spans_t), whole_block(level_a)],
        out_specs=[cols] * 5 + [pl.BlockSpec((4, lanes), lambda p, s: (0, p))],
        out_shape=[jax.ShapeDtypeStruct((rows, c), BF)] * 4
        + [jax.ShapeDtypeStruct((rows, c), F32), jax.ShapeDtypeStruct((4, c), F32)],
        compiler_params=params,
        cost_estimate=SHORT,
        name="decay_mix_back",
    )(r, k, v, g, w, dmixed, u, gain, bias, spans_a, spans_t, level_a)


def step_shift(length, v, back=False):
    rows = v.shape[0]
    at = lax.rem(lax.broadcasted_iota(jnp.int32, v.shape, 0), length)
    edge = at == (length - 1 if back else 0)
    return jnp.where(edge, 0.0, pltpu.roll(v, rows - 1 if back else 1, 0))


def feed_kernel(length, n2, lerp, wl, *refs):
    kc_out, sq_out, fac_out = refs[-3:]
    n = n2[...].astype(F32)
    delta = step_shift(length, n) - n
    kc = (n + delta * lerp[0:1, :]).astype(BF)
    kc_out[...] = kc
    act = mm(kc, wl[...])
    soft = jnp.maximum(act, 0.0) + jnp.log1p(jnp.exp(-jnp.abs(act)))
    fac_out[...] = 2.0 * soft * jax.nn.sigmoid(act)
    sq_out[...] = (soft * soft).astype(BF)


def feed(length, n2, lerp, wl, part, earlier=()):
    g, d = n2.shape
    f = wl.shape[1]
    half = g // 2
    rows = 2 * length if half % (2 * length) == 0 else length
    first = part * (half // rows)
    block = lambda w: pl.BlockSpec((rows, w), lambda s: (first + s, 0))
    shape = lambda w, t: jax.ShapeDtypeStruct((g, w), t)
    return pl.pallas_call(
        functools.partial(feed_kernel, length),
        grid=(half // rows,),
        in_specs=[block(d), whole_block(lerp), whole_block(wl)]
        + [pl.BlockSpec(memory_space=pl.ANY)] * len(earlier),
        out_specs=[block(d), block(f), block(f)],
        out_shape=[shape(d, BF), shape(f, BF), shape(f, F32)],
        input_output_aliases={3 + i: i for i in range(len(earlier))},
        compiler_params=pltpu.CompilerParams(vmem_limit_bytes=52 * MIB),
        cost_estimate=lasts(6),
        name="feed",
    )(n2, lerp, wl, *earlier)


def value_kernel(own_order, order, sq, wc, near_out, far_out):
    some, _, c = near_out.shape
    for i in range(2 * some):
        at = pl.ds(pl.multiple_of(order[i] * c, c), c) if own_order else slice(i * c, (i + 1) * c)
        out = near_out if i < some else far_out
        out[i % some] = mm(sq[...], wc[:, at]).astype(BF)


def value_product(length, sq, wc, part):
    g, f = sq.shape
    d = wc.shape[1]
    n = lax.axis_size("fsdp")
    half = g // 2
    rows = 2 * length if half % (2 * length) == 0 else length
    first = part * (half // rows)
    return pl.pallas_call(
        functools.partial(value_kernel, paired()),
        grid_spec=pltpu.PrefetchScalarGridSpec(
            num_scalar_prefetch=1,
            grid=(half // rows,),
            in_specs=[pl.BlockSpec((rows, f), lambda s, o: (first + s, 0)), whole_block(wc)],
            out_specs=[pl.BlockSpec((n // 2, rows, d // n), lambda s, o: (0, s, 0))] * 2,
        ),
        out_shape=[jax.ShapeDtypeStruct((n // 2, half, d // n), BF)] * 2,
        compiler_params=pltpu.CompilerParams(vmem_limit_bytes=40 * MIB),
        cost_estimate=lasts(4),
        name="value_product",
    )(orders(), sq, wc)


def pair_kernel(near0, near1, got0, got1, *outs):
    half = near0.shape[1]
    for q, out in enumerate(outs):

        @pl.when(pl.program_id(0) == q)
        def _():
            out[:half, :] = (near0[0].astype(F32) + got1[0].astype(F32)).astype(BF)
            out[half:, :] = (near1[0].astype(F32) + got0[0].astype(F32)).astype(BF)


def gated_kernel(paired_order, adj, gate, *refs):
    *parts, gated_out, dgate_out = refs
    rows = adj.shape[0] // (8 if paired_order else 1)
    for i, own in enumerate(ORDER if paired_order else (0,)):
        at = slice(i * rows, (i + 1) * rows)
        value = parts[0][at, :].astype(F32)
        for q, part in enumerate(parts[1:]):
            p = ORDER.index((2 * q + 2) ^ own)
            value = value + part[p * rows : (p + 1) * rows, :].astype(F32)
        g = gate[at, :].astype(F32)
        gated = g * value
        gated_out[at, :] = gated.astype(BF)
        dgate_out[at, :] = (adj[at, :].astype(F32) * gated * (1.0 - g)).astype(BF)


def gated_value(adj, gate, halves_of_value):
    (near0, far0), (near1, far1) = halves_of_value
    g, c = gate.shape
    if paired():
        got0, got1 = swap(far0, 1), swap(far1, 1)
        block = pl.BlockSpec((1, g // 2, c), lambda q: (q, 0, 0))
        parts = pl.pallas_call(
            pair_kernel,
            grid=(4,),
            in_specs=[block] * 4,
            out_specs=[pl.BlockSpec((g, c), lambda q: (0, 0))] * 4,
            out_shape=[jax.ShapeDtypeStruct((g, c), BF)] * 4,
            compiler_params=pltpu.CompilerParams(vmem_limit_bytes=32 * MIB),
            cost_estimate=SHORT,
            name="pairs",
        )(near0, near1, got0, got1)
        parts = [parts[0]] + [swap(parts[q], 2 * q) for q in (1, 2, 3)]
        rows = g
    else:
        sums = [
            lax.psum_scatter(
                jnp.concatenate(t, axis=0), "fsdp", scatter_dimension=0, tiled=True
            )[0]
            for t in halves_of_value
        ]
        parts = [jnp.concatenate(sums, axis=0)]
        rows = g // lax.axis_size("fsdp")
    block = pl.BlockSpec((rows, c), lambda s: (s, 0))
    return pl.pallas_call(
        functools.partial(gated_kernel, paired()),
        grid=(g // rows,),
        in_specs=[block] * (2 + len(parts)),
        out_specs=[block] * 2,
        out_shape=[jax.ShapeDtypeStruct((g, c), BF)] * 2,
        compiler_params=pltpu.CompilerParams(vmem_limit_bytes=32 * MIB),
        cost_estimate=SHORT,
        name="gated_value",
    )(adj, gate, *parts)


def gate_kernel(length, n2, adj, lerp, wa, rc_out, gate_out, dv_out):
    n = n2[...].astype(F32)
    rc = (n + (step_shift(length, n) - n) * lerp[1:2, :]).astype(BF)
    rc_out[...] = rc
    gate = jax.nn.sigmoid(mm(rc, wa[...]))
    gate_out[...] = gate.astype(BF)
    dv_out[...] = (adj[...].astype(F32) * gate).astype(BF)


def feed_gate(length, n2, adj, lerp, wa):
    g, d = n2.shape
    c = wa.shape[1]
    rows = 2 * length if g % (2 * length) == 0 else length
    block = lambda w: pl.BlockSpec((rows, w), lambda s: (s, 0))
    return pl.pallas_call(
        functools.partial(gate_kernel, length),
        grid=(g // rows,),
        in_specs=[block(d), block(c), whole_block(lerp), whole_block(wa)],
        out_specs=[block(d), block(c), block(c)],
        out_shape=[jax.ShapeDtypeStruct((g, w), BF) for w in (d, c, c)],
        compiler_params=pltpu.CompilerParams(vmem_limit_bytes=32 * MIB),
        cost_estimate=SHORT,
        name="feed_gate",
    )(n2, adj, lerp, wa)


def feed_back_kernel(length, dv, n2, fac, dgate, lerp, wl, wa, wc, dkey_out, dn_out, vec_out):
    @pl.when(pl.program_id(0) == 0)
    def _():
        vec_out[...] = jnp.zeros_like(vec_out)

    dkey = (mm_nt(dv[...], wc[...]) * fac[...]).astype(BF)
    dkey_out[...] = dkey
    n = n2[...].astype(F32)
    delta = step_shift(length, n) - n
    dk = mm_nt(dkey, wl[...])
    dr = mm_nt(dgate[...], wa[...])
    vec_out[0:1, :] += jnp.sum(dk * delta, axis=0, keepdims=True)
    vec_out[1:2, :] += jnp.sum(dr * delta, axis=0, keepdims=True)
    moved = dk * lerp[0:1, :] + dr * lerp[1:2, :]
    dn_out[...] = (dk + dr - moved + step_shift(length, moved, True)).astype(BF)


def feed_back(length, dv, n2, fac, dgate, lerp, wl, wa, wc):
    g, d = n2.shape
    f, c = wc.shape[0], dgate.shape[1]
    rows = 2 * length if g % (2 * length) == 0 else length
    block = lambda w: pl.BlockSpec((rows, w), lambda s: (s, 0))
    return pl.pallas_call(
        functools.partial(feed_back_kernel, length),
        grid=(g // rows,),
        in_specs=[block(d), block(d), block(f), block(c)]
        + [whole_block(a) for a in (lerp, wl, wa, wc)],
        out_specs=[block(f), block(d), pl.BlockSpec((2, d), lambda s: (0, 0))],
        out_shape=[
            jax.ShapeDtypeStruct((g, f), BF),
            jax.ShapeDtypeStruct((g, d), BF),
            jax.ShapeDtypeStruct((2, d), F32),
        ],
        compiler_params=pltpu.CompilerParams(vmem_limit_bytes=52 * MIB),
        cost_estimate=SHORT,
        name="feed_back",
    )(dv, n2, fac, dgate, lerp, wl, wa, wc)


def body(
    incoming_symbols,
    string_extents,
    adjoint_signal,
    first_scaling_factor,
    first_scaling_shift,
    lerp_factors,
    lerp_narrow_weights,
    lerp_widen_weights,
    fading_baseline,
    fading_narrow_weights,
    fading_widen_weights,
    present_reward,
    acceptor_weights,
    lookup_weights,
    content_weights,
    valve_weights,
    emission_weights,
    cluster_scaling_factor,
    cluster_scaling_shift,
    second_scaling_factor,
    second_scaling_shift_vec,
    feed_lerp_factors,
    feed_lookup_weights,
    feed_content_weights,
    feed_acceptor_weights,
):
    seqs, length, d = incoming_symbols.shape
    n = lax.axis_size("fsdp")
    me = lax.axis_index("fsdp")
    c = d // n
    home = seqs * length
    plane = home * n
    ranks = lerp_widen_weights.shape[1]
    fd = fading_narrow_weights.shape[1]

    tok_home = incoming_symbols.reshape(home, d)
    tokens = lax.all_gather(tok_home, "fsdp", axis=0, tiled=True)
    mix_weights = Exchange(
        (
            lookup_weights,
            content_weights,
            acceptor_weights,
            valve_weights,
        ),
        1,
    )
    mix_weights.across_cores()
    mix_weights.across_chips()
    positions = lax.broadcasted_iota(jnp.int32, (seqs, length), 1)
    mask = (positions < string_extents[:, None]).astype(F32).reshape(home, 1)
    adjoint = adjoint_signal.reshape(home, d) * mask.astype(BF)
    d_out = adjoint.astype(F32)

    row = lambda v: v.reshape(1, -1)
    mine = lambda v: lax.dynamic_slice_in_dim(v, me * c, c, v.ndim - 1)
    gain1, shift1 = row(first_scaling_factor), row(first_scaling_shift)
    narrow, fnarrow = lerp_narrow_weights.T, fading_narrow_weights.T
    widen = lerp_widen_weights.reshape(5 * ranks, d)
    feed_weights = Exchange([feed_lookup_weights, feed_acceptor_weights], 1)
    feed_weights.across_cores()
    (tokens,) = feed_weights.after(*mix_weights.arrived(tokens, count=2))
    xk, xv, xr, xg, hidden, low = front(
        length, tokens, gain1, shift1, lerp_factors, narrow, widen, fnarrow
    )
    (low,) = feed_weights.after(*mix_weights.arrived(low))
    feed_weights.across_chips()
    wk, wv, wr, wg = mix_weights.results()
    fwiden_mine = mine(fading_widen_weights)
    base, u, gn_gain, gn_bias = (
        mine(row(t))
        for t in (
            fading_baseline,
            present_reward,
            cluster_scaling_factor,
            cluster_scaling_shift,
        )
    )
    k, v, r, g, w, mixed, near, far = mix(
        length,
        (xk, xv, xr, xg),
        low,
        (wk, wv, wr, wg),
        emission_weights,
        (base, u, gn_gain, gn_bias),
        fwiden_mine,
    )
    near, far = feed_weights.arrived(near, far)
    branch = scatter_tokens(near, far)
    wl, wa = feed_weights.results()
    branch, wl, wa = hold(branch, wl, wa)
    branch, adjoint = hold(branch, adjoint)
    adjoint_cols = spread_features(adjoint)
    residual = tok_home.astype(F32) + branch

    center = residual - jnp.mean(residual, axis=-1, keepdims=True)
    rstd2 = lax.rsqrt(jnp.mean(center * center, axis=-1, keepdims=True) + norm_eps)
    unit2 = center * rstd2
    normed2, _ = gather_tokens(
        (unit2 * second_scaling_factor + second_scaling_shift_vec).astype(BF)
    )
    fc = feed_content_weights.shape[0]
    recept_chan, gate, d_value_mine = feed_gate(
        length, normed2, adjoint_cols, feed_lerp_factors, wa
    )
    feed_part = lambda *t: feed(length, normed2, feed_lerp_factors, wl, *t)
    d_value, (key_chan, squared, factor) = gather_features_of_tokens(
        d_value_mine, (lambda: feed_part(0), lambda *done: feed_part(1, done))
    )
    d_content = mm_tn(squared, d_value).astype(BF)
    d_value, d_content, squared = hold(d_value, d_content, squared)
    content_share = rep_scatter(d_content)
    value_part = lambda part: value_product(length, squared, feed_content_weights, part)
    gated, d_gate = gated_value(adjoint_cols, gate, (value_part(0), value_part(1)))

    d_key, d_normed2, feed_lerp_part = feed_back(
        length, d_value, normed2, factor, d_gate, feed_lerp_factors, wl, wa, feed_content_weights
    )
    d_normed2, content_share = hold(d_normed2, content_share)
    content_sum = rep_gather(content_share)
    feed_share = rep_scatter_cols(
        (mm_tn(key_chan, d_key).astype(BF), mm_tn(recept_chan, d_gate).astype(BF))
    )
    d_normed2 = scatter_tokens(d_normed2[: plane // 2], d_normed2[plane // 2 :])

    def norm_back(unit, rstd, e):
        return rstd * (
            e
            - jnp.mean(e, axis=-1, keepdims=True)
            - unit * jnp.mean(e * unit, axis=-1, keepdims=True)
        )

    layer_output = (residual + home_features(gated).astype(F32)) * mask
    d_residual = d_out + norm_back(unit2, rstd2, d_normed2 * second_scaling_factor)
    norm2_part = jnp.stack([jnp.sum(d_normed2 * unit2, axis=0), jnp.sum(d_normed2, axis=0)])

    d_branch, _ = gather_tokens(d_residual.astype(BF))
    d_mixed = mm_nt(d_branch, emission_weights)
    d_emission = mm_tn(mixed, d_branch).astype(BF)
    d_r, d_k, d_v, d_g, d_raw, mix_vec = mix_back(
        length, r, k, v, g, w, u, gn_gain, gn_bias, d_mixed
    )
    d_r, d_k, d_v, d_g, feed_share = hold(d_r, d_k, d_v, d_g, feed_share)
    time_share, emission_share = rep_scatter_cols(
        [mm_tn(x, t).astype(BF) for x, t in ((xk, d_k), (xv, d_v), (xr, d_r), (xg, d_g))],
        d_emission,
    )
    feed_sums = Exchange([feed_share[:, :fc], feed_share[:, fc:]], 0)
    feed_sums.across_cores()
    feed_sums.across_chips()
    d_normed, vec_part, widen_part, narrow_part, fnarrow_part = back(
        length,
        tokens,
        hidden,
        low,
        (d_k, d_v, d_r, d_g),
        d_raw,
        (gain1, shift1, lerp_factors, narrow, widen, fnarrow, fwiden_mine),
        (wk, wv, wr, wg),
    )
    d_normed, content_sum = feed_sums.arrived(*hold(d_normed, content_sum))
    feed_sum = rep_gather(jnp.concatenate(feed_sums.results(), axis=1))
    d_normed = scatter_tokens(d_normed[: plane // 2], d_normed[plane // 2 :])
    small = scatter_features(
        jnp.concatenate(
            [vec_part, widen_part, narrow_part, fnarrow_part, norm2_part, feed_lerp_part], axis=0
        ).astype(BF)
    )
    fwiden_part = mm_tn(low.astype(BF), d_raw.astype(BF))
    small = rep_sum(jnp.concatenate([small, fwiden_part, mix_vec], axis=0).astype(BF))
    small = gather_features(small.astype(BF)).astype(F32)
    small, time_share = hold(small, time_share)
    time_sums = Exchange([time_share[:, i * c : (i + 1) * c] for i in range(4)], 0)
    time_sums.across_cores()
    time_sums.across_chips()
    time_sum = rep_gather(jnp.concatenate([*time_sums.results(), emission_share], axis=1))
    (feed_content_grads,) = widened(content_sum, (d,))
    feed_lookup_grads, feed_acceptor_grads = widened(feed_sum, (n * fc, n * c))
    (
        lookup_weights_grads,
        content_weights_grads,
        acceptor_weights_grads,
        valve_weights_grads,
        emission_weights_grads,
    ) = widened(time_sum, (d,) * 5)
    tok_f = tok_home.astype(F32)
    center1 = tok_f - jnp.mean(tok_f, axis=-1, keepdims=True)
    rstd1 = lax.rsqrt(jnp.mean(center1 * center1, axis=-1, keepdims=True) + norm_eps)
    token_grad = d_residual + norm_back(center1 * rstd1, rstd1, d_normed * first_scaling_factor)
    cuts = np.cumsum([8, 5 * ranks, 5 * ranks, fd, 2, 2, fd, 4])
    vec, widen_g, narrow_g, fnarrow_g, norm2_g, feed_lerp_g, fwiden_g, mix_g = (
        small[a:b] for a, b in zip([0, *cuts[:-1]], cuts)
    )
    return (
        layer_output.reshape(seqs, length, d),
        token_grad.reshape(seqs, length, d),
        vec[6],
        vec[7],
        vec[:6],
        narrow_g.T,
        widen_g.reshape(5, ranks, d),
        mix_g[3],
        fnarrow_g.T,
        fwiden_g,
        mix_g[0],
        acceptor_weights_grads,
        lookup_weights_grads,
        content_weights_grads,
        valve_weights_grads,
        emission_weights_grads,
        mix_g[1],
        mix_g[2],
        norm2_g[0],
        norm2_g[1],
        feed_lerp_g,
        feed_lookup_grads,
        feed_content_grads,
        feed_acceptor_grads,
    )


def solution(mesh):
    seq = P(("fsdp", "rep"), None, None)
    row = P("fsdp", None)
    in_specs = (
        (seq, P(("fsdp", "rep")), seq) + (P(),) * 9 + (row,) * 5 + (P(),) * 5 + (row,) * 3
    )
    out_specs = (seq, seq) + (P(),) * 9 + (row,) * 5 + (P(),) * 5 + (row,) * 3
    return jax.shard_map(body, mesh=mesh, in_specs=in_specs, out_specs=out_specs, check_vma=False)
```

```python
import functools

import jax
import jax.numpy as jnp
import numpy as np
from jax import lax
from jax.experimental import pallas as pl
from jax.experimental.pallas import tpu as pltpu
from jax.sharding import PartitionSpec as P

HEADS = 32
norm_eps = 1e-05
group_eps = 1.0
BF = jnp.bfloat16
F32 = jnp.float32
MIB = 1 << 20
SHORT = pl.CostEstimate(flops=1, bytes_accessed=1, transcendentals=0)


def lasts(us):
    return pl.CostEstimate(flops=int(us * 1e9), bytes_accessed=1, transcendentals=0)


def mm(a, b):
    return jnp.dot(a, b, preferred_element_type=F32)


def mm_nt(a, b):
    return lax.dot_general(a, b, (((1,), (1,)), ((), ())), preferred_element_type=F32)


def mm_tn(a, b):
    return lax.dot_general(a, b, (((0,), (0,)), ((), ())), preferred_element_type=F32)


def halves(v):
    high = v.astype(BF)
    return high, (v - high.astype(F32)).astype(BF)


def hold(*values):
    return lax.optimization_barrier(values)


def paired():
    return lax.axis_size("fsdp") == 8


def swap(v, m):
    return lax.ppermute(v, "fsdp", [(i, i ^ m) for i in range(8)])


def place():
    me = lax.axis_index("fsdp")
    return me // 2, lax.rem(me, 2)


def by_core(core, mine, other, axis):
    return jnp.where(
        core == 0,
        jnp.concatenate([mine, other], axis=axis),
        jnp.concatenate([other, mine], axis=axis),
    )


def gather_tokens(v, beside=tuple):
    if not paired():
        return lax.all_gather(v, "fsdp", axis=0, tiled=True), beside()
    r = v.shape[0] // 2
    a, b = v[:r], v[r:]
    a1, b1 = swap(a, 2), swap(b, 4)
    a2 = swap(jnp.concatenate([a, a1], axis=0), 4)
    b2 = swap(jnp.concatenate([b, b1], axis=0), 2)
    held = beside()
    if held:
        a2, b2, *held = hold(a2, b2, *held)
    near = jnp.concatenate([v, a1, b2[:r], a2[:r], b1, a2[r:], b2[r:]], axis=0)
    return jnp.concatenate([near, swap(near, 1)], axis=0), held


def scatter_tokens(near, far):
    if not paired():
        v = jnp.concatenate([near, far], axis=0)
        return lax.psum_scatter(v, "fsdp", scatter_dimension=0, tiled=True).astype(F32)
    r = near.shape[0] // 4
    got = swap(far, 1)
    pair = lambda q: near[q * r : (q + 1) * r].astype(F32) + got[q * r : (q + 1) * r].astype(F32)
    far = [swap(pair(q).astype(BF), 2 * q) for q in (1, 2, 3)]
    return pair(0) + (far[0].astype(F32) + far[1].astype(F32)) + far[2].astype(F32)


def home_features(v):
    if not paired():
        return lax.all_to_all(v, "fsdp", split_axis=0, concat_axis=1, tiled=True)
    chip, core = place()
    r, c = v.shape[0] // 8, v.shape[1]
    both = by_core(core, v[: 4 * r], swap(v[4 * r :], 1), 1)
    out = jnp.zeros((r, 8 * c), v.dtype)
    for q in range(4):
        piece = both[q * r : (q + 1) * r]
        piece = piece if q == 0 else swap(piece, 2 * q)
        out = lax.dynamic_update_slice_in_dim(out, piece, (chip ^ q) * (2 * c), 1)
    return out


ORDER = (0, 2, 4, 6, 1, 3, 5, 7)


def line_up_kernel(order, near, far, out):
    rows = near.shape[1] // 8
    for i, m in enumerate(ORDER):

        @pl.when(pl.program_id(0) == i)
        def _():
            source = near if i < 4 else far
            for q, own in enumerate(ORDER):
                p = ORDER.index(m ^ own)
                out[q * rows : (q + 1) * rows, :] = source[0, p * rows : (p + 1) * rows, :]


def gather_features_of_tokens(v, beside):
    first, second = beside
    if not paired():
        return lax.all_gather(v, "fsdp", axis=1, tiled=True), second(*first())
    g, c = v.shape
    r = g // 2
    a, b = v[:r], v[r:]
    a1, b1 = swap(a, 2), swap(b, 4)
    a1, b1, *held = hold(a1, b1, *first())
    a2 = swap(jnp.concatenate([a, a1], axis=0), 4)
    b2 = swap(jnp.concatenate([b, b1], axis=0), 2)
    a2, b2, *held = hold(a2, b2, *second(*held))
    near = jnp.concatenate([v, a1, b2[:r], a2[:r], b1, a2[r:], b2[r:]], axis=0).reshape(4, g, c)
    far = swap(near, 1)
    lined = pl.pallas_call(
        line_up_kernel,
        grid_spec=pltpu.PrefetchScalarGridSpec(
            num_scalar_prefetch=1,
            grid=(8,),
            in_specs=[
                pl.BlockSpec((1, g, c), lambda i, o: (jnp.minimum(i, 3), 0, 0)),
                pl.BlockSpec((1, g, c), lambda i, o: (jnp.maximum(i - 4, 0), 0, 0)),
            ],
            out_specs=pl.BlockSpec((g, c), lambda i, o: (0, o[i])),
        ),
        out_shape=jax.ShapeDtypeStruct((g, 8 * c), v.dtype),
        compiler_params=pltpu.CompilerParams(vmem_limit_bytes=32 * MIB),
        cost_estimate=SHORT,
        name="line_up",
    )(orders(), near, far)
    return lined, held


def spread_features(v):
    if not paired():
        return lax.all_to_all(v, "fsdp", split_axis=1, concat_axis=0, tiled=True)
    chip, core = place()
    c = v.shape[1] // 8
    near = []
    for q in range(4):
        piece = lax.dynamic_slice_in_dim(v, (chip ^ q) * (2 * c), 2 * c, 1)
        near.append(piece if q == 0 else swap(piece, 2 * q))
    near = jnp.concatenate(near, axis=0)
    cut = lambda which: lax.dynamic_slice_in_dim(near, which * c, c, 1)
    return jnp.concatenate([cut(core), swap(cut(1 - core), 1)], axis=0)


def orders():
    me = lax.axis_index("fsdp")
    if not paired():
        return jnp.arange(lax.axis_size("fsdp"), dtype=jnp.int32)
    return jnp.stack([me ^ m for m in ORDER]).astype(jnp.int32)


def pack_kernel(count, order, *refs):
    parts, (near, far) = refs[:count], refs[count:]
    for half, out in enumerate((near, far)):

        @pl.when(pl.program_id(0) // 4 == half)
        def _():
            at = 0
            for p in parts:
                out[0, :, at : at + p.shape[1]] = p[...]
                at += p.shape[1]


def unpack_kernel(widths, order, *refs):
    pieces, outs = refs[:8], refs[8:]
    for m, piece in enumerate(pieces):

        @pl.when(pl.program_id(0) == m)
        def _():
            at = 0
            for w, out in zip(widths, outs):
                out[...] = piece[0, :, at : at + w]
                at += w


class Exchange:
    def __init__(self, parts, side):
        self.side = side
        self.parts = parts
        if not paired():
            return
        if side == 1:
            r, self.widths = parts[0].shape[0], [p.shape[1] // 8 for p in parts]
            at = lambda m, o: (0, o[m])
        else:
            r, self.widths = parts[0].shape[0] // 8, [p.shape[1] for p in parts]
            at = lambda m, o: (o[m], 0)
        total = sum(self.widths)
        out = jax.ShapeDtypeStruct((4, r, total), parts[0].dtype)
        self.near, self.far = pl.pallas_call(
            functools.partial(pack_kernel, len(parts)),
            grid_spec=pltpu.PrefetchScalarGridSpec(
                num_scalar_prefetch=1,
                grid=(8,),
                in_specs=[pl.BlockSpec((r, w), at) for w in self.widths],
                out_specs=[
                    pl.BlockSpec((1, r, total), lambda m, o: (jnp.minimum(m, 3), 0, 0)),
                    pl.BlockSpec((1, r, total), lambda m, o: (jnp.maximum(m - 4, 0), 0, 0)),
                ],
            ),
            out_shape=[out, out],
            compiler_params=pltpu.CompilerParams(vmem_limit_bytes=32 * MIB),
            name="pack",
        )(orders(), *parts)

    def across_cores(self):
        if paired():
            self.far = swap(self.far, 1)

    def after(self, *values):
        if not paired():
            return values
        *values, self.near, self.far = hold(*values, self.near, self.far)
        return values

    def across_chips(self):
        if paired():
            self.got = [
                swap(jnp.concatenate([self.near[q : q + 1], self.far[q : q + 1]], axis=0), 2 * q)
                for q in (1, 2, 3)
            ]

    def moving(self):
        return self.got if paired() else []

    def waiting(self):
        return [self.near, self.far] if paired() else []

    def resume(self, held):
        if not paired():
            return held
        if hasattr(self, "got"):
            self.got, held = list(held[:3]), held[3:]
        else:
            (self.near, self.far), held = held[:2], held[2:]
        return held

    def arrived(self, *values, count=3):
        if not paired():
            return values
        held = hold(*values, *self.got[:count])
        self.got[:count] = held[len(values) :]
        return held[: len(values)]

    def results(self):
        if not paired():
            split, concat = (1, 0) if self.side == 1 else (0, 1)
            return [
                lax.all_to_all(p, "fsdp", split_axis=split, concat_axis=concat, tiled=True)
                for p in self.parts
            ]
        _, r, total = self.near.shape
        block = lambda i: pl.BlockSpec((1, r, total), lambda m, o: (i, 0, 0))
        if self.side == 1:
            at = lambda m, o: (o[m], 0)
            shape = lambda w: (8 * r, w)
        else:
            at = lambda m, o: (0, o[m])
            shape = lambda w: (r, 8 * w)
        return pl.pallas_call(
            functools.partial(unpack_kernel, self.widths),
            grid_spec=pltpu.PrefetchScalarGridSpec(
                num_scalar_prefetch=1,
                grid=(8,),
                in_specs=[block(0)] * 4 + [block(0)] + [block(1)] * 3,
                out_specs=[pl.BlockSpec((r, w), at) for w in self.widths],
            ),
            out_shape=[jax.ShapeDtypeStruct(shape(w), self.near.dtype) for w in self.widths],
            compiler_params=pltpu.CompilerParams(vmem_limit_bytes=32 * MIB),
            name="unpack",
        )(orders(), self.near, *self.got, self.far, *self.got)


def rep_scatter(v):
    return lax.psum_scatter(v, "rep", scatter_dimension=0, tiled=True)


def rep_gather(v):
    return lax.all_gather(v, "rep", axis=0, tiled=True)


def share_kernel(blocks, shares, rows_at_end, *refs):
    *parts, out = refs
    rows = out.shape[2]

    def put(some):
        at = 0
        for p in some:
            w = p.shape[1]
            for i in range(shares):
                out[i, 0, :, at : at + w] = p[i * rows : (i + 1) * rows, :]
            at += w

    if not rows_at_end:
        put(parts)
        return

    @pl.when(pl.program_id(0) < blocks)
    def _():
        put(parts[:-1])

    @pl.when(pl.program_id(0) >= blocks)
    def _():
        put(parts[-1:])


def rep_scatter_cols(parts, last=None):
    n, z = lax.axis_size("fsdp"), lax.axis_size("rep")
    rows, c = parts[0].shape[0], sum(p.shape[1] for p in parts)
    share = rows // (n * z)
    extra = 0 if last is None else last.shape[1] // c
    specs = [
        pl.BlockSpec((rows // n, p.shape[1]), lambda i: (jnp.minimum(i, n - 1), 0)) for p in parts
    ]
    if extra:
        specs.append(pl.BlockSpec((rows // n, c), lambda i: (0, jnp.maximum(i - n, 0))))
        parts = [*parts, last]
    v = pl.pallas_call(
        functools.partial(share_kernel, n, z, extra > 0),
        grid=(n + extra,),
        in_specs=specs,
        out_specs=pl.BlockSpec((z, 1, share, c), lambda i: (0, i, 0, 0)),
        out_shape=jax.ShapeDtypeStruct((z, n + extra, share, c), parts[0].dtype),
        compiler_params=pltpu.CompilerParams(vmem_limit_bytes=32 * MIB),
        cost_estimate=SHORT,
        name="shares",
    )(*parts)
    v = rep_scatter(v.reshape(z * (n + extra) * share, c))
    if last is None:
        return v
    tail = v[n * share :].reshape(extra, share, c).transpose(1, 0, 2).reshape(share, extra * c)
    return v[: n * share], tail


def widen_kernel(*refs):
    joined, *outs = refs
    at = 0
    for out in outs:
        w = out.shape[1]
        out[...] = joined[:, at : at + w].astype(F32)
        at += w


def widened(v, widths):
    r = v.shape[0]
    rows = min(r, 32)
    return pl.pallas_call(
        widen_kernel,
        grid=(r // rows,),
        in_specs=[pl.BlockSpec((rows, v.shape[1]), lambda i: (i, 0))],
        out_specs=[pl.BlockSpec((rows, w), lambda i: (i, 0)) for w in widths],
        out_shape=[jax.ShapeDtypeStruct((r, w), F32) for w in widths],
        compiler_params=pltpu.CompilerParams(vmem_limit_bytes=32 * MIB),
        cost_estimate=SHORT,
        name="widened",
    )(v)


def rep_sum(v):
    n = lax.axis_size("rep")
    if n & (n - 1):
        return lax.psum(v, "rep").astype(F32)
    total, step = v.astype(F32), 1
    while step < n:
        got = lax.ppermute(total.astype(v.dtype), "rep", [(i, i ^ step) for i in range(n)])
        total, step = total + got.astype(F32), step * 2
    return total


def scatter_features(v):
    if not paired():
        return lax.psum_scatter(v, "fsdp", scatter_dimension=1, tiled=True).astype(F32)
    chip, core = place()
    r = v.shape[0]
    v = v.reshape(r, 4, 2, -1)
    cut = lambda which: lax.dynamic_index_in_dim(v, which, 2, keepdims=False).transpose(1, 0, 2)
    pair = cut(core).astype(F32) + swap(cut(1 - core), 1).astype(F32)
    low = pair.astype(BF)
    total = lax.dynamic_index_in_dim(pair, chip, 0, keepdims=False)
    for q in (1, 2, 3):
        got = swap(lax.dynamic_index_in_dim(low, chip ^ q, 0, keepdims=False), 2 * q)
        total = total + got.astype(F32)
    return total


def gather_features(v):
    if not paired():
        return lax.all_gather(v, "fsdp", axis=1, tiled=True)
    chip, core = place()
    r, c = v.shape
    both = by_core(core, v, swap(v, 1), 1)
    out = jnp.zeros((r, 8 * c), v.dtype)
    for q in range(4):
        got = both if q == 0 else swap(both, 2 * q)
        out = lax.dynamic_update_slice_in_dim(out, got, (chip ^ q) * (2 * c), 1)
    return out


def whole_block(a):
    return pl.BlockSpec(a.shape, lambda *_: (0,) * a.ndim, pipeline_mode=pl.Buffered(1))


def shifted(v):
    first = lax.broadcasted_iota(jnp.int32, v.shape, 0) == 0
    return jnp.where(first, 0.0, pltpu.roll(v, 1, 0))


def shifted_back(v):
    last = lax.broadcasted_iota(jnp.int32, v.shape, 0) == v.shape[0] - 1
    return jnp.where(last, 0.0, pltpu.roll(v, v.shape[0] - 1, 0))


def normal_rows(v):
    center = v - jnp.mean(v, axis=-1, keepdims=True)
    spread = jnp.mean(center * center, axis=-1, keepdims=True)
    return center * lax.rsqrt(spread + norm_eps)


def front_kernel(ranks, length, count, order, *refs):
    tokens, (gain, shift, lerp, narrow, widen, fnarrow) = refs[:count], refs[count : count + 6]
    xk, xv, xr, xg, hid, low, nw, wb, fw = refs[count + 6 :]
    fd = low.shape[1]

    @pl.when(pl.program_id(0) == 0)
    def _():
        nw[...] = jnp.transpose(narrow[...]).astype(BF)
        wb[...] = widen[...].astype(BF)
        fw[:, :fd], fw[:, fd:] = halves(jnp.transpose(fnarrow[...]))

    tok = jnp.concatenate([t[...].astype(F32) for t in tokens], axis=0)
    normed = normal_rows(tok) * gain[...] + shift[...]
    delta = step_shift(length, normed) - normed
    hidden = jnp.tanh(mm((normed + delta * lerp[0:1, :]).astype(BF), nw[...]))
    hid[...] = hidden
    hb = hidden.astype(BF)
    for f, out in ((1, xk), (2, xv), (3, xr), (4, xg), (0, None)):
        rows = slice(f * ranks, (f + 1) * ranks)
        x = normed + delta * (lerp[f + 1 : f + 2, :] + mm(hb[:, rows], wb[rows, :]))
        if out is not None:
            out[...] = x.astype(BF)
        else:
            dh, dl = halves(x)
            pre = mm(dh, fw[...])
            low[...] = jnp.tanh(pre[:, :fd] + pre[:, fd:] + mm(dl, fw[:, :fd]))


def ordered_rows(seq_len, d, seqs):
    return pl.BlockSpec((seq_len, d), lambda s, o: (o[s // seqs] * seqs + lax.rem(s, seqs), 0))


def front(seq_len, tokens, gain, shift, lerp, narrow, widen, fnarrow):
    g, d = tokens.shape
    ranks = widen.shape[0] // 5
    fd = fnarrow.shape[0]
    order = orders()
    seqs = g // seq_len // order.shape[0]
    count = 2 if g % (2 * seq_len) == 0 else 1
    rows = count * seq_len
    block = lambda w: pl.BlockSpec((rows, w), lambda s, o: (s, 0))

    def sequence(i):
        def at(s, o):
            q = s * count + i
            return (o[q // seqs] * seqs + lax.rem(q, seqs), 0)

        return pl.BlockSpec((seq_len, d), at)

    return pl.pallas_call(
        functools.partial(front_kernel, ranks, seq_len, count),
        grid_spec=pltpu.PrefetchScalarGridSpec(
            num_scalar_prefetch=1,
            grid=(g // rows,),
            in_specs=[sequence(i) for i in range(count)]
            + [whole_block(a) for a in (gain, shift, lerp, narrow, widen, fnarrow)],
            out_specs=[block(d)] * 4 + [block(5 * ranks), block(fd)],
            scratch_shapes=[
                pltpu.VMEM((d, 5 * ranks), BF),
                pltpu.VMEM((5 * ranks, d), BF),
                pltpu.VMEM((d, 2 * fd), BF),
            ],
        ),
        out_shape=[jax.ShapeDtypeStruct((g, d), BF)] * 4
        + [
            jax.ShapeDtypeStruct((g, 5 * ranks), F32),
            jax.ShapeDtypeStruct((g, fd), F32),
        ],
        compiler_params=pltpu.CompilerParams(vmem_limit_bytes=48 * MIB),
        cost_estimate=SHORT,
        name="token_shift",
    )(order, *[tokens] * count, gain, shift, lerp, narrow, widen, fnarrow)


def back_kernel(
    ranks,
    order,
    tok,
    hid,
    low,
    dk,
    dv,
    dr,
    dg,
    draw,
    gain,
    shift,
    lerp,
    narrow,
    widen,
    fnarrow,
    fwiden,
    wk,
    wv,
    wr,
    wg,
    dn_out,
    vec_out,
    dwid_out,
    dnar_out,
    dfn_out,
    narrow_low,
    widen_low,
    fnarrow_low,
    fwiden_low,
):
    @pl.when(pl.program_id(0) == 0)
    def _():
        narrow_low[...] = narrow[...].astype(BF)
        widen_low[...] = widen[...].astype(BF)
        fnarrow_low[...] = fnarrow[...].astype(BF)
        fwiden_low[...] = fwiden[...].astype(BF)
        for ref in (vec_out, dwid_out, dnar_out, dfn_out):
            ref[...] = jnp.zeros_like(ref)

    unit = normal_rows(tok[...].astype(F32))
    normed = unit * gain[...] + shift[...]
    delta = shifted(normed) - normed
    hidden = hid[...]
    hb = hidden.astype(BF)
    lowv = low[...]
    colsum = lambda v: jnp.sum(v, axis=0, keepdims=True)
    dlow = mm_nt(draw[...].astype(BF), fwiden_low[...]) * (1.0 - lowv * lowv)
    dlow = dlow.astype(BF)
    total = jnp.zeros(normed.shape, F32)
    moved = jnp.zeros(normed.shape, F32)
    dhid = []
    for f, d_ref, w_ref in (
        (0, None, None),
        (1, dk, wk),
        (2, dv, wv),
        (3, dr, wr),
        (4, dg, wg),
    ):
        rows = slice(f * ranks, (f + 1) * ranks)
        mu = lerp[f + 1 : f + 2, :] + mm(hb[:, rows], widen_low[rows, :])
        if f == 0:
            dx = mm(dlow, fnarrow_low[...])
            dfn_out[...] += mm_tn(dlow, (normed + delta * mu).astype(BF))
        else:
            dx = mm_nt(d_ref[...], w_ref[...])
        total = total + dx
        moved = moved + dx * mu
        doff = dx * delta
        vec_out[f + 1 : f + 2, :] += colsum(doff)
        db = doff.astype(BF)
        dwid_out[rows, :] += mm_tn(hb[:, rows], db)
        dhid.append(mm_nt(db, widen_low[rows, :]))
    dpre = (jnp.concatenate(dhid, axis=1) * (1.0 - hidden * hidden)).astype(BF)
    dblend = mm(dpre, narrow_low[...])
    base = lerp[0:1, :]
    dnar_out[...] += mm_tn(dpre, (normed + delta * base).astype(BF))
    vec_out[0:1, :] += colsum(dblend * delta)
    total = total + dblend
    moved = moved + dblend * base
    dn = total - moved + shifted_back(moved)
    vec_out[6:7, :] += colsum(dn * unit)
    vec_out[7:8, :] += colsum(dn)
    dn_out[...] = dn.astype(BF)


def back(seq_len, tokens, hid, low, grads, draw, params, weights):
    g, d = tokens.shape
    c = draw.shape[1]
    gain, shift, lerp, narrow, widen, fnarrow, fwiden = params
    ranks = widen.shape[0] // 5
    fd = low.shape[1]
    order = orders()
    per_seq = lambda w: pl.BlockSpec((seq_len, w), lambda s, o: (s, 0))
    kept = lambda r: pl.BlockSpec((r, d), lambda s, o: (0, 0))
    return pl.pallas_call(
        functools.partial(back_kernel, ranks),
        grid_spec=pltpu.PrefetchScalarGridSpec(
            num_scalar_prefetch=1,
            grid=(g // seq_len,),
            in_specs=[
                ordered_rows(seq_len, d, g // seq_len // order.shape[0]),
                per_seq(5 * ranks),
                per_seq(fd),
            ]
            + [per_seq(c)] * 5
            + [whole_block(a) for a in params]
            + [whole_block(a) for a in weights],
            out_specs=[per_seq(d), kept(8), kept(5 * ranks), kept(5 * ranks), kept(fd)],
            scratch_shapes=[
                pltpu.VMEM((5 * ranks, d), BF),
                pltpu.VMEM((5 * ranks, d), BF),
                pltpu.VMEM((fd, d), BF),
                pltpu.VMEM((fd, c), BF),
            ],
        ),
        out_shape=[
            jax.ShapeDtypeStruct((g, d), BF),
            jax.ShapeDtypeStruct((8, d), F32),
            jax.ShapeDtypeStruct((5 * ranks, d), F32),
            jax.ShapeDtypeStruct((5 * ranks, d), F32),
            jax.ShapeDtypeStruct((fd, d), F32),
        ],
        compiler_params=pltpu.CompilerParams(vmem_limit_bytes=56 * MIB),
        cost_estimate=SHORT,
        name="token_shift_back",
    )(order, tokens, hid, low, *grads, draw, *params, *weights)


def level_tables(length):
    p = np.arange(length)[:, None]
    u = np.arange(length)[None, :]
    levels = int(length).bit_length() - 1
    spans = []
    for l in range(1, levels):
        b = 1 << l
        same = (p // b) == (u // b)
        upper = (p // b) % 2 == 1
        spans.append(same & np.where(upper, u < p, u > p))
    spans = np.concatenate(spans, 0).astype(np.float32)
    diff = p ^ u
    level = np.where(u < p, np.floor(np.log2(np.maximum(diff, 1))), -1)
    return levels, spans, level.astype(np.int32)


def per_head(lanes, width, count, v):
    out = jnp.sum(jnp.where(lanes == 0, v, 0.0), axis=1, keepdims=True)
    if count == 1:
        return jnp.broadcast_to(out, v.shape)
    for h in range(1, count):
        one = jnp.sum(jnp.where(lanes == h, v, 0.0), axis=1, keepdims=True)
        out = jnp.where(lanes == h, one, out)
    return out


def stack_heads(lanes, count, v):
    zero = jnp.zeros_like(v)
    return jnp.concatenate([jnp.where(lanes == h, v, zero) for h in range(count)], axis=0)


def side_by_side(length, count, v):
    return jnp.concatenate([v[h * length : (h + 1) * length] for h in range(count)], axis=1)


def mix_forward(levels, count, width, r, k, v, w, u, spans, level):
    length, lanes_n = r.shape
    lanes = lax.broadcasted_iota(jnp.int32, (length, lanes_n), 1) // width
    gaps = mm(spans, jnp.concatenate(halves(w), axis=0))
    factors = [None] + [
        jnp.exp(gaps[l * length : (l + 1) * length]) for l in range(levels - 1)
    ]
    level2 = jnp.concatenate([level] * count, axis=0)
    scores = jnp.zeros((length * count, length), F32)
    parts = []
    for l in range(levels):
        e = factors[l]
        re = (r if e is None else r * e).astype(BF)
        ke = (k if e is None else k * e).astype(BF)
        parts.append((e, re, ke))
        scores = scores + jnp.where(
            level2 == l, mm_nt(stack_heads(lanes, count, re), ke), 0.0
        )
    vb = v.astype(BF)
    bonus = per_head(lanes, width, count, r * u * k)
    wkv = (
        mm(side_by_side(length, count, scores).astype(BF), stack_heads(lanes, count, vb))
        + bonus * v
    )
    center = wkv - per_head(lanes, width, count, wkv) * (1.0 / width)
    spread = per_head(lanes, width, count, center * center) * (1.0 / width)
    rstd = lax.rsqrt(spread + group_eps)
    return lanes, level2, parts, scores, bonus, vb, center * rstd, rstd


def mix_kernel(levels, count, width, *refs):
    xk, xv, xr, xg, low, wk, wv, wr, wg, we, base, fwiden, u, gain, bias, spans, level = refs[:17]
    k_out, v_out, r_out, g_out, w_out, mixed_out, near_out, far_out = refs[17:]
    for x, weights, out in ((xk, wk, k_out), (xv, wv, v_out), (xr, wr, r_out), (xg, wg, g_out)):
        out[...] = mm(x[...], weights[...])
    lh, ll = halves(low[...])
    fh, fl = halves(fwiden[...])
    w_out[...] = -jnp.exp(base[...] + (mm(lh, fh) + mm(lh, fl) + mm(ll, fh)))
    lanes = count * width
    for p in range(u.shape[1] // lanes):
        at = slice(p * lanes, (p + 1) * lanes)
        unit = mix_forward(
            levels,
            count,
            width,
            r_out[:, at],
            k_out[:, at],
            v_out[:, at],
            w_out[:, at],
            u[:, at],
            spans[...],
            level[...],
        )[6]
        gate = g_out[:, at]
        mixed_out[:, at] = (
            (unit * gain[:, at] + bias[:, at]) * (gate * jax.nn.sigmoid(gate))
        ).astype(BF)
    product = mm(mixed_out[...], we[...]).astype(BF)
    step, steps = pl.program_id(0), pl.num_programs(0)

    @pl.when(step < steps // 2)
    def _():
        near_out[...] = product

    @pl.when(step >= steps // 2)
    def _():
        far_out[...] = product


def mix(seq_len, xs, low, weights, we, vectors, fwiden):
    rows, d = xs[0].shape
    c = we.shape[0]
    half = rows // 2
    heads_here = c * HEADS // d
    width = c // heads_here
    count = 2 if heads_here % 2 == 0 else 1
    levels, spans, level = level_tables(seq_len)
    spans_a = jnp.asarray(np.concatenate([spans, spans], axis=1), BF)
    level_a = jnp.asarray(level)
    steps = half // seq_len
    block = lambda w: pl.BlockSpec((seq_len, w), lambda s: (s, 0))
    base, u, gain, bias = vectors
    kept = (*weights, we, base, fwiden, u, gain, bias, spans_a, level_a)
    shape = lambda w, t: jax.ShapeDtypeStruct((rows, w), t)
    return pl.pallas_call(
        functools.partial(mix_kernel, levels, count, width),
        grid=(2 * steps,),
        in_specs=[block(d)] * 4 + [block(low.shape[1])] + [whole_block(t) for t in kept],
        out_specs=[block(c)] * 6
        + [
            pl.BlockSpec((seq_len, d), lambda s: (jnp.minimum(s, steps - 1), 0)),
            pl.BlockSpec((seq_len, d), lambda s: (jnp.maximum(s - steps, 0), 0)),
        ],
        out_shape=[shape(c, F32)] * 5
        + [shape(c, BF)]
        + [jax.ShapeDtypeStruct((half, d), BF)] * 2,
        compiler_params=pltpu.CompilerParams(vmem_limit_bytes=28 * MIB),
        cost_estimate=lasts(20),
        name="decay_mix",
    )(*xs, low, *kept)


def wkv_back_kernel(
    levels,
    count,
    width,
    r_ref,
    k_ref,
    v_ref,
    g_ref,
    w_ref,
    dm_ref,
    u_ref,
    gain_ref,
    bias_ref,
    spans,
    spans_t,
    level_ref,
    dr_out,
    dk_out,
    dv_out,
    dg_out,
    draw_out,
    vec_out,
):
    @pl.when(pl.program_id(1) == 0)
    def _():
        vec_out[...] = jnp.zeros_like(vec_out)

    r, k, v, w, u = r_ref[...], k_ref[...], v_ref[...], w_ref[...], u_ref[...]
    level = level_ref[...]
    lanes, level2, parts, scores, bonus, vb, unit, rstd = mix_forward(
        levels, count, width, r, k, v, w, u, spans[...], level
    )
    length = r.shape[0]
    heads = functools.partial(per_head, lanes, width, count)
    stack = functools.partial(stack_heads, lanes, count)
    beside = functools.partial(side_by_side, length, count)
    colsum = lambda x: jnp.sum(x, axis=0, keepdims=True)

    gate, dm, gain = g_ref[...], dm_ref[...], gain_ref[...]
    sig = jax.nn.sigmoid(gate)
    scaled = unit * gain + bias_ref[...]
    dg_out[...] = (dm * scaled * sig * (1.0 + gate * (1.0 - sig))).astype(BF)
    dscaled = dm * gate * sig
    dunit = dscaled * gain
    dwkv = rstd * (
        dunit - heads(dunit) * (1.0 / width) - unit * (heads(dunit * unit) * (1.0 / width))
    )
    db = dwkv.astype(BF)
    dbs = stack(db)
    dscores = mm_nt(dbs, vb)

    def turned(x):
        return jnp.concatenate(
            [jnp.transpose(x[h * length : (h + 1) * length]) for h in range(count)], axis=0
        )

    dscores_t = turned(dscores)
    level_t = jnp.transpose(level)
    level2_t = jnp.concatenate([level_t] * count, axis=0)
    dv = mm(beside(turned(scores)).astype(BF), dbs) + bonus * dwkv
    dbonus = heads(dwkv * v)
    dr = dbonus * u * k
    dk = dbonus * u * r
    flows = []
    for l in range(levels):
        e, re, ke = parts[l]
        dre = mm(beside(jnp.where(level2 == l, dscores, 0.0)).astype(BF), stack(ke))
        dke = mm(beside(jnp.where(level2_t == l, dscores_t, 0.0)).astype(BF), stack(re))
        if e is None:
            dr = dr + dre
            dk = dk + dke
        else:
            dre = dre * e
            dke = dke * e
            dr = dr + dre
            dk = dk + dke
            flows.append(dre * r + dke * k)
    fh, fl = halves(jnp.concatenate(flows, axis=0))
    dw = mm(spans_t[...], fh) + mm(spans_t[...], fl)
    draw = dw * w
    dr_out[...] = dr.astype(BF)
    dk_out[...] = dk.astype(BF)
    dv_out[...] = dv.astype(BF)
    draw_out[...] = draw
    vec_out[0:1, :] += colsum(dbonus * r * k)
    vec_out[1:2, :] += colsum(dscaled * unit)
    vec_out[2:3, :] += colsum(dscaled)
    vec_out[3:4, :] += colsum(draw)


def mix_back(seq_len, r, k, v, g, w, u, gain, bias, dmixed):
    rows, c = r.shape
    heads_here = HEADS // lax.axis_size("fsdp")
    width = c // heads_here
    count = 2 if heads_here % 2 == 0 else 1
    lanes = count * width
    levels, spans, level = level_tables(seq_len)
    spans_a = jnp.asarray(np.concatenate([spans, spans], axis=1), BF)
    level_a = jnp.asarray(level)
    cols = pl.BlockSpec((seq_len, lanes), lambda p, s: (s, p))
    vec = pl.BlockSpec((1, lanes), lambda p, s: (0, p))
    grid = (c // lanes, rows // seq_len)
    params = pltpu.CompilerParams(vmem_limit_bytes=40 * MIB)
    spans_t = jnp.asarray(
        np.concatenate([s.T for s in spans.reshape(levels - 1, seq_len, seq_len)], 1), BF
    )
    return pl.pallas_call(
        functools.partial(wkv_back_kernel, levels, count, width),
        grid=grid,
        in_specs=[cols] * 6
        + [vec] * 3
        + [whole_block(spans_a), whole_block(spans_t), whole_block(level_a)],
        out_specs=[cols] * 5 + [pl.BlockSpec((4, lanes), lambda p, s: (0, p))],
        out_shape=[jax.ShapeDtypeStruct((rows, c), BF)] * 4
        + [jax.ShapeDtypeStruct((rows, c), F32), jax.ShapeDtypeStruct((4, c), F32)],
        compiler_params=params,
        cost_estimate=SHORT,
        name="decay_mix_back",
    )(r, k, v, g, w, dmixed, u, gain, bias, spans_a, spans_t, level_a)


def step_shift(length, v, back=False):
    rows = v.shape[0]
    at = lax.rem(lax.broadcasted_iota(jnp.int32, v.shape, 0), length)
    edge = at == (length - 1 if back else 0)
    return jnp.where(edge, 0.0, pltpu.roll(v, rows - 1 if back else 1, 0))


def feed_kernel(length, n2, lerp, wl, *refs):
    kc_out, sq_out, fac_out = refs[-3:]
    n = n2[...].astype(F32)
    delta = step_shift(length, n) - n
    kc = (n + delta * lerp[0:1, :]).astype(BF)
    kc_out[...] = kc
    act = mm(kc, wl[...])
    soft = jnp.maximum(act, 0.0) + jnp.log1p(jnp.exp(-jnp.abs(act)))
    fac_out[...] = 2.0 * soft * jax.nn.sigmoid(act)
    sq_out[...] = (soft * soft).astype(BF)


def feed(length, n2, lerp, wl, part, earlier=()):
    g, d = n2.shape
    f = wl.shape[1]
    half = g // 2
    rows = 2 * length if half % (2 * length) == 0 else length
    first = part * (half // rows)
    block = lambda w: pl.BlockSpec((rows, w), lambda s: (first + s, 0))
    shape = lambda w, t: jax.ShapeDtypeStruct((g, w), t)
    return pl.pallas_call(
        functools.partial(feed_kernel, length),
        grid=(half // rows,),
        in_specs=[block(d), whole_block(lerp), whole_block(wl)]
        + [pl.BlockSpec(memory_space=pl.ANY)] * len(earlier),
        out_specs=[block(d), block(f), block(f)],
        out_shape=[shape(d, BF), shape(f, BF), shape(f, F32)],
        input_output_aliases={3 + i: i for i in range(len(earlier))},
        compiler_params=pltpu.CompilerParams(vmem_limit_bytes=52 * MIB),
        cost_estimate=lasts(6),
        name="feed",
    )(n2, lerp, wl, *earlier)


def value_kernel(own_order, order, sq, wc, near_out, far_out):
    some, _, c = near_out.shape
    for i in range(2 * some):
        at = pl.ds(pl.multiple_of(order[i] * c, c), c) if own_order else slice(i * c, (i + 1) * c)
        out = near_out if i < some else far_out
        out[i % some] = mm(sq[...], wc[:, at]).astype(BF)


def value_product(length, sq, wc, part):
    g, f = sq.shape
    d = wc.shape[1]
    n = lax.axis_size("fsdp")
    half = g // 2
    rows = 2 * length if half % (2 * length) == 0 else length
    first = part * (half // rows)
    return pl.pallas_call(
        functools.partial(value_kernel, paired()),
        grid_spec=pltpu.PrefetchScalarGridSpec(
            num_scalar_prefetch=1,
            grid=(half // rows,),
            in_specs=[pl.BlockSpec((rows, f), lambda s, o: (first + s, 0)), whole_block(wc)],
            out_specs=[pl.BlockSpec((n // 2, rows, d // n), lambda s, o: (0, s, 0))] * 2,
        ),
        out_shape=[jax.ShapeDtypeStruct((n // 2, half, d // n), BF)] * 2,
        compiler_params=pltpu.CompilerParams(vmem_limit_bytes=40 * MIB),
        cost_estimate=lasts(4),
        name="value_product",
    )(orders(), sq, wc)


def pair_kernel(near0, near1, got0, got1, *outs):
    half = near0.shape[1]
    for q, out in enumerate(outs):

        @pl.when(pl.program_id(0) == q)
        def _():
            out[:half, :] = (near0[0].astype(F32) + got1[0].astype(F32)).astype(BF)
            out[half:, :] = (near1[0].astype(F32) + got0[0].astype(F32)).astype(BF)


def gated_kernel(paired_order, adj, gate, *refs):
    *parts, gated_out, dgate_out = refs
    rows = adj.shape[0] // (8 if paired_order else 1)
    for i, own in enumerate(ORDER if paired_order else (0,)):
        at = slice(i * rows, (i + 1) * rows)
        value = parts[0][at, :].astype(F32)
        for q, part in enumerate(parts[1:]):
            p = ORDER.index((2 * q + 2) ^ own)
            value = value + part[p * rows : (p + 1) * rows, :].astype(F32)
        g = gate[at, :].astype(F32)
        gated = g * value
        gated_out[at, :] = gated.astype(BF)
        dgate_out[at, :] = (adj[at, :].astype(F32) * gated * (1.0 - g)).astype(BF)


def gated_value(adj, gate, halves_of_value):
    (near0, far0), (near1, far1) = halves_of_value
    g, c = gate.shape
    if paired():
        got0, got1 = swap(far0, 1), swap(far1, 1)
        block = pl.BlockSpec((1, g // 2, c), lambda q: (q, 0, 0))
        parts = pl.pallas_call(
            pair_kernel,
            grid=(4,),
            in_specs=[block] * 4,
            out_specs=[pl.BlockSpec((g, c), lambda q: (0, 0))] * 4,
            out_shape=[jax.ShapeDtypeStruct((g, c), BF)] * 4,
            compiler_params=pltpu.CompilerParams(vmem_limit_bytes=32 * MIB),
            cost_estimate=SHORT,
            name="pairs",
        )(near0, near1, got0, got1)
        parts = [parts[0]] + [swap(parts[q], 2 * q) for q in (1, 2, 3)]
        rows = g
    else:
        sums = [
            lax.psum_scatter(
                jnp.concatenate(t, axis=0), "fsdp", scatter_dimension=0, tiled=True
            )[0]
            for t in halves_of_value
        ]
        parts = [jnp.concatenate(sums, axis=0)]
        rows = g // lax.axis_size("fsdp")
    block = pl.BlockSpec((rows, c), lambda s: (s, 0))
    return pl.pallas_call(
        functools.partial(gated_kernel, paired()),
        grid=(g // rows,),
        in_specs=[block] * (2 + len(parts)),
        out_specs=[block] * 2,
        out_shape=[jax.ShapeDtypeStruct((g, c), BF)] * 2,
        compiler_params=pltpu.CompilerParams(vmem_limit_bytes=32 * MIB),
        cost_estimate=SHORT,
        name="gated_value",
    )(adj, gate, *parts)


def gate_kernel(length, n2, adj, lerp, wa, rc_out, gate_out, dv_out):
    n = n2[...].astype(F32)
    rc = (n + (step_shift(length, n) - n) * lerp[1:2, :]).astype(BF)
    rc_out[...] = rc
    gate = jax.nn.sigmoid(mm(rc, wa[...]))
    gate_out[...] = gate.astype(BF)
    dv_out[...] = (adj[...].astype(F32) * gate).astype(BF)


def feed_gate(length, n2, adj, lerp, wa):
    g, d = n2.shape
    c = wa.shape[1]
    rows = 2 * length if g % (2 * length) == 0 else length
    block = lambda w: pl.BlockSpec((rows, w), lambda s: (s, 0))
    return pl.pallas_call(
        functools.partial(gate_kernel, length),
        grid=(g // rows,),
        in_specs=[block(d), block(c), whole_block(lerp), whole_block(wa)],
        out_specs=[block(d), block(c), block(c)],
        out_shape=[jax.ShapeDtypeStruct((g, w), BF) for w in (d, c, c)],
        compiler_params=pltpu.CompilerParams(vmem_limit_bytes=32 * MIB),
        cost_estimate=SHORT,
        name="feed_gate",
    )(n2, adj, lerp, wa)


def feed_back_kernel(length, dv, n2, fac, dgate, lerp, wl, wa, wc, dkey_out, dn_out, vec_out):
    @pl.when(pl.program_id(0) == 0)
    def _():
        vec_out[...] = jnp.zeros_like(vec_out)

    dkey = (mm_nt(dv[...], wc[...]) * fac[...]).astype(BF)
    dkey_out[...] = dkey
    n = n2[...].astype(F32)
    delta = step_shift(length, n) - n
    dk = mm_nt(dkey, wl[...])
    dr = mm_nt(dgate[...], wa[...])
    vec_out[0:1, :] += jnp.sum(dk * delta, axis=0, keepdims=True)
    vec_out[1:2, :] += jnp.sum(dr * delta, axis=0, keepdims=True)
    moved = dk * lerp[0:1, :] + dr * lerp[1:2, :]
    dn_out[...] = (dk + dr - moved + step_shift(length, moved, True)).astype(BF)


def feed_back(length, dv, n2, fac, dgate, lerp, wl, wa, wc):
    g, d = n2.shape
    f, c = wc.shape[0], dgate.shape[1]
    rows = 2 * length if g % (2 * length) == 0 else length
    block = lambda w: pl.BlockSpec((rows, w), lambda s: (s, 0))
    return pl.pallas_call(
        functools.partial(feed_back_kernel, length),
        grid=(g // rows,),
        in_specs=[block(d), block(d), block(f), block(c)]
        + [whole_block(a) for a in (lerp, wl, wa, wc)],
        out_specs=[block(f), block(d), pl.BlockSpec((2, d), lambda s: (0, 0))],
        out_shape=[
            jax.ShapeDtypeStruct((g, f), BF),
            jax.ShapeDtypeStruct((g, d), BF),
            jax.ShapeDtypeStruct((2, d), F32),
        ],
        compiler_params=pltpu.CompilerParams(vmem_limit_bytes=52 * MIB),
        cost_estimate=SHORT,
        name="feed_back",
    )(dv, n2, fac, dgate, lerp, wl, wa, wc)


def body(
    incoming_symbols,
    string_extents,
    adjoint_signal,
    first_scaling_factor,
    first_scaling_shift,
    lerp_factors,
    lerp_narrow_weights,
    lerp_widen_weights,
    fading_baseline,
    fading_narrow_weights,
    fading_widen_weights,
    present_reward,
    acceptor_weights,
    lookup_weights,
    content_weights,
    valve_weights,
    emission_weights,
    cluster_scaling_factor,
    cluster_scaling_shift,
    second_scaling_factor,
    second_scaling_shift_vec,
    feed_lerp_factors,
    feed_lookup_weights,
    feed_content_weights,
    feed_acceptor_weights,
):
    seqs, length, d = incoming_symbols.shape
    n = lax.axis_size("fsdp")
    me = lax.axis_index("fsdp")
    c = d // n
    home = seqs * length
    plane = home * n
    ranks = lerp_widen_weights.shape[1]
    fd = fading_narrow_weights.shape[1]

    tok_home = incoming_symbols.reshape(home, d)
    tokens = lax.all_gather(tok_home, "fsdp", axis=0, tiled=True)
    mix_weights = Exchange(
        (
            lookup_weights,
            content_weights,
            acceptor_weights,
            valve_weights,
        ),
        1,
    )
    mix_weights.across_cores()
    mix_weights.across_chips()
    positions = lax.broadcasted_iota(jnp.int32, (seqs, length), 1)
    mask = (positions < string_extents[:, None]).astype(F32).reshape(home, 1)
    adjoint = adjoint_signal.reshape(home, d) * mask.astype(BF)
    d_out = adjoint.astype(F32)

    row = lambda v: v.reshape(1, -1)
    mine = lambda v: lax.dynamic_slice_in_dim(v, me * c, c, v.ndim - 1)
    gain1, shift1 = row(first_scaling_factor), row(first_scaling_shift)
    narrow, fnarrow = lerp_narrow_weights.T, fading_narrow_weights.T
    widen = lerp_widen_weights.reshape(5 * ranks, d)
    feed_weights = Exchange([feed_lookup_weights, feed_acceptor_weights], 1)
    feed_weights.across_cores()
    (tokens,) = feed_weights.after(*mix_weights.arrived(tokens, count=2))
    feed_weights.across_chips()
    xk, xv, xr, xg, hidden, low = front(
        length, tokens, gain1, shift1, lerp_factors, narrow, widen, fnarrow
    )
    (low,) = mix_weights.arrived(low)
    wk, wv, wr, wg = mix_weights.results()
    fwiden_mine = mine(fading_widen_weights)
    base, u, gn_gain, gn_bias = (
        mine(row(t))
        for t in (
            fading_baseline,
            present_reward,
            cluster_scaling_factor,
            cluster_scaling_shift,
        )
    )
    k, v, r, g, w, mixed, near, far = mix(
        length,
        (xk, xv, xr, xg),
        low,
        (wk, wv, wr, wg),
        emission_weights,
        (base, u, gn_gain, gn_bias),
        fwiden_mine,
    )
    near, far = feed_weights.arrived(near, far)
    branch = scatter_tokens(near, far)
    wl, wa = feed_weights.results()
    branch, wl, wa = hold(branch, wl, wa)
    branch, adjoint = hold(branch, adjoint)
    adjoint_cols = spread_features(adjoint)
    residual = tok_home.astype(F32) + branch

    center = residual - jnp.mean(residual, axis=-1, keepdims=True)
    rstd2 = lax.rsqrt(jnp.mean(center * center, axis=-1, keepdims=True) + norm_eps)
    unit2 = center * rstd2
    normed2, _ = gather_tokens(
        (unit2 * second_scaling_factor + second_scaling_shift_vec).astype(BF)
    )
    fc = feed_content_weights.shape[0]
    recept_chan, gate, d_value_mine = feed_gate(
        length, normed2, adjoint_cols, feed_lerp_factors, wa
    )
    feed_part = lambda *t: feed(length, normed2, feed_lerp_factors, wl, *t)
    d_value, (key_chan, squared, factor) = gather_features_of_tokens(
        d_value_mine, (lambda: feed_part(0), lambda *done: feed_part(1, done))
    )
    d_content = mm_tn(squared, d_value).astype(BF)
    d_value, d_content, squared = hold(d_value, d_content, squared)
    content_share = rep_scatter(d_content)
    value_part = lambda part: value_product(length, squared, feed_content_weights, part)
    gated, d_gate = gated_value(adjoint_cols, gate, (value_part(0), value_part(1)))

    d_key, d_normed2, feed_lerp_part = feed_back(
        length, d_value, normed2, factor, d_gate, feed_lerp_factors, wl, wa, feed_content_weights
    )
    d_normed2, content_share = hold(d_normed2, content_share)
    content_sum = rep_gather(content_share)
    feed_share = rep_scatter_cols(
        (mm_tn(key_chan, d_key).astype(BF), mm_tn(recept_chan, d_gate).astype(BF))
    )
    d_normed2 = scatter_tokens(d_normed2[: plane // 2], d_normed2[plane // 2 :])

    def norm_back(unit, rstd, e):
        return rstd * (
            e
            - jnp.mean(e, axis=-1, keepdims=True)
            - unit * jnp.mean(e * unit, axis=-1, keepdims=True)
        )

    layer_output = (residual + home_features(gated).astype(F32)) * mask
    d_residual = d_out + norm_back(unit2, rstd2, d_normed2 * second_scaling_factor)
    norm2_part = jnp.stack([jnp.sum(d_normed2 * unit2, axis=0), jnp.sum(d_normed2, axis=0)])

    d_branch, _ = gather_tokens(d_residual.astype(BF))
    d_mixed = mm_nt(d_branch, emission_weights)
    d_emission = mm_tn(mixed, d_branch).astype(BF)
    d_r, d_k, d_v, d_g, d_raw, mix_vec = mix_back(
        length, r, k, v, g, w, u, gn_gain, gn_bias, d_mixed
    )
    d_r, d_k, d_v, d_g, feed_share = hold(d_r, d_k, d_v, d_g, feed_share)
    time_share, emission_share = rep_scatter_cols(
        [mm_tn(x, t).astype(BF) for x, t in ((xk, d_k), (xv, d_v), (xr, d_r), (xg, d_g))],
        d_emission,
    )
    feed_sums = Exchange([feed_share[:, :fc], feed_share[:, fc:]], 0)
    feed_sums.across_cores()
    feed_sums.across_chips()
    d_normed, vec_part, widen_part, narrow_part, fnarrow_part = back(
        length,
        tokens,
        hidden,
        low,
        (d_k, d_v, d_r, d_g),
        d_raw,
        (gain1, shift1, lerp_factors, narrow, widen, fnarrow, fwiden_mine),
        (wk, wv, wr, wg),
    )
    d_normed, content_sum = feed_sums.arrived(*hold(d_normed, content_sum))
    feed_sum = rep_gather(jnp.concatenate(feed_sums.results(), axis=1))
    d_normed = scatter_tokens(d_normed[: plane // 2], d_normed[plane // 2 :])
    small = scatter_features(
        jnp.concatenate(
            [vec_part, widen_part, narrow_part, fnarrow_part, norm2_part, feed_lerp_part], axis=0
        ).astype(BF)
    )
    fwiden_part = mm_tn(low.astype(BF), d_raw.astype(BF))
    small = rep_sum(jnp.concatenate([small, fwiden_part, mix_vec], axis=0).astype(BF))
    small = gather_features(small.astype(BF)).astype(F32)
    small, time_share = hold(small, time_share)
    time_sums = Exchange([time_share[:, i * c : (i + 1) * c] for i in range(4)], 0)
    time_sums.across_cores()
    time_sums.across_chips()
    time_sum = rep_gather(jnp.concatenate([*time_sums.results(), emission_share], axis=1))
    (feed_content_grads,) = widened(content_sum, (d,))
    feed_lookup_grads, feed_acceptor_grads = widened(feed_sum, (n * fc, n * c))
    (
        lookup_weights_grads,
        content_weights_grads,
        acceptor_weights_grads,
        valve_weights_grads,
        emission_weights_grads,
    ) = widened(time_sum, (d,) * 5)
    tok_f = tok_home.astype(F32)
    center1 = tok_f - jnp.mean(tok_f, axis=-1, keepdims=True)
    rstd1 = lax.rsqrt(jnp.mean(center1 * center1, axis=-1, keepdims=True) + norm_eps)
    token_grad = d_residual + norm_back(center1 * rstd1, rstd1, d_normed * first_scaling_factor)
    cuts = np.cumsum([8, 5 * ranks, 5 * ranks, fd, 2, 2, fd, 4])
    vec, widen_g, narrow_g, fnarrow_g, norm2_g, feed_lerp_g, fwiden_g, mix_g = (
        small[a:b] for a, b in zip([0, *cuts[:-1]], cuts)
    )
    return (
        layer_output.reshape(seqs, length, d),
        token_grad.reshape(seqs, length, d),
        vec[6],
        vec[7],
        vec[:6],
        narrow_g.T,
        widen_g.reshape(5, ranks, d),
        mix_g[3],
        fnarrow_g.T,
        fwiden_g,
        mix_g[0],
        acceptor_weights_grads,
        lookup_weights_grads,
        content_weights_grads,
        valve_weights_grads,
        emission_weights_grads,
        mix_g[1],
        mix_g[2],
        norm2_g[0],
        norm2_g[1],
        feed_lerp_g,
        feed_lookup_grads,
        feed_content_grads,
        feed_acceptor_grads,
    )


def solution(mesh):
    seq = P(("fsdp", "rep"), None, None)
    row = P("fsdp", None)
    in_specs = (
        (seq, P(("fsdp", "rep")), seq) + (P(),) * 9 + (row,) * 5 + (P(),) * 5 + (row,) * 3
    )
    out_specs = (seq, seq) + (P(),) * 9 + (row,) * 5 + (P(),) * 5 + (row,) * 3
    return jax.shard_map(body, mesh=mesh, in_specs=in_specs, out_specs=out_specs, check_vma=False)
```
